32 devices in a mesh: dp: 16 (over z, y, x), tensor: 2 (over core).
Axes of the slice: x: 2, y: 2, z: 4, core: 2. Of those that a mesh axis runs over, the one named last changes fastest.
Arguments:
- patches: bfloat16 [2048, 1152], P('dp'), may hold values from -6 to 6
- cotangent: bfloat16 [2048, 1152], P('dp'), may hold values from -6 to 6
- image_lengths: int32 [64], replicated, may hold values from 4 to 256, as said below
- image_owner: int32 [64], replicated, may hold values from 0 to 15, as said below
- first_gain: float32 [1152], replicated, may hold values from 0.1 to 1.9
- first_shift: float32 [1152], replicated, may hold values from -3 to 3
- query_weight: bfloat16 [1152, 1152], P(None, 'tensor'), may hold values from -0.25 to 0.25
- query_bias: float32 [1152], P('tensor'), may hold values from -3 to 3
- key_weight: bfloat16 [1152, 1152], P(None, 'tensor'), may hold values from -0.25 to 0.25
- value_weight: bfloat16 [1152, 1152], P(None, 'tensor'), may hold values from -0.1875 to 0.1875
- value_bias: float32 [1152], P('tensor'), may hold values from -3 to 3
- output_weight: bfloat16 [1152, 1152], P(None, 'tensor'), may hold values from -0.75 to 0.75
- output_bias: float32 [1152], replicated, may hold values from -3 to 3
- second_gain: float32 [1152], replicated, may hold values from 0.1 to 1.9
- second_shift: float32 [1152], replicated, may hold values from -3 to 3
- expand_weight: bfloat16 [1152, 4304], P(None, 'tensor'), may hold values from -0.1875 to 0.1875
- expand_bias: float32 [4304], P('tensor'), may hold values from -3 to 3
- reduce_weight: bfloat16 [1152, 4304], P(None, 'tensor'), may hold values from -0.125 to 0.125
- reduce_bias: float32 [1152], replicated, may hold values from -3 to 3
Outputs:
- mixed: bfloat16 [2048, 1152], P('dp')
- patch_gradient: bfloat16 [2048, 1152], P('dp')
- first_gain_gradient: float32 [1152], replicated
- first_shift_gradient: float32 [1152], replicated
- query_weight_gradient: float32 [1152, 1152], P('dp', 'tensor')
- query_bias_gradient: float32 [1152], P('tensor')
- key_weight_gradient: float32 [1152, 1152], P('dp', 'tensor')
- value_weight_gradient: float32 [1152, 1152], P('dp', 'tensor')
- value_bias_gradient: float32 [1152], P('tensor')
- output_weight_gradient: float32 [1152, 1152], P('dp', 'tensor')
- output_bias_gradient: float32 [1152], replicated
- second_gain_gradient: float32 [1152], replicated
- second_shift_gradient: float32 [1152], replicated
- expand_weight_gradient: float32 [1152, 4304], P('dp', 'tensor')
- expand_bias_gradient: float32 [4304], P('tensor')
- reduce_weight_gradient: float32 [1152, 4304], P('dp', 'tensor')
- reduce_bias_gradient: float32 [1152], replicated
The draws below stay inside these ranges and needn't reach their ends.
Inputs may be any that keep to these rules, and one draw needn't show every extreme that they name: `image_lengths`: images of one owner stand together in the stream; all lengths add up to 2048, and one image has exactly 256 patches. `image_owner`: never falls from one image to the next; every index of dp owns 1 to 7 images, whose patches add up to at most 256, and to exactly 256 for some index.
All inputs are finite; a program needn't handle non-finite values.
Results may differ from the reference program's by a relative error of at most 0.015.
Values may be sent and summed in bfloat16 or wider, within the bound.
No kernel may reach another device: no remote copies, remote signals or barrier semaphores. Data moves between devices by JAX's collectives and lax.ppermute only.
A program may use at most 192 MiB of HBM per device.

```python
import jax
import jax.numpy as jnp
from jax import lax

D = 1152
HEADS = 16
HD = 72
FF = 4304
TOK_DEV = 128
IMG_DEV = 4
HHD = 1152
CAP = 256
NIMG = 64
TOKENS = 2048
N_DP = 16


def image_layout(key):
    dev_count = NIMG // IMG_DEV
    least = max(1, CAP // 64)
    key_root, key_spread, key_count, key_cuts = jax.random.split(key, 4)
    root_rank = jax.random.randint(key_root, (), 0, dev_count)
    relative = (jnp.arange(dev_count, dtype=jnp.int32) - root_rank) % dev_count
    pair_index = jnp.maximum(relative - 3, 0) // 2
    sign_one = jnp.where((relative - 3) % 2 == 0, 1, -1)
    single = jnp.logical_and(relative - 3 == dev_count - 4, (dev_count - 3) % 2 == 1)
    spread = jax.random.randint(key_spread, (dev_count,), -(3 * CAP // 8), 3 * CAP // 8 + 1)
    used_rows = CAP // 2 + jnp.where(single, 0, sign_one * jnp.take(spread, pair_index))
    used_rows = jnp.where(relative == 0, CAP, jnp.where(relative < 3, CAP // 4, used_rows))
    shift_count = jax.random.randint(key_count, (dev_count,), 1 - IMG_DEV, IMG_DEV)
    counts = IMG_DEV + jnp.where(single, 0, sign_one * jnp.take(shift_count, pair_index))
    counts = jnp.where(relative == 0, 1, jnp.where(relative == 1, IMG_DEV + 1, jnp.where(relative == 2, 2 * IMG_DEV - 2, counts)))
    end_index = jnp.cumsum(counts)
    image_ids = jnp.arange(NIMG, dtype=jnp.int32)
    owner = jnp.sum((end_index[None, :] <= image_ids[:, None]).astype(jnp.int32), axis=1)
    first_image = jnp.take(end_index - counts, owner)
    within = image_ids - first_image
    extra_rows = jnp.take(used_rows - least * counts, owner)
    is_last = within == jnp.take(counts, owner) - 1
    cut_points = jax.random.randint(key_cuts, (NIMG,), 0, extra_rows + 1)
    cut_points = jnp.where(is_last, extra_rows, cut_points)
    ordered = jnp.sort(owner * (CAP + 1) + cut_points) - owner * (CAP + 1)
    previous = jnp.where(within == 0, 0, jnp.roll(ordered, 1))
    lengths = least + ordered - previous
    return (lengths.astype(jnp.int32), owner.astype(jnp.int32))


def draw_image_lengths(key, part):
    return image_layout(key)[0]


def draw_image_owner(key, part):
    return image_layout(key)[1]


def raised(values, key, source, target, blocks, factor):
    owner, partner = [(jnp.arange(values.shape[dim]) // (values.shape[dim] // blocks)).reshape([-1 if axis == dim else 1 for axis in range(values.ndim)]) for dim in (source, target)]
    chosen = jax.random.permutation(key, blocks)[partner]
    strong = (owner == chosen) | (owner == (partner + blocks // 2) % blocks)
    return jnp.where(strong, factor * values, values)


def levels(key, shape, shards, low, largest):
    def one(axis_at, shards_of):
        steps = jax.random.uniform(jax.random.fold_in(jax.random.fold_in(key, 6), axis_at), (shards_of,), jnp.float32, low / len(shards), largest / len(shards))
        return jnp.repeat(jnp.exp(steps), shape[axis_at] // shards_of).reshape((-1,) + (1,) * (len(shape) - axis_at - 1))

    loudness = one(*shards[0])
    for cut in shards[1:]:
        loudness = loudness * one(*cut)
    return loudness


def gaussian(key, extent, scale, most, shards=(), kind=jnp.bfloat16):
    values = scale * jax.random.normal(key, extent, jnp.float32)
    if shards:
        values = values * levels(key, extent, shards, -0.22, 0.18)
    return jnp.clip(values, -most, most).astype(kind)


def noise_with(key, shape, scale, limit, pieces, heavy, kind=jnp.bfloat16):
    result = scale * jax.random.normal(key, shape, jnp.float32)
    if pieces:
        result = result * levels(key, shape, pieces, -0.22, 0.18)
    return jnp.clip(raised(result, jax.random.fold_in(key, 3), *heavy), -limit, limit).astype(kind)


def setup_inputs(seed: int = 0) -> dict:
    seeds = jax.random.split(jax.random.key(seed), 20)
    return {
        "patches": noise_with(seeds[0], (TOKENS, D), 1.0, 6.0, ((0, 16),), (0, 1, 16, 2.0)),
        "cotangent": gaussian(seeds[1], (TOKENS, D), 1.0, 6.0, ((0, 16),)),
        "image_lengths": draw_image_lengths(jax.random.fold_in(seeds[19], 71), 0),
        "image_owner": draw_image_owner(jax.random.fold_in(seeds[19], 71), 0),
        "first_gain": jnp.clip(1.0 + 0.18 * jax.random.normal(seeds[4], (D,), jnp.float32), 0.1, 1.9),
        "first_shift": gaussian(seeds[5], (D,), 0.5, 3.0, (), jnp.float32),
        "query_weight": gaussian(seeds[6], (D, HHD), (D // 2) ** -0.5, 0.25, ((1, 2),)),
        "query_bias": gaussian(seeds[7], (HHD,), 0.5, 3.0, ((0, 2),), jnp.float32),
        "key_weight": gaussian(seeds[8], (D, HHD), (D // 2) ** -0.5, 0.25, ((1, 2),)),
        "value_weight": gaussian(seeds[9], (D, HHD), D ** -0.5, 0.1875, ((1, 2),)),
        "value_bias": gaussian(seeds[10], (HHD,), 0.5, 3.0, ((0, 2),), jnp.float32),
        "output_weight": gaussian(seeds[11], (D, HHD), (HHD // 16) ** -0.5, 0.75, ((1, 2),)),
        "output_bias": gaussian(seeds[12], (D,), 0.5, 3.0, (), jnp.float32),
        "second_gain": jnp.clip(1.0 + 0.18 * jax.random.normal(seeds[13], (D,), jnp.float32), 0.1, 1.9),
        "second_shift": gaussian(seeds[14], (D,), 0.5, 3.0, (), jnp.float32),
        "expand_weight": gaussian(seeds[15], (D, FF), D ** -0.5, 0.1875, ((1, 2),)),
        "expand_bias": gaussian(seeds[16], (FF,), 0.5, 3.0, ((0, 2),), jnp.float32),
        "reduce_weight": gaussian(seeds[17], (D, FF), (FF // 2) ** -0.5, 0.125, ((1, 2),)),
        "reduce_bias": gaussian(seeds[18], (D,), 0.5, 3.0, (), jnp.float32),
    }


@jax.custom_vjp
def low(v):
    return lax.optimization_barrier(v.astype(jnp.bfloat16)).astype(jnp.float32)

@jax.custom_vjp
def low_back(v):
    return v

def low_keep(v):
    return (low(v), None)

def low_pass(kept, grad):
    return (grad,)

def back_keep(v):
    return (v, None)

def back_low(kept, grad):
    return (low(grad),)
low.defvjp(low_keep, low_pass)
low_back.defvjp(back_keep, back_low)
masked_score = -1000000000.0
norm_eps = 1e-06

def layer_norm(values, gain_row, shift_row):
    centered = values - lax.optimization_barrier(jnp.mean(values, axis=-1, keepdims=True))
    variance = lax.optimization_barrier(jnp.mean(centered * centered, axis=-1, keepdims=True))
    return centered * lax.rsqrt(variance + norm_eps) * gain_row + shift_row

def matmul(left_side, right_side):
    return jnp.dot(left_side, right_side, precision=lax.Precision.HIGHEST)

def block_layer(weights, rows_in, segment):
    first_gain, first_shift, query_weight, query_bias, key_weight, value_weight, value_bias, output_weight, output_bias, second_gain, second_shift, expand_weight, expand_bias, reduce_weight, reduce_bias = weights
    cap_rows = rows_in.shape[0]
    normed = low(layer_norm(rows_in, first_gain, first_shift))
    query_rows = low(low_back(matmul(normed, query_weight) + query_bias)).reshape(cap_rows, HEADS, HD)
    key_rows = low(low_back(matmul(normed, key_weight))).reshape(cap_rows, HEADS, HD)
    value_rows = low(low_back(matmul(normed, value_weight) + value_bias)).reshape(cap_rows, HEADS, HD)
    same_image = segment[:, None] == segment[None, :]
    scores = jnp.einsum('phd,rhd->hpr', query_rows, key_rows, precision=lax.Precision.HIGHEST) * HD ** (-0.5)
    scores = low_back(jnp.where(same_image[None, :, :], scores, masked_score))
    prob_rows = jax.nn.softmax(scores, axis=2)
    attended = jnp.einsum('hpr,rhd->phd', low(prob_rows), value_rows, precision=lax.Precision.HIGHEST)
    attended = low(low_back(attended.reshape(cap_rows, HEADS * HD)))
    branch = low_back(matmul(attended, output_weight.T) + output_bias)
    middle = rows_in + branch
    normed_two = low(layer_norm(middle, second_gain, second_shift))
    expanded = low_back(matmul(normed_two, expand_weight) + expand_bias)
    hidden = low(jax.nn.gelu(expanded, approximate=True))
    branch_two = low_back(matmul(hidden, reduce_weight.T) + reduce_bias)
    return middle + branch_two

def reference(patches, cotangent, image_lengths, image_owner, first_gain, first_shift, query_weight, query_bias, key_weight, value_weight, value_bias, output_weight, output_bias, second_gain, second_shift, expand_weight, expand_bias, reduce_weight, reduce_bias):
    owners = jnp.arange(N_DP, dtype=jnp.int32)
    base_rows = lax.optimization_barrier(jnp.sum(jnp.where(image_owner[None, :] < owners[:, None], image_lengths[None, :], 0), axis=1)).astype(jnp.int32)
    used_rows = lax.optimization_barrier(jnp.sum(jnp.where(image_owner[None, :] == owners[:, None], image_lengths[None, :], 0), axis=1)).astype(jnp.int32)
    starts = (jnp.cumsum(image_lengths) - image_lengths).astype(jnp.int32)
    positions = jnp.arange(CAP, dtype=jnp.int32)
    stream_index = (base_rows[:, None] + positions[None, :]).astype(jnp.int32)
    is_valid = positions[None, :] < used_rows[:, None]
    image_index = lax.optimization_barrier(jnp.sum((starts[None, None, :] <= stream_index[:, :, None]).astype(jnp.int32), axis=2)) - 1
    segments = jnp.where(is_valid, image_index, -1).astype(jnp.int32)
    safe_index = jnp.where(is_valid, stream_index, 0).astype(jnp.int32)
    source_row = (safe_index % N_DP * TOK_DEV + safe_index // N_DP).astype(jnp.int32)
    blocks = jnp.where(is_valid[:, :, None], jnp.take(patches.astype(jnp.float32), source_row, axis=0), 0.0)
    cot_blocks = jnp.where(is_valid[:, :, None], jnp.take(cotangent.astype(jnp.float32), source_row, axis=0), 0.0)
    weights = tuple((weight_arg.astype(jnp.float32) for weight_arg in (first_gain, first_shift, query_weight, query_bias, key_weight, value_weight, value_bias, output_weight, output_bias, second_gain, second_shift, expand_weight, expand_bias, reduce_weight, reduce_bias)))

    def forward(weight_set, block_set):

        def one_block(operands):
            return jax.checkpoint(block_layer)(weight_set, operands[0], operands[1])
        return lax.map(one_block, (block_set, segments))
    outputs, pull_back = jax.vjp(forward, weights, blocks)
    weight_grads, block_grads = pull_back(cot_blocks)
    first_gain_gradient, first_shift_gradient, query_weight_gradient, query_bias_gradient, key_weight_gradient, value_weight_gradient, value_bias_gradient, output_weight_gradient, output_bias_gradient, second_gain_gradient, second_shift_gradient, expand_weight_gradient, expand_bias_gradient, reduce_weight_gradient, reduce_bias_gradient = weight_grads
    row_ids = jnp.arange(TOKENS, dtype=jnp.int32)
    stream_of_row = (row_ids % TOK_DEV * N_DP + row_ids // TOK_DEV).astype(jnp.int32)
    owner_of_row = (lax.optimization_barrier(jnp.sum((base_rows[None, :] <= stream_of_row[:, None]).astype(jnp.int32), axis=1)) - 1).astype(jnp.int32)
    flat_index = (owner_of_row * CAP + stream_of_row - jnp.take(base_rows, owner_of_row)).astype(jnp.int32)
    mixed = jnp.take(outputs.reshape(N_DP * CAP, D), flat_index, axis=0).astype(jnp.bfloat16)
    patch_gradient = jnp.take(block_grads.reshape(N_DP * CAP, D), flat_index, axis=0).astype(jnp.bfloat16)
    return (mixed, patch_gradient, first_gain_gradient, first_shift_gradient, query_weight_gradient, query_bias_gradient, key_weight_gradient, value_weight_gradient, value_bias_gradient, output_weight_gradient, output_bias_gradient, second_gain_gradient, second_shift_gradient, expand_weight_gradient, expand_bias_gradient, reduce_weight_gradient, reduce_bias_gradient)
```

```python
import functools

import jax
import jax.numpy as jnp
from jax import lax
from jax.experimental import pallas as pl
from jax.experimental.pallas import tpu as pltpu
from jax.sharding import PartitionSpec as P

HD = 72
masked_score = -1000000000.0
norm_eps = 1e-06
gelu_scale = 0.7978845608028654
gelu_cubic = 0.044715
f32 = jnp.float32
bf16 = jnp.bfloat16
MIB = 1024 * 1024


def dot(left, right):
    return lax.dot_general(left, right, (((1,), (0,)), ((), ())), preferred_element_type=f32)


def dot_cols(left, right):
    return lax.dot_general(left, right, (((1,), (1,)), ((), ())), preferred_element_type=f32)


def dot_rows(left, right):
    return lax.dot_general(left, right, (((0,), (0,)), ((), ())), preferred_element_type=f32)


def iota(shape, dim):
    return lax.broadcasted_iota(jnp.int32, shape, dim).astype(f32)


def row_sum(values):
    return jnp.sum(values, axis=0, keepdims=True)


def lane_sum(values):
    return jnp.sum(values, axis=1, keepdims=True)


def lane_mean(values):
    return jnp.mean(values, axis=1, keepdims=True)


def my_span(lengths, owners, me):
    base = lane_sum(jnp.where(owners < me, lengths, 0.0))
    used = lane_sum(jnp.where(owners == me, lengths, 0.0))
    return base, used


def token_slots(lengths, owners, me, n_dev, tokens, half_rows):
    device = iota((n_dev, lengths.shape[1]), 0)
    base = lane_sum(jnp.where(owners < device, lengths, 0.0))
    pos = iota((1, tokens), 1) * n_dev + me
    below = base <= pos
    target = row_sum(jnp.where(below, 1.0, 0.0)) - 1.0
    start = jnp.max(jnp.where(below, base, -1.0), axis=0, keepdims=True)
    slot = jnp.floor((pos - start) * (1.0 / n_dev))
    half = jnp.floor(slot * (1.0 / half_rows))
    return half, target * half_rows + slot - half * half_rows


def block_slots(base, n_dev, cap, half_rows):
    p = iota((cap, 1), 0)
    pos = base + p
    source = pos - n_dev * jnp.floor(pos * (1.0 / n_dev))
    slot = jnp.floor(p * (1.0 / n_dev))
    half = jnp.floor(slot * (1.0 / half_rows))
    return half, source * half_rows + slot - half * half_rows


def one_hot(index, shape, dim):
    return jnp.where(index == iota(shape, dim), 1.0, 0.0).astype(bf16)


def place():
    return lax.axis_index("dp").astype(f32), lax.axis_index("tensor").astype(f32)


def norm_parts(values):
    centered = values - lane_mean(values)
    scale = lax.rsqrt(lane_mean(centered * centered) + norm_eps)
    return centered * scale, scale


def norm_back(normed, scale, grad, gain):
    inner = grad * gain
    return scale * (inner - lane_mean(inner) - normed * lane_mean(inner * normed))


def gelu_both(values):
    square = values * values
    bent = jnp.tanh(gelu_scale * values * (1.0 + gelu_cubic * square))
    half = 0.5 * (1.0 + bent)
    slope = half + 0.5 * values * (1.0 - bent * bent) * (
        gelu_scale * (1.0 + 3.0 * gelu_cubic * square)
    )
    return values * half, slope


def pack_kernel(n_dev, half_rows, len_ref, own_ref, x_ref, g_ref, send_x, send_g):
    me, core = place()
    half, index = token_slots(
        len_ref[...].astype(f32), own_ref[...].astype(f32), me, n_dev, x_ref.shape[0], half_rows
    )
    index = jnp.where(half == core, index, -1.0)
    pick = one_hot(index, (n_dev * half_rows, x_ref.shape[0]), 0)
    send_x[...] = dot(pick, x_ref[...]).astype(bf16)
    send_g[...] = dot(pick, g_ref[...]).astype(bf16)


def block_pick(len_ref, own_ref, n_dev, cap, half_rows):
    me, core = place()
    base, used = my_span(len_ref[...].astype(f32), own_ref[...].astype(f32), me)
    half, index = block_slots(base, n_dev, cap, half_rows)
    index = jnp.where(half == core, index, index + n_dev * half_rows)
    return one_hot(index, (cap, cap), 1)


def unpack_kernel(n_dev, half_rows, len_ref, own_ref, mine_ref, other_ref, out_ref):
    cap = out_ref.shape[0]
    pick = block_pick(len_ref, own_ref, n_dev, cap, half_rows)
    rows = jnp.concatenate([mine_ref[...], other_ref[...]], axis=0)
    out_ref[...] = dot(pick, rows).astype(bf16)


def image_mask(len_ref, own_ref, cap):
    lengths, owners = len_ref[...].astype(f32), own_ref[...].astype(f32)
    me, _ = place()
    base, used = my_span(lengths, owners, me)
    n_img = lengths.shape[1]
    starts = lane_sum(
        jnp.where(iota((n_img, n_img), 1) < iota((n_img, n_img), 0), lengths, 0.0)
    )
    p = iota((1, cap), 1)
    count = row_sum(jnp.where(starts <= base + p, 1.0, 0.0))
    seg_row = jnp.where(p < used, count, 0.0)
    on_diagonal = iota((cap, cap), 0) == iota((cap, cap), 1)
    seg_col = lane_sum(jnp.where(on_diagonal, seg_row, 0.0))
    return jnp.where(seg_col == seg_row, 1.0, 0.0)


def attend_kernel(
    n_dev, half_rows, len_ref, own_ref, mine_ref, other_ref, gain_ref, shift_ref,
    wq_ref, bq_ref, wk_ref, wv_ref, bv_ref, wo_ref,
    x_ref, h1_ref, q_ref, k_ref, v_ref, log_ref, mask_ref, att_ref, part_ref,
):
    cap = x_ref.shape[0]
    pick = block_pick(len_ref, own_ref, n_dev, cap, half_rows)
    rows = jnp.concatenate([mine_ref[...], other_ref[...]], axis=0)
    x = dot(pick, rows)
    x_ref[...] = x.astype(bf16)
    same = image_mask(len_ref, own_ref, cap)
    mask_ref[...] = same
    normed, _ = norm_parts(x)
    h1 = (normed * gain_ref[...] + shift_ref[...]).astype(bf16)
    h1_ref[...] = h1
    q_ref[...] = (dot(h1, wq_ref[...]) + bq_ref[...]).astype(bf16)
    k_ref[...] = dot(h1, wk_ref[...]).astype(bf16)
    v_ref[...] = (dot(h1, wv_ref[...]) + bv_ref[...]).astype(bf16)
    for h in range(q_ref.shape[1] // HD):
        cols = slice(h * HD, (h + 1) * HD)
        s = dot_cols(q_ref[:, cols], k_ref[:, cols]) * HD ** (-0.5)
        s = jnp.where(same > 0.5, s, masked_score)
        top = jnp.max(s, axis=1, keepdims=True)
        e = jnp.exp(s - top)
        total = lane_sum(e)
        log_ref[:, h : h + 1] = top + jnp.log(total)
        att_ref[:, cols] = dot((e / total).astype(bf16), v_ref[:, cols]).astype(bf16)
    part_ref[...] = dot_cols(att_ref[...], wo_ref[...])


def middle_kernel(x_ref, mine_ref, other_ref, bias_ref, gain_ref, shift_ref, mid_ref, h2_ref):
    middle = x_ref[...].astype(f32) + (mine_ref[...] + other_ref[...] + bias_ref[...])
    mid_ref[...] = middle
    normed, _ = norm_parts(middle)
    h2_ref[...] = (normed * gain_ref[...] + shift_ref[...]).astype(bf16)


def column_chunks(width, step):
    full = width // step
    return full, full * step, width - full * step


def mlp_kernel(h2_ref, g_ref, we_ref, be_ref, wr_ref, out_ref, dh2_ref, be_grad_ref):
    full, done, rest = column_chunks(we_ref.shape[1], 512)
    out_ref[...] = jnp.zeros_like(out_ref)
    dh2_ref[...] = jnp.zeros_like(dh2_ref)

    def chunk(cols):
        we, wr = we_ref[:, cols], wr_ref[:, cols]
        hidden, slope = gelu_both(dot(h2_ref[...], we) + be_ref[:, cols])
        dexp = (dot(g_ref[...], wr) * slope).astype(bf16)
        be_grad_ref[:, cols] = row_sum(dexp.astype(f32))
        out_ref[...] += dot_cols(hidden.astype(bf16), wr)
        dh2_ref[...] += dot_cols(dexp, we)

    @pl.loop(0, full)
    def _(i):
        chunk(pl.ds(pl.multiple_of(i * 512, 512), 512))

    if rest:
        chunk(slice(done, done + rest))


def middle_back_kernel(
    mid_ref, mine_ref, other_ref, g_ref, gain_ref, wo_ref, att_ref,
    dmid_ref, datt_ref, wo_grad_ref, gain_grad_ref, shift_grad_ref, bo_grad_ref, br_grad_ref,
):
    dh2 = mine_ref[...] + other_ref[...]
    normed, scale = norm_parts(mid_ref[...])
    gain_grad_ref[...] = row_sum(dh2 * normed)
    shift_grad_ref[...] = row_sum(dh2)
    g = g_ref[...].astype(f32)
    br_grad_ref[...] = row_sum(g)
    dmid = g + norm_back(normed, scale, dh2, gain_ref[...])
    dmid_ref[...] = dmid
    branch = dmid.astype(bf16)
    bo_grad_ref[...] = row_sum(branch.astype(f32))
    datt_ref[...] = dot(branch, wo_ref[...]).astype(bf16)
    wo_grad_ref[...] = dot_rows(branch, att_ref[...]).astype(bf16)


def attend_back_kernel(
    q_ref, k_ref, v_ref, log_ref, mask_ref, datt_ref, wq_ref, wk_ref, wv_ref,
    dq_ref, dk_ref, dv_ref, part_ref, bq_grad_ref, bv_grad_ref,
):
    same = mask_ref[...] > 0.5
    for h in range(q_ref.shape[1] // HD):
        cols = slice(h * HD, (h + 1) * HD)
        q, k, v, datt = q_ref[:, cols], k_ref[:, cols], v_ref[:, cols], datt_ref[:, cols]
        s = jnp.where(same, dot_cols(q, k) * HD ** (-0.5), masked_score)
        prob = jnp.exp(s - log_ref[:, h : h + 1])
        dprob = dot_cols(datt, v)
        ds = (prob * (dprob - lane_sum(prob * dprob))).astype(bf16)
        dq_ref[:, cols] = (dot(ds, k) * HD ** (-0.5)).astype(bf16)
        dk_ref[:, cols] = (dot_rows(ds, q) * HD ** (-0.5)).astype(bf16)
        dv_ref[:, cols] = dot_rows(prob.astype(bf16), datt).astype(bf16)
    part_ref[...] = (
        dot_cols(dq_ref[...], wq_ref[...])
        + dot_cols(dk_ref[...], wk_ref[...])
        + dot_cols(dv_ref[...], wv_ref[...])
    )
    bq_grad_ref[...] = row_sum(dq_ref[...].astype(f32))
    bv_grad_ref[...] = row_sum(dv_ref[...].astype(f32))


def attend_weights_kernel(h1_ref, dq_ref, dk_ref, dv_ref, wq_ref, wk_ref, wv_ref):
    wq_ref[...] = dot_rows(h1_ref[...], dq_ref[...]).astype(bf16)
    wk_ref[...] = dot_rows(h1_ref[...], dk_ref[...]).astype(bf16)
    wv_ref[...] = dot_rows(h1_ref[...], dv_ref[...]).astype(bf16)


def back_pick(len_ref, own_ref, n_dev, cap, half_rows):
    me, core = place()
    base, _ = my_span(len_ref[...].astype(f32), own_ref[...].astype(f32), me)
    half, index = block_slots(base, n_dev, cap, half_rows)
    index = jnp.where(half == core, index, -1.0)
    return one_hot(index, (cap, n_dev * half_rows), 1)


def out_kernel(n_dev, half_rows, len_ref, own_ref, mid_ref, mine_ref, other_ref, bias_ref, back_ref):
    out = mid_ref[...] + (mine_ref[...] + other_ref[...] + bias_ref[...])
    pick = back_pick(len_ref, own_ref, n_dev, out.shape[0], half_rows)
    back_ref[...] = dot_rows(pick, out.astype(bf16)).astype(bf16)


def first_back_kernel(
    n_dev, half_rows, len_ref, own_ref, x_ref, mine_ref, other_ref, gain_ref, dmid_ref,
    back_ref, gain_grad_ref, shift_grad_ref,
):
    dh1 = mine_ref[...] + other_ref[...]
    normed, scale = norm_parts(x_ref[...].astype(f32))
    gain_grad_ref[...] = row_sum(dh1 * normed)
    shift_grad_ref[...] = row_sum(dh1)
    dx = dmid_ref[...] + norm_back(normed, scale, dh1, gain_ref[...])
    pick = back_pick(len_ref, own_ref, n_dev, dx.shape[0], half_rows)
    back_ref[...] = dot_rows(pick, dx.astype(bf16)).astype(bf16)


def home_kernel(n_dev, half_rows, len_ref, own_ref, mine_ref, other_ref, out_ref):
    me, core = place()
    tokens = out_ref.shape[0]
    half, index = token_slots(
        len_ref[...].astype(f32), own_ref[...].astype(f32), me, n_dev, tokens, half_rows
    )
    index = jnp.where(half == core, index, index + n_dev * half_rows)
    rows = jnp.concatenate([mine_ref[...], other_ref[...]], axis=0)
    pick = one_hot(index, (rows.shape[0], tokens), 0)
    out_ref[...] = dot_rows(pick, rows).astype(bf16)


def mlp_weights_kernel(line, h2_ref, g_ref, *refs):
    n_far = 2 * (line - 1)
    h2_far, g_far = refs[:n_far], refs[n_far : 2 * n_far]
    we_ref, be_ref, wr_ref, wr_grad_ref, we_grad_ref, h2_all, g_all, h2_t, g_t = refs[2 * n_far :]
    cap, width = h2_ref.shape
    part = wr_grad_ref.shape[0]
    for rows, first, far in ((h2_all, h2_ref, h2_far), (g_all, g_ref, g_far)):
        rows[:cap, :] = first[...]
        for i, ref in enumerate(far):
            rows[cap + i * (cap // 2) : cap + (i + 1) * (cap // 2), :] = ref[...]
    share = lax.axis_index("dp") // (lax.axis_size("dp") // line)
    first_row = (share * part).astype(f32)
    pick = one_hot(iota((part, width), 0) + first_row, (part, width), 1)
    h2_t[...] = dot_cols(pick, h2_all[...]).astype(bf16)
    g_t[...] = dot_cols(pick, g_all[...]).astype(bf16)
    full, done, rest = column_chunks(we_ref.shape[1], 256)

    def chunk(cols):
        hidden, slope = gelu_both(dot(h2_all[...], we_ref[:, cols]) + be_ref[:, cols])
        dexp = (dot(g_all[...], wr_ref[:, cols]) * slope).astype(bf16)
        wr_grad_ref[:, cols] = dot(g_t[...], hidden.astype(bf16)).astype(bf16)
        we_grad_ref[:, cols] = dot(h2_t[...], dexp).astype(bf16)

    @pl.loop(0, full)
    def _(i):
        chunk(pl.ds(pl.multiple_of(i * 256, 256), 256))

    if rest:
        chunk(slice(done, done + rest))


def call(kernel, name, outs, *ins, scratch=(), vmem=40):
    return pl.pallas_call(
        kernel,
        name=name,
        out_shape=[jax.ShapeDtypeStruct(shape, dtype) for shape, dtype in outs],
        in_specs=[pl.BlockSpec(memory_space=pltpu.VMEM)] * len(ins),
        out_specs=[pl.BlockSpec(memory_space=pltpu.VMEM)] * len(outs),
        scratch_shapes=list(scratch),
        compiler_params=pltpu.CompilerParams(vmem_limit_bytes=vmem * MIB),
    )(*ins)


def swap_cores(values):
    return lax.ppermute(values, "tensor", [(0, 1), (1, 0)])


def swap_dp(values, flip):
    return lax.ppermute(values, "dp", [(i, i ^ flip) for i in range(lax.axis_size("dp"))])


def spread(rows):
    return lax.all_to_all(rows, "dp", split_axis=0, concat_axis=0, tiled=True)


def scatter_sum(partial, order):
    me = lax.axis_index("dp")
    bits = sorted(order, reverse=True)
    rows = partial.shape[0] // 2 ** len(bits)
    value = partial.reshape((2,) * len(bits) + (rows, partial.shape[1]))
    for step, bit in enumerate(order):
        axis = bits.index(bit)
        bits.remove(bit)
        mine = (me >> bit) & 1
        keep = lax.dynamic_index_in_dim(value, mine, axis, keepdims=False)
        give = lax.dynamic_index_in_dim(value, 1 - mine, axis, keepdims=False)
        total = keep.astype(f32) + swap_dp(give, 1 << bit).astype(f32)
        value = total if step == len(order) - 1 else total.astype(bf16)
    return value


def sum_dp(values):
    flip = 1
    while flip < lax.axis_size("dp"):
        values = values + swap_dp(values, flip)
        flip *= 2
    return values


def on_device(
    patches, cotangent, image_lengths, image_owner, first_gain, first_shift, query_weight,
    query_bias, key_weight, value_weight, value_bias, output_weight, output_bias, second_gain,
    second_shift, expand_weight, expand_bias, reduce_weight, reduce_bias,
):
    n_dev = lax.axis_size("dp")
    tokens, width = patches.shape
    cap = 2 * tokens
    half_rows = cap // n_dev // 2
    heads_width, hidden_width = query_weight.shape[1], expand_weight.shape[1]
    heads = heads_width // HD
    n_bits = n_dev.bit_length() - 1
    line = 4

    def row(vector):
        return vector.reshape(1, -1)

    sizes = (row(image_lengths), row(image_owner))
    half_shape = ((n_dev * half_rows, width), bf16)
    wide32, wide16 = ((cap, width), f32), ((cap, width), bf16)
    head16 = ((cap, heads_width), bf16)
    vector_d, vector_h = ((1, width), f32), ((1, heads_width), f32)
    place_args = (n_dev, half_rows)

    send_x, send_g = call(
        functools.partial(pack_kernel, *place_args), "pack",
        [half_shape, half_shape], *sizes, patches, cotangent,
    )
    recv_x = spread(send_x)
    recv_g = spread(send_g)

    x, h1, q, k, v, logs, mask, attended, branch = call(
        functools.partial(attend_kernel, *place_args), "attend",
        [wide16, wide16, head16, head16, head16, ((cap, heads), f32), ((cap, cap), f32), head16, wide32],
        *sizes, recv_x, swap_cores(recv_x), row(first_gain), row(first_shift),
        query_weight, row(query_bias), key_weight, value_weight, row(value_bias), output_weight,
    )

    (g,) = call(
        functools.partial(unpack_kernel, *place_args), "unpack",
        [wide16], *sizes, recv_g, swap_cores(recv_g),
    )
    core = lax.axis_index("tensor")
    stride = n_dev // line

    def along_line(block):
        half = lax.dynamic_slice_in_dim(block, core * (cap // 2), cap // 2, 0)
        far = [swap_dp(half, stride * i) for i in range(1, line)]
        return far + [swap_cores(rows) for rows in far]

    g_far = along_line(g)

    middle, h2 = call(
        middle_kernel, "middle", [wide32, wide16],
        x, branch, swap_cores(branch), row(output_bias), row(second_gain), row(second_shift),
    )
    h2_far = along_line(h2)
    out_part, dh2, be_grad = call(
        mlp_kernel, "mlp", [wide32, wide32, ((1, hidden_width), f32)],
        h2, g, expand_weight, row(expand_bias), reduce_weight,
    )
    dmid, datt, wo_part, gain2_grad, shift2_grad, bo_grad, br_grad = call(
        middle_back_kernel, "middle_back",
        [wide32, head16, ((width, heads_width), bf16), vector_d, vector_d, vector_d, vector_d],
        middle, dh2, swap_cores(dh2), g, row(second_gain), output_weight, attended,
    )
    dq, dk, dv, dh1, bq_grad, bv_grad = call(
        attend_back_kernel, "attend_back", [head16, head16, head16, wide32, vector_h, vector_h],
        q, k, v, logs, mask, datt, query_weight, key_weight, value_weight,
    )
    wq_part, wk_part, wv_part = call(
        attend_weights_kernel, "attend_weights", [((width, heads_width), bf16)] * 3, h1, dq, dk, dv
    )
    back_grad, gain1_grad, shift1_grad = call(
        functools.partial(first_back_kernel, *place_args), "first_back",
        [half_shape, vector_d, vector_d],
        *sizes, x, dh1, swap_cores(dh1), row(first_gain), dmid,
    )
    (back_out,) = call(
        functools.partial(out_kernel, *place_args), "out", [half_shape],
        *sizes, middle, out_part, swap_cores(out_part), row(reduce_bias),
    )
    home_out = spread(back_out)
    home_grad = spread(back_grad)
    token_shape = ((tokens, width), bf16)
    (mixed,) = call(
        functools.partial(home_kernel, *place_args), "home_out", [token_shape],
        *sizes, home_out, swap_cores(home_out),
    )
    (patch_gradient,) = call(
        functools.partial(home_kernel, *place_args), "home_grad", [token_shape],
        *sizes, home_grad, swap_cores(home_grad),
    )

    wr_part, we_part = call(
        functools.partial(mlp_weights_kernel, line), "mlp_weights",
        [((width // line, hidden_width), bf16)] * 2,
        h2, g, *h2_far, *g_far, expand_weight, row(expand_bias), reduce_weight,
        scratch=[pltpu.VMEM((line * cap, width), bf16)] * 2
        + [pltpu.VMEM((width // line, line * cap), bf16)] * 2,
        vmem=56,
    )

    low_bits, line_bits = list(range(n_bits - 2)), [n_bits - 2, n_bits - 1]
    one_way, other_way = low_bits, low_bits[1::-1] + low_bits[2:]
    wo_sum = scatter_sum(wo_part, one_way + line_bits)
    wv_sum = scatter_sum(wv_part, one_way + line_bits)
    wk_sum = scatter_sum(wk_part, other_way + line_bits)
    wq_sum = scatter_sum(wq_part, line_bits + one_way)
    wr_sum = scatter_sum(wr_part, one_way)
    we_sum = scatter_sum(we_part, other_way)

    vectors = [
        gain1_grad, shift1_grad, bq_grad, bv_grad, bo_grad, gain2_grad, shift2_grad, be_grad, br_grad,
    ]
    total = sum_dp(jnp.concatenate([v.reshape(-1) for v in vectors]))
    sums, at = [], 0
    for vector in vectors:
        sums.append(total[at : at + vector.size])
        at += vector.size
    gain1_sum, shift1_sum, bq_sum, bv_sum, bo_sum, gain2_sum, shift2_sum, be_sum, br_sum = sums
    return (
        mixed, patch_gradient, gain1_sum, shift1_sum, wq_sum, bq_sum, wk_sum, wv_sum, bv_sum,
        wo_sum, bo_sum, gain2_sum, shift2_sum, we_sum, be_sum, wr_sum, br_sum,
    )


def solution(mesh):
    rows, all_same = P("dp", None), P()
    cols, vector = P(None, "tensor"), P("tensor")
    both = P("dp", "tensor")
    in_specs = (
        rows, rows, all_same, all_same, all_same, all_same, cols, vector, cols, cols, vector, cols,
        all_same, all_same, all_same, cols, vector, cols, all_same,
    )
    out_specs = (
        rows, rows, all_same, all_same, both, vector, both, both, vector, both, all_same, all_same,
        all_same, both, vector, both, all_same,
    )
    return jax.shard_map(
        on_device, mesh=mesh, in_specs=in_specs, out_specs=out_specs, check_vma=False
    )
```

```python
import functools

import jax
import jax.numpy as jnp
from jax import lax
from jax.experimental import pallas as pl
from jax.experimental.pallas import tpu as pltpu
from jax.sharding import PartitionSpec as P

HD = 72
masked_score = -1000000000.0
norm_eps = 1e-06
gelu_scale = 0.7978845608028654
gelu_cubic = 0.044715
f32 = jnp.float32
bf16 = jnp.bfloat16
MIB = 1024 * 1024


def dot(left, right):
    return lax.dot_general(left, right, (((1,), (0,)), ((), ())), preferred_element_type=f32)


def dot_cols(left, right):
    return lax.dot_general(left, right, (((1,), (1,)), ((), ())), preferred_element_type=f32)


def dot_rows(left, right):
    return lax.dot_general(left, right, (((0,), (0,)), ((), ())), preferred_element_type=f32)


def iota(shape, dim):
    return lax.broadcasted_iota(jnp.int32, shape, dim).astype(f32)


def row_sum(values):
    return jnp.sum(values, axis=0, keepdims=True)


def lane_sum(values):
    return jnp.sum(values, axis=1, keepdims=True)


def lane_mean(values):
    return jnp.mean(values, axis=1, keepdims=True)


def my_span(lengths, owners, me):
    base = lane_sum(jnp.where(owners < me, lengths, 0.0))
    used = lane_sum(jnp.where(owners == me, lengths, 0.0))
    return base, used


def token_slots(lengths, owners, me, n_dev, tokens, half_rows):
    device = iota((n_dev, lengths.shape[1]), 0)
    base = lane_sum(jnp.where(owners < device, lengths, 0.0))
    pos = iota((1, tokens), 1) * n_dev + me
    below = base <= pos
    target = row_sum(jnp.where(below, 1.0, 0.0)) - 1.0
    start = jnp.max(jnp.where(below, base, -1.0), axis=0, keepdims=True)
    slot = jnp.floor((pos - start) * (1.0 / n_dev))
    half = jnp.floor(slot * (1.0 / half_rows))
    return half, target * half_rows + slot - half * half_rows


def block_slots(base, n_dev, cap, half_rows):
    p = iota((cap, 1), 0)
    pos = base + p
    source = pos - n_dev * jnp.floor(pos * (1.0 / n_dev))
    slot = jnp.floor(p * (1.0 / n_dev))
    half = jnp.floor(slot * (1.0 / half_rows))
    return half, source * half_rows + slot - half * half_rows


def one_hot(index, shape, dim):
    return jnp.where(index == iota(shape, dim), 1.0, 0.0).astype(bf16)


def lane_pad(size):
    return -(-size // 128) * 128


def place():
    return lax.axis_index("dp").astype(f32), lax.axis_index("tensor").astype(f32)


def norm_parts(values):
    centered = values - lane_mean(values)
    scale = lax.rsqrt(lane_mean(centered * centered) + norm_eps)
    return centered * scale, scale


def norm_back(normed, scale, grad, gain):
    inner = grad * gain
    return scale * (inner - lane_mean(inner) - normed * lane_mean(inner * normed))


def gelu_both(values):
    square = values * values
    bent = jnp.tanh(gelu_scale * values * (1.0 + gelu_cubic * square))
    half = 0.5 * (1.0 + bent)
    slope = half + 0.5 * values * (1.0 - bent * bent) * (
        gelu_scale * (1.0 + 3.0 * gelu_cubic * square)
    )
    return values * half, slope


def flip_of(block, order):
    flip = 0 * block
    for step, bit in enumerate(order):
        flip = flip | (((block >> (len(order) - 1 - step)) & 1) << bit)
    return flip


def feature_pick(rows, width, n_dev, order):
    owner_rows = width // n_dev
    i = iota((rows, 1), 0)
    block = jnp.floor((i + 0.5) * (1.0 / owner_rows))
    owner = flip_of(block.astype(jnp.int32), order) ^ lax.axis_index("dp")
    return one_hot(owner.astype(f32) * owner_rows + (i - block * owner_rows), (rows, width), 1)


def pack_kernel(n_dev, half_rows, len_ref, own_ref, x_ref, g_ref, send_ref):
    me, core = place()
    half, index = token_slots(
        len_ref[...].astype(f32), own_ref[...].astype(f32), me, n_dev, x_ref.shape[0], half_rows
    )
    target = jnp.floor(index * (1.0 / half_rows))
    index = jnp.where(half == core, index + target * half_rows, -1e6)
    shape = (2 * n_dev * half_rows, x_ref.shape[0])
    rows = dot(one_hot(index, shape, 0), x_ref[...])
    rows += dot(one_hot(index + half_rows, shape, 0), g_ref[...])
    send_ref[...] = rows.astype(bf16)


def block_pick(len_ref, own_ref, n_dev, cap, half_rows, kind):
    me, core = place()
    base, _ = my_span(len_ref[...].astype(f32), own_ref[...].astype(f32), me)
    half, index = block_slots(base, n_dev, cap, half_rows)
    source = jnp.floor(index * (1.0 / half_rows))
    index = index + (source + kind) * half_rows
    index = jnp.where(half == core, index, index + 2 * n_dev * half_rows)
    return one_hot(index, (cap, 2 * cap), 1)


def unpack_kernel(n_dev, half_rows, len_ref, own_ref, mine_ref, other_ref, out_ref):
    cap = out_ref.shape[0]
    pick = block_pick(len_ref, own_ref, n_dev, cap, half_rows, 1)
    rows = jnp.concatenate([mine_ref[...], other_ref[...]], axis=0)
    out_ref[...] = dot(pick, rows).astype(bf16)


def image_mask(len_ref, own_ref, cap):
    lengths, owners = len_ref[...].astype(f32), own_ref[...].astype(f32)
    me, _ = place()
    base, used = my_span(lengths, owners, me)
    n_img = lengths.shape[1]
    starts = lane_sum(
        jnp.where(iota((n_img, n_img), 1) < iota((n_img, n_img), 0), lengths, 0.0)
    )
    p = iota((1, cap), 1)
    count = row_sum(jnp.where(starts <= base + p, 1.0, 0.0))
    seg_row = jnp.where(p < used, count, 0.0)
    on_diagonal = iota((cap, cap), 0) == iota((cap, cap), 1)
    seg_col = lane_sum(jnp.where(on_diagonal, seg_row, 0.0))
    return jnp.where(seg_col == seg_row, 1.0, 0.0)


class Vectors:
    def __init__(self, width, heads_width, hidden_width):
        self.at = {}
        end = 0
        for name, size in (
            ("gain1", width), ("shift1", width), ("bo", width), ("gain2", width),
            ("shift2", width), ("br", width), ("be", hidden_width), ("bq", heads_width),
            ("bv", heads_width),
        ):
            self.at[name] = slice(end, end + size)
            end += lane_pad(size)
        self.size = end


def attend_kernel(
    n_dev, half_rows, vec, len_ref, own_ref, mine_ref, other_ref, vec_ref,
    wq_ref, wk_ref, wv_ref, wo_ref,
    x_ref, h1_ref, q_ref, k_ref, v_ref, log_ref, mask_ref, att_ref, part_ref,
):
    cap = x_ref.shape[0]
    pick = block_pick(len_ref, own_ref, n_dev, cap, half_rows, 0)
    rows = jnp.concatenate([mine_ref[...], other_ref[...]], axis=0)
    x = dot(pick, rows)
    x_ref[...] = x.astype(bf16)
    same = image_mask(len_ref, own_ref, cap)
    mask_ref[...] = same
    normed, _ = norm_parts(x)
    h1 = (normed * vec_ref[:, vec.at["gain1"]] + vec_ref[:, vec.at["shift1"]]).astype(bf16)
    h1_ref[...] = h1
    q_ref[...] = (dot_cols(h1, wq_ref[...]) + vec_ref[:, vec.at["bq"]]).astype(bf16)
    k_ref[...] = dot_cols(h1, wk_ref[...]).astype(bf16)
    v_ref[...] = (dot_cols(h1, wv_ref[...]) + vec_ref[:, vec.at["bv"]]).astype(bf16)
    for h in range(q_ref.shape[1] // HD):
        cols = slice(h * HD, (h + 1) * HD)
        s = dot_cols(q_ref[:, cols], k_ref[:, cols]) * HD ** (-0.5)
        s = jnp.where(same > 0.5, s, masked_score)
        top = jnp.max(s, axis=1, keepdims=True)
        e = jnp.exp(s - top)
        total = lane_sum(e)
        log_ref[:, h : h + 1] = top + jnp.log(total)
        att_ref[:, cols] = dot((e / total).astype(bf16), v_ref[:, cols]).astype(bf16)
    part_ref[...] = dot(att_ref[...], wo_ref[...])


def middle_kernel(vec, x_ref, mine_ref, other_ref, vec_ref, mid_ref, h2_ref, h2_half_ref):
    middle = x_ref[...].astype(f32) + (
        mine_ref[...] + other_ref[...] + vec_ref[:, vec.at["bo"]]
    )
    mid_ref[...] = middle
    normed, _ = norm_parts(middle)
    h2_ref[...] = (
        normed * vec_ref[:, vec.at["gain2"]] + vec_ref[:, vec.at["shift2"]]
    ).astype(bf16)
    rows = h2_half_ref.shape[0]
    start = lax.axis_index("tensor") * rows
    h2_half_ref[...] = h2_ref[pl.ds(pl.multiple_of(start, rows), rows), :]


def chunks_of(width, step):
    full = width // step
    return full, full * step, width - full * step


def mlp_kernel(vec, h2_ref, g_ref, we_ref, vec_ref, wr_ref, out_ref, dh2_ref, be_grad_ref):
    step = 512
    full, done, rest = chunks_of(we_ref.shape[0], step)
    first = vec.at["be"].start
    out_ref[...] = jnp.zeros_like(out_ref)
    dh2_ref[...] = jnp.zeros_like(dh2_ref)
    be_grad_ref[...] = jnp.zeros_like(be_grad_ref)

    def chunk(rows, lanes, bias):
        we, wr = we_ref[rows, :], wr_ref[rows, :]
        hidden, slope = gelu_both(dot_cols(h2_ref[...], we) + vec_ref[:, bias])
        dexp = (dot_cols(g_ref[...], wr) * slope).astype(bf16)
        be_grad_ref[:, lanes] = row_sum(dexp.astype(f32))
        out_ref[...] += dot(hidden.astype(bf16), wr)
        dh2_ref[...] += dot(dexp, we)

    @pl.loop(0, full)
    def _(i):
        at = pl.multiple_of(i * step, step)
        lanes = pl.ds(at, step)
        chunk(lanes, lanes, pl.ds(pl.multiple_of(first + at, 128), step))

    if rest:
        lanes = slice(done, done + rest)
        chunk(lanes, lanes, slice(first + done, first + done + rest))


def middle_back_kernel(
    vec, mid_ref, mine_ref, other_ref, g_ref, vec_ref, wo_ref,
    dmid_ref, branch_ref, datt_ref, vec_grad_ref,
):
    width = mid_ref.shape[1]
    dh2 = mine_ref[...] + other_ref[...]
    normed, scale = norm_parts(mid_ref[...])
    g = g_ref[...].astype(f32)
    dmid = g + norm_back(normed, scale, dh2, vec_ref[:, vec.at["gain2"]])
    dmid_ref[...] = dmid
    branch = dmid.astype(bf16)
    branch_ref[...] = branch
    datt_ref[...] = dot_cols(branch, wo_ref[...]).astype(bf16)
    sums = [branch.astype(f32), dh2 * normed, dh2, g]
    for i, values in enumerate(sums):
        vec_grad_ref[:, i * width : (i + 1) * width] = row_sum(values)


def attend_back_kernel(
    q_ref, k_ref, v_ref, log_ref, mask_ref, datt_ref, wq_ref, wk_ref, wv_ref,
    dq_ref, dk_ref, dv_ref, part_ref, vec_grad_ref,
):
    same = mask_ref[...] > 0.5
    heads_width = q_ref.shape[1]
    for h in range(heads_width // HD):
        cols = slice(h * HD, (h + 1) * HD)
        q, k, v, datt = q_ref[:, cols], k_ref[:, cols], v_ref[:, cols], datt_ref[:, cols]
        s = jnp.where(same, dot_cols(q, k) * HD ** (-0.5), masked_score)
        prob = jnp.exp(s - log_ref[:, h : h + 1])
        dprob = dot_cols(datt, v)
        ds = (prob * (dprob - lane_sum(prob * dprob))).astype(bf16)
        dq_ref[:, cols] = (dot(ds, k) * HD ** (-0.5)).astype(bf16)
        dk_ref[:, cols] = (dot_rows(ds, q) * HD ** (-0.5)).astype(bf16)
        dv_ref[:, cols] = dot_rows(prob.astype(bf16), datt).astype(bf16)
    part_ref[...] = (
        dot(dq_ref[...], wq_ref[...])
        + dot(dk_ref[...], wk_ref[...])
        + dot(dv_ref[...], wv_ref[...])
    )
    vec_grad_ref[...] = jnp.zeros_like(vec_grad_ref)
    vec_grad_ref[:, :heads_width] = row_sum(dq_ref[...].astype(f32))
    second = lane_pad(heads_width)
    vec_grad_ref[:, second : second + heads_width] = row_sum(dv_ref[...].astype(f32))


def put_transposed(turned_ref, out_ref, values, n_dev, order):
    width = values.shape[1]
    owner_rows = width // n_dev
    if owner_rows % 8:
        out_ref[...] = dot_cols(feature_pick(width, width, n_dev, order), values)
        return
    me = lax.axis_index("dp")
    for block in range(n_dev):
        start = pl.multiple_of((me ^ flip_of(block, order)) * owner_rows, 8)
        rows = slice(block * owner_rows, (block + 1) * owner_rows)
        out_ref[rows, :] = turned_ref[pl.ds(start, owner_rows), :]


def attend_weights_kernel(
    n_dev, orders, h1_ref, branch_ref, dq_ref, dk_ref, dv_ref, att_ref, *refs
):
    (turned_ref, turned_branch, left_ref, branch_left_ref), outs = refs[-4:], refs[:-4]
    heads_width = dq_ref.shape[1]
    total = 4 * heads_width // len(orders)
    half = h1_ref.shape[1] // 2
    turned_ref[...] = jnp.transpose(h1_ref[...].astype(f32))
    turned_branch[...] = jnp.transpose(branch_ref[...].astype(f32))
    right = [dq_ref, dk_ref, dv_ref, att_ref]
    for group, order in enumerate(orders):
        put_transposed(turned_ref, left_ref, h1_ref[...], n_dev, order)
        keep_ref, give_ref = outs[2 * group], outs[2 * group + 1]
        for i, ref in enumerate(right):
            first = max(i * heads_width, group * total)
            last = min((i + 1) * heads_width, (group + 1) * total)
            if first >= last:
                continue
            if i == 3:
                put_transposed(turned_branch, branch_left_ref, branch_ref[...], n_dev, order)
            left = (branch_left_ref if i == 3 else left_ref)[...].astype(bf16)
            cols = ref[:, first - i * heads_width : last - i * heads_width]
            product = dot(left, cols).astype(bf16)
            lanes = slice(first - group * total, last - group * total)
            keep_ref[:, lanes] = product[:half, :]
            give_ref[:, lanes] = product[half:, :]


def back_slots(len_ref, own_ref, n_dev, cap, half_rows):
    me, core = place()
    base, _ = my_span(len_ref[...].astype(f32), own_ref[...].astype(f32), me)
    half, index = block_slots(base, n_dev, cap, half_rows)
    source = jnp.floor(index * (1.0 / half_rows))
    return jnp.where(half == core, index + source * half_rows, -1e6)


def first_back_kernel(
    n_dev, half_rows, vec, len_ref, own_ref, x_ref, mine_ref, other_ref, vec_ref, dmid_ref,
    mid_ref, out_mine_ref, out_other_ref, back_ref, vec_grad_ref,
):
    width = x_ref.shape[1]
    cap = x_ref.shape[0]
    dh1 = mine_ref[...] + other_ref[...]
    normed, scale = norm_parts(x_ref[...].astype(f32))
    vec_grad_ref[:, :width] = row_sum(dh1 * normed)
    vec_grad_ref[:, width:] = row_sum(dh1)
    dx = dmid_ref[...] + norm_back(normed, scale, dh1, vec_ref[:, vec.at["gain1"]])
    out = mid_ref[...] + (
        out_mine_ref[...] + out_other_ref[...] + vec_ref[:, vec.at["br"]]
    )
    index = back_slots(len_ref, own_ref, n_dev, cap, half_rows)
    rows = dot_rows(one_hot(index, (cap, cap), 1), out.astype(bf16))
    rows += dot_rows(one_hot(index + half_rows, (cap, cap), 1), dx.astype(bf16))
    back_ref[...] = rows.astype(bf16)


def home_kernel(n_dev, half_rows, len_ref, own_ref, mine_ref, other_ref, out_ref, grad_ref):
    me, core = place()
    tokens = out_ref.shape[0]
    half, index = token_slots(
        len_ref[...].astype(f32), own_ref[...].astype(f32), me, n_dev, tokens, half_rows
    )
    index = index + jnp.floor(index * (1.0 / half_rows)) * half_rows
    index = jnp.where(half == core, index, index + 2 * n_dev * half_rows)
    rows = jnp.concatenate([mine_ref[...], other_ref[...]], axis=0)
    shape = (rows.shape[0], tokens)
    out_ref[...] = dot_rows(one_hot(index, shape, 0), rows).astype(bf16)
    grad_ref[...] = dot_rows(one_hot(index + half_rows, shape, 0), rows).astype(bf16)


def mlp_weights_kernel(
    flips, orders, n_dev, half_rows, vec, len_ref, own_ref, h2_ref, h2_mine_ref, h2_other_ref, g_ref,
    g_mine_ref, g_other_ref, we_ref, vec_ref, wr_ref, wr_keep, wr_give, we_keep, we_give,
    h2_all, g_all, h2_t, g_t,
):
    cap, width = h2_ref.shape
    hidden_width = we_ref.shape[0]
    half_cap = cap // 2
    me = lax.axis_index("dp")
    _, core = place()
    lengths, owners = len_ref[...].astype(f32), own_ref[...].astype(f32)
    h2_all[:cap, :] = h2_ref[...]
    g_all[:cap, :] = g_ref[...]
    for i, flip in enumerate(flips):
        far = slice(i * half_cap, (i + 1) * half_cap)
        rows = slice((i + 1) * cap, (i + 2) * cap)
        h2_all[rows, :] = jnp.concatenate([h2_mine_ref[far, :], h2_other_ref[far, :]], axis=0)
        base, _ = my_span(lengths, owners, (me ^ flip).astype(f32))
        half, index = block_slots(base, n_dev, cap, half_rows)
        index = jnp.where(half == core, index, index + half_cap)
        index = jnp.where(core == 0.0, index, jnp.concatenate([index[half_cap:], index[:half_cap]]))
        g_rows = jnp.concatenate([g_mine_ref[far, :], g_other_ref[far, :]], axis=0)
        g_all[rows, :] = dot(one_hot(index, (cap, cap), 1), g_rows).astype(bf16)
    part = h2_t.shape[0]
    g_t[...] = dot_cols(feature_pick(part, width, n_dev, orders[0]), g_all[...]).astype(bf16)
    h2_t[...] = dot_cols(feature_pick(part, width, n_dev, orders[1]), h2_all[...]).astype(bf16)
    step = 256
    full, done, rest = chunks_of(hidden_width, step)
    first = vec.at["be"].start

    def chunk(rows, lanes, bias):
        we, wr = we_ref[rows, :], wr_ref[rows, :]
        hidden, slope = gelu_both(dot_cols(h2_all[...], we) + vec_ref[:, bias])
        dexp = (dot_cols(g_all[...], wr) * slope).astype(bf16)
        wr_grad = dot(g_t[...], hidden.astype(bf16)).astype(bf16)
        wr_keep[:, lanes] = wr_grad[: part // 2, :]
        wr_give[:, lanes] = wr_grad[part // 2 :, :]
        we_grad = dot(h2_t[...], dexp).astype(bf16)
        we_keep[:, lanes] = we_grad[: part // 2, :]
        we_give[:, lanes] = we_grad[part // 2 :, :]

    @pl.loop(0, full)
    def _(i):
        at = pl.multiple_of(i * step, step)
        chunk(pl.ds(at, step), pl.ds(at, step), pl.ds(pl.multiple_of(first + at, 128), step))

    if rest:
        end = done + rest
        chunk(slice(done, end), slice(done, end), slice(first + done, first + end))


def turn_kernel(*refs):
    count = len(refs) // 4
    for i in range(count):
        total = refs[2 * i][...].astype(f32) + refs[2 * i + 1][...].astype(f32)
        half = total.shape[0] // 2
        refs[2 * count + 2 * i][...] = total[:half, :]
        refs[2 * count + 2 * i + 1][...] = total[half:, :].astype(bf16)


def last_kernel(heads_width, *refs):
    count = (len(refs) - 4) // 2
    total = 4 * heads_width // count
    for group in range(count):
        value = refs[2 * group][...].astype(f32) + refs[2 * group + 1][...].astype(f32)
        for i, ref in enumerate(refs[2 * count :]):
            first = max(i * heads_width, group * total)
            last = min((i + 1) * heads_width, (group + 1) * total)
            if first < last:
                lanes = slice(first - i * heads_width, last - i * heads_width)
                ref[:, lanes] = value[:, first - group * total : last - group * total]


def call(kernel, name, outs, *ins, scratch=(), vmem=16):
    return pl.pallas_call(
        kernel,
        name=name,
        out_shape=[jax.ShapeDtypeStruct(shape, dtype) for shape, dtype in outs],
        in_specs=[pl.BlockSpec(memory_space=pltpu.VMEM)] * len(ins),
        out_specs=[pl.BlockSpec(memory_space=pltpu.VMEM)] * len(outs),
        scratch_shapes=list(scratch),
        compiler_params=pltpu.CompilerParams(vmem_limit_bytes=vmem * MIB),
    )(*ins)


def swap_cores(values):
    return lax.ppermute(values, "tensor", [(0, 1), (1, 0)])


def swap_dp(values, flip):
    return lax.ppermute(values, "dp", [(i, i ^ flip) for i in range(lax.axis_size("dp"))])


def spread(rows):
    return lax.all_to_all(rows, "dp", split_axis=0, concat_axis=0, tiled=True)


def after(values, earlier):
    return lax.optimization_barrier((values, earlier))[0]


def turn(name, pairs):
    rows = pairs[0][0].shape[0] // 2
    if rows % 8:
        totals = [keep.astype(f32) + got.astype(f32) for keep, got in pairs]
        return [(total[:rows], total[rows:].astype(bf16)) for total in totals]
    outs = []
    for keep, _ in pairs:
        shape = (rows, keep.shape[1])
        outs += [(shape, f32), (shape, bf16)]
    flat = call(turn_kernel, name, outs, *[values for pair in pairs for values in pair])
    return list(zip(flat[::2], flat[1::2]))


def sum_dp(values):
    flip = 1
    while flip < lax.axis_size("dp"):
        values = values + swap_dp(values, flip)
        flip *= 2
    return values


def on_device(
    patches, cotangent, image_lengths, image_owner, first_gain, first_shift, query_weight,
    query_bias, key_weight, value_weight, value_bias, output_weight, output_bias, second_gain,
    second_shift, expand_weight, expand_bias, reduce_weight, reduce_bias,
):
    n_dev = lax.axis_size("dp")
    tokens, width = patches.shape
    cap = 2 * tokens
    half_rows = cap // n_dev // 2
    heads_width, hidden_width = query_weight.shape[1], expand_weight.shape[1]
    heads = heads_width // HD
    n_bits = n_dev.bit_length() - 1
    far_bits = (1, n_bits - 2)
    flips = (1 << far_bits[0], 1 << far_bits[1], (1 << far_bits[0]) | (1 << far_bits[1]))
    rest = [bit for bit in range(n_bits) if bit not in far_bits]
    mlp_orders = (rest, rest[::-1])
    others = list(range(2, n_bits - 2))
    attend_orders = (
        [0, 1] + others + [n_bits - 1, n_bits - 2],
        [1, n_bits - 2, 0] + others + [n_bits - 1],
        [n_bits - 2, 0, 1] + others + [n_bits - 1],
    )
    wq, wk, wv, wo, we, wr = (
        w.T for w in (query_weight, key_weight, value_weight, output_weight, expand_weight, reduce_weight)
    )
    vec = Vectors(width, heads_width, hidden_width)
    named = dict(
        gain1=first_gain, shift1=first_shift, bo=output_bias, gain2=second_gain,
        shift2=second_shift, br=reduce_bias, be=expand_bias, bq=query_bias, bv=value_bias,
    )
    vectors = jnp.concatenate(
        [jnp.pad(named[n], (0, lane_pad(named[n].shape[0]) - named[n].shape[0])) for n in vec.at]
    ).reshape(1, -1)
    sizes = (image_lengths.reshape(1, -1), image_owner.reshape(1, -1))
    wide32, wide16 = ((cap, width), f32), ((cap, width), bf16)
    half16 = ((cap // 2, width), bf16)
    head16 = ((cap, heads_width), bf16)
    place_args = (n_dev, half_rows)

    (send,) = call(
        functools.partial(pack_kernel, *place_args), "pack", [wide16], *sizes, patches, cotangent
    )
    got = spread(send)
    got_other = swap_cores(got)

    x, h1, q, k, v, logs, mask, attended, branch = call(
        functools.partial(attend_kernel, *place_args, vec), "attend",
        [wide16, wide16, head16, head16, head16, ((cap, heads), f32), ((cap, cap), f32), head16, wide32],
        *sizes, got, got_other, vectors, wq, wk, wv, wo, vmem=20,
    )
    branch_other = swap_cores(branch)
    (g,) = call(
        functools.partial(unpack_kernel, *place_args), "unpack", [wide16], *sizes, got, got_other
    )
    g_half = got.reshape(n_dev, 2, half_rows, width)[:, 1].reshape(cap // 2, width)
    g_near = swap_dp(g_half, flips[0])
    g_next = swap_dp(jnp.concatenate([g_half, g_near]), flips[1])
    g_far = jnp.concatenate([g_near, g_next])

    middle, h2, h2_half = call(
        functools.partial(middle_kernel, vec), "middle", [wide32, wide16, half16],
        x, branch, branch_other, vectors,
    )
    h2_far = jnp.concatenate([swap_dp(h2_half, flip) for flip in flips])
    out_part, dh2, be_grad = call(
        functools.partial(mlp_kernel, vec), "mlp", [wide32, wide32, ((1, lane_pad(hidden_width)), f32)],
        h2, g, we, vectors, wr, vmem=24,
    )
    dmid, branch_grad, datt, vec_grad2 = call(
        functools.partial(middle_back_kernel, vec), "middle_back",
        [wide32, wide16, head16, ((1, 4 * width), f32)],
        middle, dh2, swap_cores(dh2), g, vectors, wo,
    )
    dq, dk, dv, dh1, vec_grad3 = call(
        attend_back_kernel, "attend_back",
        [head16, head16, head16, wide32, ((1, 2 * lane_pad(heads_width)), f32)],
        q, k, v, logs, mask, datt, wq, wk, wv,
    )
    dh1_other = swap_cores(dh1)
    n_groups = len(attend_orders)
    group_shape = ((width // 2, 4 * heads_width // n_groups), bf16)
    turned_scratch = pltpu.VMEM((width, cap), f32)
    pieces = call(
        functools.partial(attend_weights_kernel, n_dev, attend_orders), "attend_weights",
        [group_shape] * (2 * n_groups), h1, branch_grad, dq, dk, dv, attended,
        scratch=[turned_scratch] * 4, vmem=24,
    )
    attend_pairs = list(zip(pieces[::2], pieces[1::2]))

    def send(pairs, orders, step):
        return [(keep, swap_dp(give, 1 << order[step])) for (keep, give), order in zip(pairs, orders)]

    attend_pairs = send(attend_pairs, attend_orders, 0)
    back, vec_grad1 = call(
        functools.partial(first_back_kernel, *place_args, vec), "first_back",
        [wide16, ((1, 2 * width), f32)],
        *sizes, x, dh1, dh1_other, vectors, dmid, middle, out_part, swap_cores(out_part),
    )
    home = spread(back)
    token_shape = ((tokens, width), bf16)
    mixed, patch_gradient = call(
        functools.partial(home_kernel, *place_args), "home", [token_shape] * 2,
        *sizes, home, swap_cores(home),
    )

    far_mine, back = lax.optimization_barrier((jnp.concatenate([h2_far, g_far]), back))
    far_other = swap_cores(far_mine)
    far_rows = h2_far.shape[0]
    part = 4 * (width // n_dev) * (n_dev // 16)
    mlp_piece = ((part // 2, hidden_width), bf16)
    mlp_pieces = call(
        functools.partial(mlp_weights_kernel, flips, mlp_orders, *place_args, vec), "mlp_weights",
        [mlp_piece] * 4, *sizes, h2, far_mine[:far_rows], far_other[:far_rows],
        g, far_mine[far_rows:], far_other[far_rows:], we, vectors, wr,
        scratch=[pltpu.VMEM((4 * cap, width), bf16)] * 2 + [pltpu.VMEM((part, 4 * cap), bf16)] * 2,
        vmem=40,
    )
    mlp_pairs = send(list(zip(mlp_pieces[::2], mlp_pieces[1::2])), mlp_orders, 0)
    attend_pairs = after(attend_pairs, mlp_pieces[0])
    for step in range(1, n_bits):
        attend_pairs = send(turn(f"attend_turn_{step}", attend_pairs), attend_orders, step)
    for step in range(1, len(rest)):
        turned = [turn(f"mlp_turn_{step}_{i}", [pair])[0] for i, pair in enumerate(mlp_pairs)]
        mlp_pairs = send(turned, mlp_orders, step)
    own_shape = ((width // n_dev, heads_width), f32)
    wq_sum, wk_sum, wv_sum, wo_sum = call(
        functools.partial(last_kernel, heads_width), "last", [own_shape] * 4,
        *[values for pair in attend_pairs for values in pair],
    )
    wr_sum, we_sum = [keep.astype(f32) + got.astype(f32) for keep, got in mlp_pairs]

    grads = sum_dp(jnp.concatenate([vec_grad1, vec_grad2, be_grad, vec_grad3], axis=1))
    total = {name: grads[0, at] for name, at in vec.at.items()}
    return (
        mixed, patch_gradient, total["gain1"], total["shift1"], wq_sum, total["bq"], wk_sum, wv_sum,
        total["bv"], wo_sum, total["bo"], total["gain2"], total["shift2"], we_sum, total["be"],
        wr_sum, total["br"],
    )


def solution(mesh):
    rows, all_same = P("dp", None), P()
    cols, vector = P(None, "tensor"), P("tensor")
    both = P("dp", "tensor")
    in_specs = (
        rows, rows, all_same, all_same, all_same, all_same, cols, vector, cols, cols, vector, cols,
        all_same, all_same, all_same, cols, vector, cols, all_same,
    )
    out_specs = (
        rows, rows, all_same, all_same, both, vector, both, both, vector, both, all_same, all_same,
        all_same, both, vector, both, all_same,
    )
    return jax.shard_map(
        on_device, mesh=mesh, in_specs=in_specs, out_specs=out_specs, check_vma=False
    )
```

```python
import functools

import jax
import jax.numpy as jnp
from jax import lax
from jax.experimental import pallas as pl
from jax.experimental.pallas import tpu as pltpu
from jax.sharding import PartitionSpec as P

HD = 72
masked_score = -1000000000.0
norm_eps = 1e-06
gelu_scale = 0.7978845608028654
gelu_cubic = 0.044715
f32 = jnp.float32
bf16 = jnp.bfloat16
MIB = 1024 * 1024


def dot(left, right):
    return lax.dot_general(left, right, (((1,), (0,)), ((), ())), preferred_element_type=f32)


def dot_cols(left, right):
    return lax.dot_general(left, right, (((1,), (1,)), ((), ())), preferred_element_type=f32)


def dot_rows(left, right):
    return lax.dot_general(left, right, (((0,), (0,)), ((), ())), preferred_element_type=f32)


def iota(shape, dim):
    return lax.broadcasted_iota(jnp.int32, shape, dim).astype(f32)


def row_sum(values):
    return jnp.sum(values, axis=0, keepdims=True)


def lane_sum(values):
    return jnp.sum(values, axis=1, keepdims=True)


def lane_mean(values):
    return jnp.mean(values, axis=1, keepdims=True)


def my_span(lengths, owners, me):
    base = lane_sum(jnp.where(owners < me, lengths, 0.0))
    used = lane_sum(jnp.where(owners == me, lengths, 0.0))
    return base, used


def token_slots(lengths, owners, me, n_dev, tokens, half_rows):
    device = iota((n_dev, lengths.shape[1]), 0)
    base = lane_sum(jnp.where(owners < device, lengths, 0.0))
    pos = iota((1, tokens), 1) * n_dev + me
    below = base <= pos
    target = row_sum(jnp.where(below, 1.0, 0.0)) - 1.0
    start = jnp.max(jnp.where(below, base, -1.0), axis=0, keepdims=True)
    slot = jnp.floor((pos - start) * (1.0 / n_dev))
    half = jnp.floor(slot * (1.0 / half_rows))
    return half, target * half_rows + slot - half * half_rows


def block_slots(base, n_dev, cap, half_rows):
    p = iota((cap, 1), 0)
    pos = base + p
    source = pos - n_dev * jnp.floor(pos * (1.0 / n_dev))
    slot = jnp.floor(p * (1.0 / n_dev))
    half = jnp.floor(slot * (1.0 / half_rows))
    return half, source * half_rows + slot - half * half_rows


def one_hot(index, shape, dim):
    return jnp.where(index == iota(shape, dim), 1.0, 0.0).astype(bf16)


def lane_pad(size):
    return -(-size // 128) * 128


def place():
    return lax.axis_index("dp").astype(f32), lax.axis_index("tensor").astype(f32)


def norm_parts(values):
    centered = values - lane_mean(values)
    scale = lax.rsqrt(lane_mean(centered * centered) + norm_eps)
    return centered * scale, scale


def norm_back(normed, scale, grad, gain):
    inner = grad * gain
    return scale * (inner - lane_mean(inner) - normed * lane_mean(inner * normed))


def gelu_both(values):
    square = values * values
    bent = jnp.tanh(gelu_scale * values * (1.0 + gelu_cubic * square))
    half = 0.5 * (1.0 + bent)
    slope = half + 0.5 * values * (1.0 - bent * bent) * (
        gelu_scale * (1.0 + 3.0 * gelu_cubic * square)
    )
    return values * half, slope


def flip_of(block, order):
    flip = 0 * block
    for step, bit in enumerate(order):
        flip = flip | (((block >> (len(order) - 1 - step)) & 1) << bit)
    return flip


def feature_pick(rows, width, n_dev, order):
    owner_rows = width // n_dev
    i = iota((rows, 1), 0)
    block = jnp.floor((i + 0.5) * (1.0 / owner_rows))
    owner = flip_of(block.astype(jnp.int32), order) ^ lax.axis_index("dp")
    return one_hot(owner.astype(f32) * owner_rows + (i - block * owner_rows), (rows, width), 1)


def ordered_rows(out_ref, from_ref, n_dev, order):
    width = from_ref.shape[0]
    owner_rows = width // n_dev
    if owner_rows % 8:
        pick = feature_pick(width, width, n_dev, order)
        out_ref[...] = dot(pick, from_ref[...].astype(bf16))
        return
    me = lax.axis_index("dp")
    for block in range(n_dev):
        start = pl.multiple_of((me ^ flip_of(block, order)) * owner_rows, 8)
        rows = slice(block * owner_rows, (block + 1) * owner_rows)
        out_ref[rows, :] = from_ref[pl.ds(start, owner_rows), :]


class Made:
    def __init__(self, refs):
        self.refs = refs

    def __getitem__(self, name):
        return self.refs[name]

    def put(self, name, value):
        self.refs[name][...] = value.astype(self.refs[name].dtype)


class Far:
    def __init__(self, refs, near, sems):
        self.near = near
        self.copies = {
            name: pltpu.make_async_copy(ref, near[name], sems.at[i])
            for i, (name, ref) in enumerate(refs.items())
        }
        for copy in self.copies.values():
            copy.start()

    def __getitem__(self, name):
        copy = self.copies.pop(name, None)
        if copy is not None:
            copy.wait()
        return self.near[name]


def call(body, name, ins, outs, scratch=(), vmem=16, far=False, us=0.0):
    in_names, out_names = list(ins), list(outs)
    n_in, n_out = len(in_names), len(out_names)

    def kernel(*refs):
        given = dict(zip(in_names, refs))
        made = Made(dict(zip(out_names, refs[n_in:])))
        rest = refs[n_in + n_out :]
        if far:
            given = Far(given, dict(zip(in_names, rest)), rest[n_in])
            rest = rest[n_in + 1 :]
        body(given, made, *rest)

    copies = [pltpu.VMEM(x.shape, x.dtype) for x in ins.values()]
    copies += [pltpu.SemaphoreType.DMA((n_in,))]
    results = pl.pallas_call(
        kernel,
        name=name,
        out_shape=[jax.ShapeDtypeStruct(shape, dtype) for shape, dtype in outs.values()],
        in_specs=[pl.BlockSpec(memory_space=pltpu.HBM if far else pltpu.VMEM)] * n_in,
        out_specs=[pl.BlockSpec(memory_space=pltpu.VMEM)] * n_out,
        scratch_shapes=(copies if far else []) + list(scratch),
        compiler_params=pltpu.CompilerParams(vmem_limit_bytes=vmem * MIB),
    )(*ins.values())
    return dict(zip(out_names, results))


def pack_kernel(n_dev, half_rows, tokens, given, made):
    me, core = place()
    lengths, owners = given["lengths"][...].astype(f32), given["owners"][...].astype(f32)
    half, index = token_slots(lengths, owners, me, n_dev, tokens, half_rows)
    target = jnp.floor(index * (1.0 / half_rows))
    index = jnp.where(half == core, index + target * half_rows, -1e6)
    shape = (2 * n_dev * half_rows, tokens)
    x_pick, g_pick = one_hot(index, shape, 0), one_hot(index + half_rows, shape, 0)
    rows = dot(x_pick, given["x"][...])
    made.put("send", rows + dot(g_pick, given["g"][...]))


def block_rows(given, n_dev, cap, half_rows, kind):
    me, core = place()
    lengths, owners = given["lengths"][...].astype(f32), given["owners"][...].astype(f32)
    base, _ = my_span(lengths, owners, me)
    half, index = block_slots(base, n_dev, cap, half_rows)
    source = jnp.floor(index * (1.0 / half_rows))
    index = index + (source + kind) * half_rows
    index = jnp.where(half == core, index, index + 2 * n_dev * half_rows)
    pick = one_hot(index, (cap, 2 * cap), 1)
    return dot(pick, jnp.concatenate([given["mine"][...], given["other"][...]], axis=0))


def unpack_kernel(n_dev, half_rows, given, made):
    made.put("g", block_rows(given, n_dev, made["g"].shape[0], half_rows, 1))


def image_mask(lengths, owners, cap):
    me, _ = place()
    base, used = my_span(lengths, owners, me)
    n_img = lengths.shape[1]
    starts = lane_sum(
        jnp.where(iota((n_img, n_img), 1) < iota((n_img, n_img), 0), lengths, 0.0)
    )
    p = iota((1, cap), 1)
    count = row_sum(jnp.where(starts <= base + p, 1.0, 0.0))
    seg_row = jnp.where(p < used, count, 0.0)
    on_diagonal = iota((cap, cap), 0) == iota((cap, cap), 1)
    seg_col = lane_sum(jnp.where(on_diagonal, seg_row, 0.0))
    return jnp.where(seg_col == seg_row, 1.0, 0.0)


class Vectors:
    def __init__(self, width, heads_width, hidden_width):
        self.at = {}
        end = 0
        for name, size in (
            ("gain1", width), ("shift1", width), ("bo", width), ("gain2", width),
            ("shift2", width), ("br", width), ("be", hidden_width), ("bq", heads_width),
            ("bv", heads_width),
        ):
            self.at[name] = slice(end, end + size)
            end += lane_pad(size)
        self.size = end


def attend_kernel(n_dev, half_rows, vec, given, made):
    cap = made["x"].shape[0]
    lengths, owners = given["lengths"][...].astype(f32), given["owners"][...].astype(f32)
    same = image_mask(lengths, owners, cap)
    made.put("mask", same)
    x = block_rows(given, n_dev, cap, half_rows, 0)
    made.put("x", x)
    row = given["vec"]
    normed, _ = norm_parts(x)
    h1 = (normed * row[:, vec.at["gain1"]] + row[:, vec.at["shift1"]]).astype(bf16)
    made.put("h1", h1)
    made.put("q", dot_cols(h1, given["wq"][...]) + row[:, vec.at["bq"]])
    made.put("k", dot_cols(h1, given["wk"][...]))
    made.put("v", dot_cols(h1, given["wv"][...]) + row[:, vec.at["bv"]])
    for h in range(made["q"].shape[1] // HD):
        cols = slice(h * HD, (h + 1) * HD)
        s = dot_cols(made["q"][:, cols], made["k"][:, cols]) * HD ** (-0.5)
        s = jnp.where(same > 0.5, s, masked_score)
        top = jnp.max(s, axis=1, keepdims=True)
        e = jnp.exp(s - top)
        total = lane_sum(e)
        made["log"][:, h : h + 1] = top + jnp.log(total)
        made["att"][:, cols] = dot((e / total).astype(bf16), made["v"][:, cols]).astype(bf16)
    made.put("branch", dot(made["att"][...], given["wo"][...]))


def add_cores(given, name):
    return given[name][...].astype(f32) + given[name + "_other"][...].astype(f32)


def add_halves(given, name):
    return jnp.concatenate([add_cores(given, f"{name}_{i}") for i in range(2)], axis=0)


def add_sums(given, which):
    rows = given["sums_0"].shape[0] // 2
    rows = slice(which * rows, (which + 1) * rows)
    halves = [given[f"sums_{i}"][rows, :].astype(f32) for i in range(2)]
    others = [given[f"sums_{i}_other"][rows, :].astype(f32) for i in range(2)]
    return jnp.concatenate([halves[i] + others[i] for i in range(2)], axis=0)


def chunks_of(width, step):
    full = width // step
    return full, full * step, width - full * step


def mlp_kernel(n_dev, half_rows, vec, given, made, out_total, dh2_total):
    cap = made["middle"].shape[0]
    row = given["vec"]
    x = given["x"][...].astype(f32)
    middle = x + (add_cores(given, "branch") + row[:, vec.at["bo"]])
    made.put("middle", middle)
    normed, _ = norm_parts(middle)
    made.put("h2", normed * row[:, vec.at["gain2"]] + row[:, vec.at["shift2"]])
    rows = cap // 2
    start = pl.multiple_of(lax.axis_index("tensor") * rows, rows)
    made["halves"][:rows, :] = made["h2"][pl.ds(start, rows), :]
    made["halves"][rows:, :] = given["g"][pl.ds(start, rows), :]
    step = 512
    full, done, rest = chunks_of(given["we"].shape[0], step)
    first = vec.at["be"].start
    out_total[...] = jnp.zeros_like(out_total)
    dh2_total[...] = jnp.zeros_like(dh2_total)
    made["be_grad"][...] = jnp.zeros_like(made["be_grad"])

    def chunk(rows, lanes, bias):
        we, wr = given["we"][rows, :], given["wr"][rows, :]
        hidden, slope = gelu_both(dot_cols(made["h2"][...], we) + given["vec"][:, bias])
        dexp = (dot_cols(given["g"][...], wr) * slope).astype(bf16)
        made["be_grad"][:, lanes] = row_sum(dexp.astype(f32))
        out_total[...] += dot(hidden.astype(bf16), wr)
        dh2_total[...] += dot(dexp, we)

    @pl.loop(0, full)
    def _(i):
        at = pl.multiple_of(i * step, step)
        lanes = pl.ds(at, step)
        chunk(lanes, lanes, pl.ds(pl.multiple_of(first + at, 128), step))

    if rest:
        lanes = slice(done, done + rest)
        chunk(lanes, lanes, slice(first + done, first + done + rest))
    half = cap // 2
    for i in range(2):
        rows = slice(i * half, (i + 1) * half)
        made[f"sums_{i}"][:half, :] = dh2_total[rows, :].astype(bf16)
        made[f"sums_{i}"][half:, :] = out_total[rows, :].astype(bf16)


def middle_back_kernel(vec, given, made):
    width = given["middle"].shape[1]
    g = given["g"][...].astype(f32)
    normed, scale = norm_parts(given["middle"][...])
    dh2 = add_sums(given, 0)
    dmid = g + norm_back(normed, scale, dh2, given["vec"][:, vec.at["gain2"]])
    made.put("dmid", dmid)
    branch = dmid.astype(bf16)
    made.put("branch_grad", branch)
    made.put("datt", dot_cols(branch, given["wo"][...]))
    for i, values in enumerate([branch.astype(f32), dh2 * normed, dh2, g]):
        made["vec_grad"][:, i * width : (i + 1) * width] = row_sum(values)


def attend_back_kernel(given, made):
    heads_width = made["dq"].shape[1]
    same = given["mask"][...] > 0.5
    for h in range(heads_width // HD):
        cols = slice(h * HD, (h + 1) * HD)
        q, k, v, datt = (given[name][:, cols] for name in ("q", "k", "v", "datt"))
        s = jnp.where(same, dot_cols(q, k) * HD ** (-0.5), masked_score)
        prob = jnp.exp(s - given["log"][:, h : h + 1])
        dprob = dot_cols(datt, v)
        ds = (prob * (dprob - lane_sum(prob * dprob))).astype(bf16)
        made["dq"][:, cols] = (dot(ds, k) * HD ** (-0.5)).astype(bf16)
        made["dk"][:, cols] = (dot_rows(ds, q) * HD ** (-0.5)).astype(bf16)
        made["dv"][:, cols] = dot_rows(prob.astype(bf16), datt).astype(bf16)
    dh1 = dot(made["dq"][...], given["wq"][...])
    dh1 += dot(made["dk"][...], given["wk"][...])
    dh1 += dot(made["dv"][...], given["wv"][...])
    half = dh1.shape[0] // 2
    made.put("dh1_0", dh1[:half, :])
    made.put("dh1_1", dh1[half:, :])
    row = made["vec_grad"]
    row[...] = jnp.zeros_like(row)
    row[:, :heads_width] = row_sum(made["dq"][...].astype(f32))
    second = lane_pad(heads_width)
    row[:, second : second + heads_width] = row_sum(made["dv"][...].astype(f32))


def put_vectors(give_ref, first, rows, values):
    high = values.astype(bf16)
    low = (values - high.astype(f32)).astype(bf16)
    give_ref[first : first + rows, :] = high
    give_ref[first + rows : first + 2 * rows, :] = low
    return high.astype(f32) + low.astype(f32)


def got_vectors(got_ref, rows):
    first = got_ref.shape[0] - 2 * rows
    high = got_ref[first : first + rows, :].astype(f32)
    return high + got_ref[first + rows :, :].astype(f32)


def column_parts(heads_width, total, group):
    for i in range(4):
        first = max(i * heads_width, group * total)
        last = min((i + 1) * heads_width, (group + 1) * total)
        if first < last:
            yield (
                i,
                slice(first - i * heads_width, last - i * heads_width),
                slice(first - group * total, last - group * total),
            )


def attend_weights_kernel(n_dev, orders, vec_names, given, made, h1_t, branch_t, left, branch_left):
    heads_width = given["dq"].shape[1]
    total = 4 * heads_width // len(orders)
    half = given["h1"].shape[1] // 2
    h1_t[...] = jnp.transpose(given["h1"][...].astype(f32))
    branch_t[...] = jnp.transpose(given["branch_grad"][...].astype(f32))
    vec_out = made["vec"]
    columns = vec_out.shape[1]
    vec_out[...] = jnp.zeros_like(vec_out)
    at = 0
    for name in vec_names:
        size = given[name].shape[1]
        done = 0
        while done < size:
            row, lane = (at + done) // columns, (at + done) % columns
            now = min(columns - lane, size - done)
            vec_out[row : row + 1, lane : lane + now] = given[name][:, done : done + now]
            done += now
        at += size
    made.put("vec", put_vectors(made["give0"], half, vec_out.shape[0], vec_out[...]))
    right = ("dq", "dk", "dv", "att")
    for group, order in enumerate(orders):
        ordered_rows(left, h1_t, n_dev, order)
        for i, cols, lanes in column_parts(heads_width, total, group):
            if i == 3:
                ordered_rows(branch_left, branch_t, n_dev, order)
            rows = (branch_left if i == 3 else left)[...].astype(bf16)
            product = dot(rows, given[right[i]][:, cols]).astype(bf16)
            made[f"keep{group}"][:, lanes] = product[:half, :]
            made[f"give{group}"][:half, lanes] = product[half:, :]


def first_back_kernel(vec, given, made):
    width = given["x"].shape[1]
    normed, scale = norm_parts(given["x"][...].astype(f32))
    dh1 = add_halves(given, "dh1")
    made["vec_grad"][:, :width] = row_sum(dh1 * normed)
    made["vec_grad"][:, width:] = row_sum(dh1)
    gain = given["vec"][:, vec.at["gain1"]]
    made.put("dx", given["dmid"][...] + norm_back(normed, scale, dh1, gain))


def back_kernel(n_dev, half_rows, vec, given, made):
    cap = given["dx"].shape[0]
    me, core = place()
    lengths, owners = given["lengths"][...].astype(f32), given["owners"][...].astype(f32)
    base, _ = my_span(lengths, owners, me)
    half, index = block_slots(base, n_dev, cap, half_rows)
    source = jnp.floor(index * (1.0 / half_rows))
    index = jnp.where(half == core, index + source * half_rows, -1e6)
    row = given["vec"]
    out = given["middle"][...] + (add_sums(given, 1) + row[:, vec.at["br"]])
    rows = dot_rows(one_hot(index, (cap, cap), 1), out.astype(bf16))
    rows += dot_rows(one_hot(index + half_rows, (cap, cap), 1), given["dx"][...])
    made.put("back", rows)


def home_kernel(n_dev, half_rows, given, made):
    me, core = place()
    tokens = made["mixed"].shape[0]
    lengths, owners = given["lengths"][...].astype(f32), given["owners"][...].astype(f32)
    half, index = token_slots(lengths, owners, me, n_dev, tokens, half_rows)
    index = index + jnp.floor(index * (1.0 / half_rows)) * half_rows
    index = jnp.where(half == core, index, index + 2 * n_dev * half_rows)
    rows = jnp.concatenate([given["mine"][...], given["other"][...]], axis=0)
    shape = (rows.shape[0], tokens)
    made.put("mixed", dot_rows(one_hot(index, shape, 0), rows))
    made.put("grad", dot_rows(one_hot(index + half_rows, shape, 0), rows))


def share_of(far_bits):
    me = lax.axis_index("dp")
    return 2 * ((me >> far_bits[0]) & 1) + ((me >> far_bits[1]) & 1)


def mlp_weights_kernel(
    far_bits, orders, n_dev, vec, given, made, h2_all, g_all, hidden_all, dexp_all, we_part,
    wr_part, natural, ordered,
):
    cap, width = given["h2"].shape
    half_cap = cap // 2
    me = lax.axis_index("dp")
    share = share_of(far_bits)
    part, hidden_width = we_part.shape[0], given["we"].shape[0]
    be = vec.at["be"].start
    row = given["vec"]
    bias = jnp.zeros((1, part), f32)
    for i in range(4):
        end = min((i + 1) * part, hidden_width)
        piece = row[:, be + i * part : be + end]
        if end < (i + 1) * part:
            piece = jnp.concatenate([piece, jnp.zeros((1, (i + 1) * part - end), f32)], axis=1)
        bias += jnp.where(share == i, piece, 0.0)
    for name, near in (("we", we_part), ("wr", wr_part)):
        source = given[name]

        @pl.when(share < 3)
        def _():
            near[...] = source[pl.ds(pl.multiple_of(share * part, 16), part), :]

        @pl.when(share == 3)
        def _():
            near[: hidden_width - 3 * part, :] = source[3 * part :, :]
            near[hidden_width - 3 * part :, :] = jnp.zeros((4 * part - hidden_width, width), bf16)

    for k in range(4):
        rows = slice(k * cap, (k + 1) * cap)
        if k == 0:
            h2_all[rows, :] = given["h2"][...]
            g_all[rows, :] = given["g"][...]
        else:
            name = f"far_{k}"
            for i, ref in enumerate((given[name], given[name + "_other"])):
                at = slice(k * cap + i * half_cap, k * cap + (i + 1) * half_cap)
                h2_all[at, :] = ref[:half_cap, :]
                g_all[at, :] = ref[half_cap:, :]
        hidden, slope = gelu_both(dot_cols(h2_all[rows, :], we_part[...]) + bias)
        hidden_all[rows, :] = hidden.astype(bf16)
        dexp_all[rows, :] = (dot_cols(g_all[rows, :], wr_part[...]) * slope).astype(bf16)
    half = width // 2
    for name, left, right, order in (
        ("wr", g_all, hidden_all, orders[0]), ("we", h2_all, dexp_all, orders[1]),
    ):
        natural[...] = dot_rows(left[...], right[...])
        ordered_rows(ordered, natural, n_dev, order)
        made.put(name + "_give", ordered[half:, :])
        made.put(name + "_keep", ordered[:half, :])


def turn_kernel(vec_rows, given, made):
    rows = given["keep"].shape[0]
    total = given["keep"][...].astype(f32) + given["got"][:rows, :].astype(f32)
    made.put("keep", total[: rows // 2, :])
    made["give"][: rows // 2, :] = total[rows // 2 :, :].astype(bf16)
    if vec_rows:
        vec = given["vec"][...] + got_vectors(given["got"], vec_rows)
        made.put("vec", put_vectors(made["give"], rows // 2, vec_rows, vec))


def last_kernel(heads_width, vec_rows, count, given, made):
    total = 4 * heads_width // count
    sums = given["vec"][...] + got_vectors(given["0_got"], vec_rows)
    made.put("vec", sums)
    for group in range(count):
        rows = given[f"{group}_keep"].shape[0]
        value = given[f"{group}_keep"][...].astype(f32)
        value += given[f"{group}_got"][:rows, :].astype(f32)
        for i, cols, lanes in column_parts(heads_width, total, group):
            made[("wq", "wk", "wv", "wo")[i]][:, cols] = value[:, lanes]


def mlp_cut_kernel(part, given, made):
    rows = given["wr_keep"].shape[0] // 4
    for name, first in (("wr", 0), ("we", lane_pad(part))):
        total = given[name + "_keep"][...].astype(f32) + given[name + "_got"][...].astype(f32)
        for k in range(4):
            made[f"cut{k}"][:, first : first + part] = total[k * rows : (k + 1) * rows, :].astype(bf16)


def mlp_last_kernel(far_bits, part, given, made):
    share = share_of(far_bits)
    hidden_width = made["wr"].shape[1]
    pieces = [given[f"cut{k}"][...].astype(f32) for k in range(4)]
    for name, first in (("wr", 0), ("we", lane_pad(part))):
        for i in range(4):
            piece = jnp.zeros((made[name].shape[0], part), f32)
            for k in range(4):
                piece += jnp.where((share ^ k) == i, pieces[k][:, first : first + part], 0.0)
            end = min((i + 1) * part, hidden_width)
            made[name][:, i * part : end] = piece[:, : end - i * part]


def swap_cores(values):
    return lax.ppermute(values, "tensor", [(0, 1), (1, 0)])


def swap_halves(values):
    return [swap_cores(rows) for rows in values]


def swap_dp(values, flip):
    return lax.ppermute(values, "dp", [(i, i ^ flip) for i in range(lax.axis_size("dp"))])


def spread(rows):
    return lax.all_to_all(rows, "dp", split_axis=0, concat_axis=0, tiled=True)


def after(values, earlier):
    return lax.optimization_barrier((values, earlier))[0]


def turn(name, pair, vec=None):
    keep, got = pair
    rows = keep.shape[0] // 2
    vec_rows = 0 if vec is None else vec.shape[0]
    if rows % 8:
        total = keep.astype(f32) + got[: 2 * rows].astype(f32)
        kept, give = total[:rows], total[rows:].astype(bf16)
        if vec is not None:
            got = got[2 * rows :].astype(f32)
            vec = vec + (got[:vec_rows] + got[vec_rows:])
            high = vec.astype(bf16)
            low = (vec - high.astype(f32)).astype(bf16)
            vec = high.astype(f32) + low.astype(f32)
            give = jnp.concatenate([give, high, low])
        return (kept, give), vec
    ins = dict(keep=keep, got=got)
    outs = dict(
        keep=((rows, keep.shape[1]), f32), give=((rows + 2 * vec_rows, keep.shape[1]), bf16)
    )
    if vec is not None:
        ins["vec"], outs["vec"] = vec, (vec.shape, f32)
    made = call(functools.partial(turn_kernel, vec_rows), name, ins, outs)
    return (made["keep"], made["give"]), made.get("vec")


def send(pairs, orders, step):
    return [(keep, swap_dp(give, 1 << order[step])) for (keep, give), order in zip(pairs, orders)]


class Chains:
    def __init__(self, pairs, orders, name, vec=None):
        self.pairs, self.orders, self.name, self.vec = list(pairs), orders, name, vec
        self.count = len(pairs)
        self.done = [1] * self.count

    def step(self, group, earlier=None):
        step = self.done[group]
        if step == len(self.orders[group]):
            return None
        self.done[group] += 1
        pair = self.pairs[group] if earlier is None else after(self.pairs[group], earlier)
        vec = None if group else self.vec
        (keep, give), vec = turn(f"{self.name}_turn_{step}_{group}", pair, vec)
        if not group:
            self.vec = vec
        self.pairs[group] = (keep, swap_dp(give, 1 << self.orders[group][step]))
        return keep

    def finish(self):
        for group in range(self.count):
            while self.step(group) is not None:
                pass


def on_device(
    patches, cotangent, image_lengths, image_owner, first_gain, first_shift, query_weight,
    query_bias, key_weight, value_weight, value_bias, output_weight, output_bias, second_gain,
    second_shift, expand_weight, expand_bias, reduce_weight, reduce_bias,
):
    n_dev = lax.axis_size("dp")
    tokens, width = patches.shape
    cap = 2 * tokens
    half_rows = cap // n_dev // 2
    heads_width, hidden_width = query_weight.shape[1], expand_weight.shape[1]
    heads = heads_width // HD
    n_bits = n_dev.bit_length() - 1
    far_bits = (1, n_bits - 2)
    flips = [flip_of(k, far_bits) for k in range(4)]
    rest = [bit for bit in range(n_bits) if bit not in far_bits]
    mlp_orders = (rest, rest[::-1])
    others = list(range(2, n_bits - 2))
    attend_orders = (
        [0, 1] + others + [n_bits - 2, n_bits - 1],
        [1, 0] + others + [n_bits - 2, n_bits - 1],
    )
    wq, wk, wv, wo, we, wr = (
        w.T for w in (query_weight, key_weight, value_weight, output_weight, expand_weight, reduce_weight)
    )
    vec = Vectors(width, heads_width, hidden_width)
    named = dict(
        gain1=first_gain, shift1=first_shift, bo=output_bias, gain2=second_gain,
        shift2=second_shift, br=reduce_bias, be=expand_bias, bq=query_bias, bv=value_bias,
    )
    vectors = jnp.concatenate(
        [jnp.pad(named[n], (0, lane_pad(named[n].shape[0]) - named[n].shape[0])) for n in vec.at]
    ).reshape(1, -1)
    sizes = dict(lengths=image_lengths.reshape(1, -1), owners=image_owner.reshape(1, -1))
    wide32, wide16 = ((cap, width), f32), ((cap, width), bf16)
    half16 = ((cap // 2, width), bf16)
    head16 = ((cap, heads_width), bf16)
    place_args = (n_dev, half_rows)

    packed = call(
        functools.partial(pack_kernel, *place_args, tokens), "pack",
        dict(**sizes, x=patches, g=cotangent), dict(send=wide16), far=True, vmem=62,
    )
    got = spread(packed["send"])
    got_other = swap_cores(got)
    arrived = dict(**sizes, mine=got, other=got_other)
    fwd = call(
        functools.partial(attend_kernel, *place_args, vec), "attend",
        dict(**arrived, vec=vectors, wq=wq, wk=wk, wv=wv, wo=wo),
        dict(
            mask=((cap, cap), f32), x=wide16, h1=wide16, q=head16, k=head16, v=head16,
            log=((cap, heads), f32), att=head16, branch=wide16,
        ),
    )
    branch_other = swap_cores(fwd["branch"])
    g = call(
        functools.partial(unpack_kernel, *place_args), "unpack", arrived, dict(g=wide16)
    )["g"]
    mlp = call(
        functools.partial(mlp_kernel, *place_args, vec), "mlp",
        dict(
            x=fwd["x"], branch=fwd["branch"], branch_other=branch_other, g=g, vec=vectors, we=we, wr=wr
        ),
        dict(
            middle=wide32, h2=wide16, halves=wide16, sums_0=wide16, sums_1=wide16,
            be_grad=((1, lane_pad(hidden_width)), f32),
        ),
        scratch=[pltpu.VMEM((cap, width), f32)] * 2, vmem=16,
    )
    halves = [swap_dp(mlp["halves"], flip) for flip in flips[1:]]
    sums_other = swap_halves([mlp["sums_0"], mlp["sums_1"]])
    sums = dict(
        sums_0=mlp["sums_0"], sums_1=mlp["sums_1"], sums_0_other=sums_other[0],
        sums_1_other=sums_other[1],
    )
    back = call(
        functools.partial(middle_back_kernel, vec), "middle_back",
        dict(
            g=g, middle=mlp["middle"], vec=vectors, wo=wo, **sums,
        ),
        dict(dmid=wide32, branch_grad=wide16, datt=head16, vec_grad=((1, 4 * width), f32)),
    )
    att_back = call(
        attend_back_kernel, "attend_back",
        dict(
            mask=fwd["mask"], q=fwd["q"], k=fwd["k"], v=fwd["v"], datt=back["datt"], log=fwd["log"],
            wq=wq, wk=wk, wv=wv,
        ),
        dict(
            dq=head16, dk=head16, dv=head16, dh1_0=half16, dh1_1=half16,
            vec_grad=((1, 2 * lane_pad(heads_width)), f32),
        ),
    )
    dh1_other = swap_halves([att_back["dh1_0"], att_back["dh1_1"]])
    first = call(
        functools.partial(first_back_kernel, vec), "first_back",
        dict(
            x=fwd["x"], dh1_0=att_back["dh1_0"], dh1_1=att_back["dh1_1"], dh1_0_other=dh1_other[0],
            dh1_1_other=dh1_other[1], vec=vectors, dmid=back["dmid"],
        ),
        dict(dx=wide16, vec_grad=((1, 2 * width), f32)),
    )

    n_groups = len(attend_orders)
    columns = 4 * heads_width // n_groups
    vec_rows = -(-vec.size // (16 * columns)) * 16
    vec_shape = ((vec_rows, columns), f32)
    group_outs = {}
    for i in range(n_groups):
        more = 0 if i else 2 * vec_rows
        group_outs[f"keep{i}"] = ((width // 2, columns), bf16)
        group_outs[f"give{i}"] = ((width // 2 + more, columns), bf16)
    vec_parts = dict(
        v1=first["vec_grad"], v2=back["vec_grad"], v3=mlp["be_grad"], v4=att_back["vec_grad"]
    )
    pieces = call(
        functools.partial(attend_weights_kernel, n_dev, attend_orders, list(vec_parts)),
        "attend_weights",
        dict(
            h1=fwd["h1"], branch_grad=back["branch_grad"], dq=att_back["dq"], dk=att_back["dk"],
            dv=att_back["dv"], att=fwd["att"], **vec_parts,
        ),
        dict(vec=vec_shape, **group_outs),
        scratch=[pltpu.VMEM((width, cap), f32)] * 4, vmem=16,
    )
    pairs = [(pieces[f"keep{i}"], pieces[f"give{i}"]) for i in range(n_groups)]
    attend = Chains(send(pairs, attend_orders, 0), attend_orders, "attend", pieces["vec"])
    dx = after(first["dx"], pieces["keep0"])
    packed = call(
        functools.partial(back_kernel, *place_args, vec), "back",
        dict(**sizes, vec=vectors, middle=mlp["middle"], dx=dx, **sums), dict(back=wide16),
    )
    home = spread(packed["back"])
    halves = after(halves, packed["back"])
    far = {f"far_{k + 1}": rows for k, rows in enumerate(halves)}
    for k in (1, 2):
        far[f"far_{k}_other"] = swap_cores(far[f"far_{k}"])
    far["far_3"] = after(far["far_3"], far["far_1_other"])
    far["far_3_other"] = swap_cores(far["far_3"])
    part = lane_pad(-(-hidden_width // 4))
    mlp_half = ((width // 2, part), bf16)
    all_rows = pltpu.VMEM((4 * cap, width), bf16)
    all_hidden = pltpu.VMEM((4 * cap, part), bf16)
    grads = call(
        functools.partial(
            mlp_weights_kernel, far_bits, [list(o) + list(far_bits) for o in mlp_orders], n_dev, vec
        ),
        "mlp_weights",
        dict(vec=vectors, we=we, wr=wr, h2=mlp["h2"], g=g, **far),
        dict(wr_give=mlp_half, wr_keep=mlp_half, we_give=mlp_half, we_keep=mlp_half),
        scratch=[all_rows, all_rows, all_hidden, all_hidden]
        + [pltpu.VMEM((part, width), bf16)] * 2 + [pltpu.VMEM((width, part), f32)] * 2,
        vmem=32,
    )
    pairs = [(grads["wr_keep"], grads["wr_give"]), (grads["we_keep"], grads["we_give"])]
    mlp_sums = Chains(send(pairs, mlp_orders, 0), mlp_orders, "mlp")
    last = grads["wr_keep"]
    last = attend.step(0, last)
    last = attend.step(1, last)
    last = mlp_sums.step(0, last)
    last = attend.step(0, last)
    last = attend.step(1, last)
    last = mlp_sums.step(1, last)
    last = attend.step(0, last)
    last = attend.step(1, last)
    for chain in (mlp_sums, attend):
        chain.finish()
    pairs, mlp_pairs, vec_sum = attend.pairs, mlp_sums.pairs, attend.vec
    cut_shape = ((width // n_dev, 2 * lane_pad(part)), bf16)
    cuts = call(
        functools.partial(mlp_cut_kernel, part), "mlp_cut",
        dict(
            wr_keep=mlp_pairs[0][0], wr_got=mlp_pairs[0][1],
            we_keep=mlp_pairs[1][0], we_got=mlp_pairs[1][1],
        ),
        {f"cut{k}": cut_shape for k in range(4)},
    )
    cuts = [cuts["cut0"]] + [swap_dp(cuts[f"cut{k}"], flips[k]) for k in range(1, 4)]
    mixed_grad = call(
        functools.partial(home_kernel, *place_args), "home",
        dict(**sizes, mine=home, other=swap_cores(home)),
        dict(mixed=((tokens, width), bf16), grad=((tokens, width), bf16)),
    )
    own_rows = width // n_dev
    mlp_own = call(
        functools.partial(mlp_last_kernel, far_bits, part), "mlp_last",
        {f"cut{k}": cut for k, cut in enumerate(cuts)},
        dict(wr=((own_rows, hidden_width), f32), we=((own_rows, hidden_width), f32)),
    )
    ins = dict(vec=vec_sum)
    for i, (keep, received) in enumerate(pairs):
        ins[f"{i}_keep"], ins[f"{i}_got"] = keep, received
    outs = dict(vec=vec_shape)
    outs.update({name: ((own_rows, heads_width), f32) for name in ("wq", "wk", "wv", "wo")})
    own = call(
        functools.partial(last_kernel, heads_width, vec_rows, n_groups), "last", ins, outs
    )
    grads = own["vec"].reshape(-1)
    total = {name: grads[at] for name, at in vec.at.items()}
    return (
        mixed_grad["mixed"], mixed_grad["grad"], total["gain1"], total["shift1"], own["wq"],
        total["bq"], own["wk"], own["wv"], total["bv"], own["wo"], total["bo"], total["gain2"],
        total["shift2"], mlp_own["we"], total["be"], mlp_own["wr"], total["br"],
    )


def solution(mesh):
    rows, all_same = P("dp", None), P()
    cols, vector = P(None, "tensor"), P("tensor")
    both = P("dp", "tensor")
    in_specs = (
        rows, rows, all_same, all_same, all_same, all_same, cols, vector, cols, cols, vector, cols,
        all_same, all_same, all_same, cols, vector, cols, all_same,
    )
    out_specs = (
        rows, rows, all_same, all_same, both, vector, both, both, vector, both, all_same, all_same,
        all_same, both, vector, both, all_same,
    )
    return jax.shard_map(
        on_device, mesh=mesh, in_specs=in_specs, out_specs=out_specs, check_vma=False
    )
```

```python
import functools
import types

import jax
import jax.numpy as jnp
from jax import lax
from jax.experimental import pallas as pl
from jax.experimental.pallas import tpu as pltpu
from jax.sharding import PartitionSpec as P

HD = 72
DP, CORE = "dp", "tensor"
masked_score = -1000000000.0
norm_eps = 1e-06
gelu_scale = 0.7978845608028654
gelu_cubic = 0.044715
f32 = jnp.float32
bf16 = jnp.bfloat16
MIB = 1024 * 1024
NOWHERE = -1e6


def dot(left, right):
    return lax.dot_general(left, right, (((1,), (0,)), ((), ())), preferred_element_type=f32)


def dot_cols(left, right):
    return lax.dot_general(left, right, (((1,), (1,)), ((), ())), preferred_element_type=f32)


def dot_rows(left, right):
    return lax.dot_general(left, right, (((0,), (0,)), ((), ())), preferred_element_type=f32)


def iota(shape, dim):
    return lax.broadcasted_iota(jnp.int32, shape, dim).astype(f32)


def row_sum(values):
    return jnp.sum(values, axis=0, keepdims=True)


def lane_sum(values):
    return jnp.sum(values, axis=1, keepdims=True)


def lane_mean(values):
    return jnp.mean(values, axis=1, keepdims=True)


def lane_pad(size):
    return -(-size // 128) * 128


def put(ref, value):
    ref[...] = value.astype(ref.dtype)


def my_span(lengths, owners, me):
    base = lane_sum(jnp.where(owners < me, lengths, 0.0))
    used = lane_sum(jnp.where(owners == me, lengths, 0.0))
    return base, used


def token_slots(lengths, owners, me, n_dev, tokens, half_rows):
    device = iota((n_dev, lengths.shape[1]), 0)
    base = lane_sum(jnp.where(owners < device, lengths, 0.0))
    pos = iota((1, tokens), 1) * n_dev + me
    below = base <= pos
    target = row_sum(jnp.where(below, 1.0, 0.0)) - 1.0
    start = jnp.max(jnp.where(below, base, -1.0), axis=0, keepdims=True)
    slot = jnp.floor((pos - start) * (1.0 / n_dev))
    half = jnp.floor(slot * (1.0 / half_rows))
    return half, target * half_rows + slot - half * half_rows


def block_slots(base, n_dev, cap, half_rows):
    p = iota((cap, 1), 0)
    pos = base + p
    source = pos - n_dev * jnp.floor(pos * (1.0 / n_dev))
    slot = jnp.floor(p * (1.0 / n_dev))
    half = jnp.floor(slot * (1.0 / half_rows))
    return half, source * half_rows + slot - half * half_rows


def one_hot(index, shape, dim):
    return jnp.where(index == iota(shape, dim), 1.0, 0.0).astype(bf16)


def place():
    return lax.axis_index(DP).astype(f32), lax.axis_index(CORE).astype(f32)


def norm_parts(values):
    centered = values - lane_mean(values)
    scale = lax.rsqrt(lane_mean(centered * centered) + norm_eps)
    return centered * scale, scale


def norm_back(normed, scale, grad, gain):
    inner = grad * gain
    return scale * (inner - lane_mean(inner) - normed * lane_mean(inner * normed))


def gelu_both(values):
    square = values * values
    bent = jnp.tanh(gelu_scale * values * (1.0 + gelu_cubic * square))
    half = 0.5 * (1.0 + bent)
    slope = half + 0.5 * values * (1.0 - bent * bent) * (
        gelu_scale * (1.0 + 3.0 * gelu_cubic * square)
    )
    return values * half, slope


def flip_of(block, order):
    flip = 0 * block
    for step, bit in enumerate(order):
        flip = flip | (((block >> (len(order) - 1 - step)) & 1) << bit)
    return flip


def ordered_rows(out_ref, from_ref, n_dev, order):
    width = from_ref.shape[0]
    owner_rows = width // n_dev
    me = lax.axis_index(DP)
    if owner_rows % 8:
        i = iota((width, 1), 0)
        block = jnp.floor((i + 0.5) * (1.0 / owner_rows))
        owner = (flip_of(block.astype(jnp.int32), order) ^ me).astype(f32)
        pick = one_hot(owner * owner_rows + (i - block * owner_rows), (width, width), 1)
        out_ref[...] = dot(pick, from_ref[...].astype(bf16))
        return
    for block in range(n_dev):
        start = pl.multiple_of((me ^ flip_of(block, order)) * owner_rows, 8)
        rows = slice(block * owner_rows, (block + 1) * owner_rows)
        out_ref[rows, :] = from_ref[pl.ds(start, owner_rows), :]


def parts_between(bounds, group, size, count):
    for i in range(count):
        first, last = max(i * size, bounds[group]), min((i + 1) * size, bounds[group + 1])
        if first < last:
            yield (
                i,
                slice(first - i * size, last - i * size),
                slice(first - bounds[group], last - bounds[group]),
            )


def pieces_of(start, size, columns):
    done = 0
    while done < size:
        row, lane = (start + done) // columns, (start + done) % columns
        now = min(columns - lane, size - done)
        yield slice(done, done + now), slice(row, row + 1), slice(lane, lane + now)
        done += now


def call(body, ins, outs, scratch=(), vmem=16, far=False):
    ins_flat, ins_tree = jax.tree.flatten(ins)
    is_out = lambda x: isinstance(x, tuple)
    outs_flat, outs_tree = jax.tree.flatten(outs, is_leaf=is_out)
    n_in, n_out = len(ins_flat), len(outs_flat)

    def kernel(*refs):
        given, rest = refs[:n_in], refs[n_in + n_out :]
        if far:
            near, sems, rest = rest[:n_in], rest[n_in], rest[n_in + 1 :]
            copies = [
                pltpu.make_async_copy(ref, to, sems.at[i]) for i, (ref, to) in enumerate(zip(given, near))
            ]
            for copy in copies:
                copy.start()

            def arrival(copy, to):
                def wait():
                    copy.wait()
                    return to[...]

                return wait

            given = [arrival(copy, to) for copy, to in zip(copies, near)]
        given = types.SimpleNamespace(**jax.tree.unflatten(ins_tree, given))
        made = types.SimpleNamespace(**jax.tree.unflatten(outs_tree, refs[n_in : n_in + n_out]))
        body(given, made, *rest)

    copies = [pltpu.VMEM(x.shape, x.dtype) for x in ins_flat]
    copies += [pltpu.SemaphoreType.DMA((n_in,))]
    results = pl.pallas_call(
        kernel,
        name=getattr(body, "func", body).__name__,
        out_shape=[jax.ShapeDtypeStruct(shape, dtype) for shape, dtype in outs_flat],
        in_specs=[pl.BlockSpec(memory_space=pltpu.HBM if far else pltpu.VMEM)] * n_in,
        out_specs=[pl.BlockSpec(memory_space=pltpu.VMEM)] * n_out,
        scratch_shapes=(copies if far else []) + list(scratch),
        compiler_params=pltpu.CompilerParams(vmem_limit_bytes=vmem * MIB),
    )(*ins_flat)
    return types.SimpleNamespace(**jax.tree.unflatten(outs_tree, results))


def pack(n_dev, half_rows, tokens, given, made):
    me, core = place()
    lengths, owners = given.lengths().astype(f32), given.owners().astype(f32)
    half, index = token_slots(lengths, owners, me, n_dev, tokens, half_rows)
    target = jnp.floor(index * (1.0 / half_rows))
    index = jnp.where(half == core, index + target * half_rows, NOWHERE)
    shape = (2 * n_dev * half_rows, tokens)
    x_pick, g_pick = one_hot(index, shape, 0), one_hot(index + half_rows, shape, 0)
    rows = dot(x_pick, given.x())
    put(made.send, rows + dot(g_pick, given.g()))


def block_rows(given, n_dev, cap, half_rows, kind):
    me, core = place()
    base, _ = my_span(given.lengths[...].astype(f32), given.owners[...].astype(f32), me)
    half, index = block_slots(base, n_dev, cap, half_rows)
    source = jnp.floor(index * (1.0 / half_rows))
    index = index + (source + kind) * half_rows
    index = jnp.where(half == core, index, index + 2 * n_dev * half_rows)
    pick = one_hot(index, (cap, 2 * cap), 1)
    return dot(pick, jnp.concatenate([given.mine[...], given.other[...]], axis=0))


def unpack(n_dev, half_rows, given, made):
    put(made.g, block_rows(given, n_dev, made.g.shape[0], half_rows, 1))


def image_mask(lengths, owners, cap):
    me, _ = place()
    base, used = my_span(lengths, owners, me)
    n_img = lengths.shape[1]
    starts = lane_sum(jnp.where(iota((n_img, n_img), 1) < iota((n_img, n_img), 0), lengths, 0.0))
    p = iota((1, cap), 1)
    count = row_sum(jnp.where(starts <= base + p, 1.0, 0.0))
    seg_row = jnp.where(p < used, count, 0.0)
    on_diagonal = iota((cap, cap), 0) == iota((cap, cap), 1)
    seg_col = lane_sum(jnp.where(on_diagonal, seg_row, 0.0))
    return jnp.where(seg_col == seg_row, 1.0, 0.0)


class Vectors:
    def __init__(self, **sizes):
        self.names, self.size = list(sizes), 0
        for name, size in sizes.items():
            setattr(self, name, slice(self.size, self.size + size))
            self.size += lane_pad(size)


def attend(n_dev, half_rows, vec, given, made):
    cap = made.x.shape[0]
    same = image_mask(given.lengths[...].astype(f32), given.owners[...].astype(f32), cap)
    put(made.mask, same)
    x = block_rows(given, n_dev, cap, half_rows, 0)
    put(made.x, x)
    row = given.vec
    normed, _ = norm_parts(x)
    h1 = (normed * row[:, vec.gain1] + row[:, vec.shift1]).astype(bf16)
    put(made.h1, h1)
    put(made.q, dot_cols(h1, given.wq[...]) + row[:, vec.bq])
    put(made.k, dot_cols(h1, given.wk[...]))
    put(made.v, dot_cols(h1, given.wv[...]) + row[:, vec.bv])
    for h in range(made.q.shape[1] // HD):
        cols = slice(h * HD, (h + 1) * HD)
        s = dot_cols(made.q[:, cols], made.k[:, cols]) * HD ** (-0.5)
        s = jnp.where(same > 0.5, s, masked_score)
        top = jnp.max(s, axis=1, keepdims=True)
        e = jnp.exp(s - top)
        total = lane_sum(e)
        made.log[:, h : h + 1] = top + jnp.log(total)
        made.att[:, cols] = dot((e / total).astype(bf16), made.v[:, cols]).astype(bf16)
    put(made.branch, dot(made.att[...], given.wo[...]))


def both(mine, other, rows=slice(None)):
    return mine[rows, :].astype(f32) + other[rows, :].astype(f32)


def both_halves(mine, other, rows=slice(None)):
    return jnp.concatenate([both(a, b, rows) for a, b in zip(mine, other)], axis=0)


def chunks_of(width, step):
    full = width // step
    return full, full * step, width - full * step


def mlp(vec, given, made, out_total, dh2_total):
    cap = made.middle.shape[0]
    half = cap // 2
    row = given.vec
    branch = both(given.branch, given.branch_other) + row[:, vec.bo]
    middle = given.x[...].astype(f32) + branch
    put(made.middle, middle)
    normed, _ = norm_parts(middle)
    put(made.h2, normed * row[:, vec.gain2] + row[:, vec.shift2])
    start = pl.multiple_of(lax.axis_index(CORE) * half, half)
    made.halves[:half, :] = made.h2[pl.ds(start, half), :]
    made.halves[half:, :] = given.g[pl.ds(start, half), :]
    step = 512
    full, done, rest = chunks_of(given.we.shape[0], step)
    out_total[...] = jnp.zeros_like(out_total)
    dh2_total[...] = jnp.zeros_like(dh2_total)
    made.be_grad[...] = jnp.zeros_like(made.be_grad)
    first = vec.be.start

    def chunk(rows, bias):
        we, wr = given.we[rows, :], given.wr[rows, :]
        hidden, slope = gelu_both(dot_cols(made.h2[...], we) + row[:, bias])
        dexp = (dot_cols(given.g[...], wr) * slope).astype(bf16)
        made.be_grad[:, rows] = row_sum(dexp.astype(f32))
        out_total[...] += dot(hidden.astype(bf16), wr)
        dh2_total[...] += dot(dexp, we)

    @pl.loop(0, full)
    def _(i):
        at = pl.multiple_of(i * step, step)
        chunk(pl.ds(at, step), pl.ds(pl.multiple_of(first + at, 128), step))

    if rest:
        chunk(slice(done, done + rest), slice(first + done, first + done + rest))
    for i, ref in enumerate(made.sums):
        rows = slice(i * half, (i + 1) * half)
        ref[:half, :] = dh2_total[rows, :].astype(bf16)
        ref[half:, :] = out_total[rows, :].astype(bf16)


def middle_back(vec, given, made):
    width = given.middle.shape[1]
    half = given.sums[0].shape[0] // 2
    g = given.g[...].astype(f32)
    normed, scale = norm_parts(given.middle[...])
    dh2 = both_halves(given.sums, given.sums_other, slice(0, half))
    dmid = g + norm_back(normed, scale, dh2, given.vec[:, vec.gain2])
    put(made.dmid, dmid)
    branch = dmid.astype(bf16)
    put(made.branch_grad, branch)
    put(made.datt, dot_cols(branch, given.wo[...]))
    for i, values in enumerate([branch.astype(f32), dh2 * normed, dh2, g]):
        made.vec_grad[:, i * width : (i + 1) * width] = row_sum(values)


def attend_back(given, made):
    heads_width = made.dq.shape[1]
    same = given.mask[...] > 0.5
    for h in range(heads_width // HD):
        cols = slice(h * HD, (h + 1) * HD)
        q, k, v = given.q[:, cols], given.k[:, cols], given.v[:, cols]
        datt = given.datt[:, cols]
        s = jnp.where(same, dot_cols(q, k) * HD ** (-0.5), masked_score)
        prob = jnp.exp(s - given.log[:, h : h + 1])
        dprob = dot_cols(datt, v)
        ds = (prob * (dprob - lane_sum(prob * dprob))).astype(bf16)
        made.dq[:, cols] = (dot(ds, k) * HD ** (-0.5)).astype(bf16)
        made.dk[:, cols] = (dot_rows(ds, q) * HD ** (-0.5)).astype(bf16)
        made.dv[:, cols] = dot_rows(prob.astype(bf16), datt).astype(bf16)
    dh1 = dot(made.dq[...], given.wq[...])
    dh1 += dot(made.dk[...], given.wk[...])
    dh1 += dot(made.dv[...], given.wv[...])
    half = dh1.shape[0] // 2
    for i, ref in enumerate(made.dh1):
        put(ref, dh1[i * half : (i + 1) * half, :])
    row = made.vec_grad
    row[...] = jnp.zeros_like(row)
    row[:, :heads_width] = row_sum(made.dq[...].astype(f32))
    second = lane_pad(heads_width)
    row[:, second : second + heads_width] = row_sum(made.dv[...].astype(f32))


def put_vectors(give_ref, first, rows, values):
    high = values.astype(bf16)
    low = (values - high.astype(f32)).astype(bf16)
    give_ref[first : first + rows, :] = high
    give_ref[first + rows : first + 2 * rows, :] = low
    return high.astype(f32) + low.astype(f32)


def got_vectors(got_ref, rows):
    first = got_ref.shape[0] - 2 * rows
    high = got_ref[first : first + rows, :].astype(f32)
    return high + got_ref[first + rows :, :].astype(f32)


def attend_weights(n_dev, orders, bounds, given, made, h1_t, branch_t, left, branch_left):
    heads_width = given.right[0].shape[1]
    half = given.h1.shape[1] // 2
    h1_t[...] = jnp.transpose(given.h1[...].astype(f32))
    branch_t[...] = jnp.transpose(given.branch_grad[...].astype(f32))
    made.vec[...] = jnp.zeros_like(made.vec)
    at = 0
    for ref in given.vec_grads:
        for here, row, lanes in pieces_of(at, ref.shape[1], made.vec.shape[1]):
            made.vec[row, lanes] = ref[:, here]
        at += ref.shape[1]
    put(made.vec, put_vectors(made.give[0], half, made.vec.shape[0], made.vec[...]))
    for group, order in enumerate(orders):
        width = bounds[group + 1] - bounds[group]
        ordered_rows(left, h1_t, n_dev, order)
        for i, cols, lanes in parts_between(bounds, group, heads_width, 4):
            if i == 3:
                ordered_rows(branch_left, branch_t, n_dev, order)
            rows = (branch_left if i == 3 else left)[...].astype(bf16)
            product = dot(rows, given.right[i][:, cols]).astype(bf16)
            made.keep[group][:, lanes] = product[:half, :]
            made.give[group][:half, lanes] = product[half:, :]


def first_back(vec, given, made):
    width = given.x.shape[1]
    normed, scale = norm_parts(given.x[...].astype(f32))
    dh1 = both_halves(given.dh1, given.dh1_other)
    made.vec_grad[:, :width] = row_sum(dh1 * normed)
    made.vec_grad[:, width:] = row_sum(dh1)
    gain = given.vec[:, vec.gain1]
    put(made.dx, given.dmid[...] + norm_back(normed, scale, dh1, gain))


def back(n_dev, half_rows, vec, given, made):
    cap = given.dx.shape[0]
    half = given.sums[0].shape[0] // 2
    me, core = place()
    base, _ = my_span(given.lengths[...].astype(f32), given.owners[...].astype(f32), me)
    which, index = block_slots(base, n_dev, cap, half_rows)
    source = jnp.floor(index * (1.0 / half_rows))
    index = jnp.where(which == core, index + source * half_rows, NOWHERE)
    part = both_halves(given.sums, given.sums_other, slice(half, 2 * half))
    out = given.middle[...] + (part + given.vec[:, vec.br])
    rows = dot_rows(one_hot(index, (cap, cap), 1), out.astype(bf16))
    rows += dot_rows(one_hot(index + half_rows, (cap, cap), 1), given.dx[...])
    put(made.back, rows)


def home(n_dev, half_rows, given, made):
    me, core = place()
    tokens = made.mixed.shape[0]
    lengths, owners = given.lengths[...].astype(f32), given.owners[...].astype(f32)
    half, index = token_slots(lengths, owners, me, n_dev, tokens, half_rows)
    index = index + jnp.floor(index * (1.0 / half_rows)) * half_rows
    index = jnp.where(half == core, index, index + 2 * n_dev * half_rows)
    rows = jnp.concatenate([given.mine[...], given.other[...]], axis=0)
    shape = (rows.shape[0], tokens)
    put(made.mixed, dot_rows(one_hot(index, shape, 0), rows))
    put(made.grad, dot_rows(one_hot(index + half_rows, shape, 0), rows))


def share_of(far_bits):
    me = lax.axis_index(DP)
    return 2 * ((me >> far_bits[0]) & 1) + ((me >> far_bits[1]) & 1)


def mlp_weights(
    far_bits, orders, bounds, n_dev, vec, given, made, h2_all, g_all, hidden_all, dexp_all, we_part,
    wr_part, natural, ordered,
):
    cap, width = given.h2.shape
    half_cap = cap // 2
    share = share_of(far_bits)
    part, hidden_width = we_part.shape[0], given.we.shape[0]
    last = hidden_width - 3 * part
    be = vec.be.start
    bias = jnp.zeros((1, part), f32)
    for i in range(4):
        end = min((i + 1) * part, hidden_width)
        piece = given.vec[:, be + i * part : be + end]
        if end < (i + 1) * part:
            piece = jnp.concatenate([piece, jnp.zeros((1, (i + 1) * part - end), f32)], axis=1)
        bias += jnp.where(share == i, piece, 0.0)
    for source, near in ((given.we, we_part), (given.wr, wr_part)):

        @pl.when(share < 3)
        def _():
            near[...] = source[pl.ds(pl.multiple_of(share * part, 16), part), :]

        @pl.when(share == 3)
        def _():
            near[:last, :] = source[3 * part :, :]
            near[last:, :] = jnp.zeros((part - last, width), bf16)

    for k in range(4):
        rows = slice(k * cap, (k + 1) * cap)
        if k == 0:
            h2_all[rows, :] = given.h2[...]
            g_all[rows, :] = given.g[...]
        else:
            for i, ref in enumerate((given.far[k - 1], given.far_other[k - 1])):
                at = slice(k * cap + i * half_cap, k * cap + (i + 1) * half_cap)
                h2_all[at, :] = ref[:half_cap, :]
                g_all[at, :] = ref[half_cap:, :]
        hidden, slope = gelu_both(dot_cols(h2_all[rows, :], we_part[...]) + bias)
        hidden_all[rows, :] = hidden.astype(bf16)
        dexp_all[rows, :] = (dot_cols(g_all[rows, :], wr_part[...]) * slope).astype(bf16)
    half = width // 2
    natural[:, :part] = dot_rows(g_all[...], hidden_all[...])
    natural[:, part : 2 * part] = dot_rows(h2_all[...], dexp_all[...])
    if 2 * part < bounds[-1]:
        natural[:, 2 * part :] = jnp.zeros((width, bounds[-1] - 2 * part), f32)
    for group, order in enumerate(orders):
        lanes = pl.ds(bounds[group], bounds[group + 1] - bounds[group])
        here = ordered.at[:, pl.ds(0, bounds[group + 1] - bounds[group])]
        ordered_rows(here, natural.at[:, lanes], n_dev, order)
        put(made.give[group], here[half:, :])
        put(made.keep[group], here[:half, :])


def turn(vec_rows, given, made):
    rows = given.keep.shape[0]
    total = given.keep[...].astype(f32) + given.got[:rows, :].astype(f32)
    put(made.keep, total[: rows // 2, :])
    made.give[: rows // 2, :] = total[rows // 2 :, :].astype(bf16)
    if vec_rows:
        vec = given.vec[...] + got_vectors(given.got, vec_rows)
        put(made.vec, put_vectors(made.give, rows // 2, vec_rows, vec))


def last_sums(bounds, vec_rows, given, made):
    put(made.vec, given.vec[...] + got_vectors(given.got[0], vec_rows))
    for group, (keep, got) in enumerate(zip(given.keep, given.got)):
        value = keep[...].astype(f32) + got[: keep.shape[0], :].astype(f32)
        for i, cols, lanes in parts_between(bounds, group, made.weights[0].shape[1], 4):
            made.weights[i][:, cols] = value[:, lanes]


def mlp_cut(bounds, given, made):
    rows = given.keep[0].shape[0] // 4
    for group, (keep, got) in enumerate(zip(given.keep, given.got)):
        total = keep[...].astype(f32) + got[...].astype(f32)
        for k, ref in enumerate(made.cuts):
            ref[:, bounds[group] : bounds[group + 1]] = total[k * rows : (k + 1) * rows, :].astype(bf16)


def mlp_last(far_bits, part, given, made):
    share = share_of(far_bits)
    hidden_width = made.weights[0].shape[1]
    pieces = [ref[...].astype(f32) for ref in given.cuts]
    for i in range(4):
        own = jnp.zeros_like(pieces[0])
        for k, piece in enumerate(pieces):
            own += jnp.where((share ^ k) == i, piece, 0.0)
        end = min((i + 1) * part, hidden_width)
        for at, ref in enumerate(made.weights):
            ref[:, i * part : end] = own[:, at * part : at * part + end - i * part]


def swap_cores(values):
    return lax.ppermute(values, CORE, [(0, 1), (1, 0)])


def swap_dp(values, flip):
    return lax.ppermute(values, DP, [(i, i ^ flip) for i in range(lax.axis_size(DP))])


def spread(rows):
    return lax.all_to_all(rows, DP, split_axis=0, concat_axis=0, tiled=True)


def after(values, earlier):
    return lax.optimization_barrier((values, earlier))[0]


def next_step(pair, vec):
    keep, got = pair
    rows = keep.shape[0] // 2
    vec_rows = 0 if vec is None else vec.shape[0]
    if rows % 8:
        total = keep.astype(f32) + got[: 2 * rows].astype(f32)
        kept, give = total[:rows], total[rows:].astype(bf16)
        if vec is not None:
            got = got[2 * rows :].astype(f32)
            vec = vec + (got[:vec_rows] + got[vec_rows:])
            high = vec.astype(bf16)
            low = (vec - high.astype(f32)).astype(bf16)
            vec = high.astype(f32) + low.astype(f32)
            give = jnp.concatenate([give, high, low])
        return kept, give, vec
    columns = keep.shape[1]
    ins, outs = dict(keep=keep, got=got), dict(keep=((rows, columns), f32))
    outs.update(give=((rows + 2 * vec_rows, columns), bf16))
    if vec is not None:
        ins.update(vec=vec)
        outs.update(vec=(vec.shape, f32))
    made = call(functools.partial(turn, vec_rows), ins, outs)
    return made.keep, made.give, None if vec is None else made.vec


class Chains:
    def __init__(self, keep, give, orders, vec=None):
        self.orders, self.vec = orders, vec
        self.done = [1] * len(orders)
        self.pairs = [(k, swap_dp(g, 1 << order[0])) for k, g, order in zip(keep, give, orders)]

    def step(self, group, earlier):
        step = self.done[group]
        self.done[group] += 1
        pair = after(self.pairs[group], earlier)
        keep, give, vec = next_step(pair, None if group else self.vec)
        if not group:
            self.vec = vec
        self.pairs[group] = (keep, swap_dp(give, 1 << self.orders[group][step]))
        return keep

    def finish(self, earlier):
        for group, order in enumerate(self.orders):
            while self.done[group] < len(order):
                earlier = self.step(group, earlier)

    def kept(self):
        return [pair[0] for pair in self.pairs]

    def received(self):
        return [pair[1] for pair in self.pairs]


def on_device(
    patches, cotangent, image_lengths, image_owner, first_gain, first_shift, query_weight,
    query_bias, key_weight, value_weight, value_bias, output_weight, output_bias, second_gain,
    second_shift, expand_weight, expand_bias, reduce_weight, reduce_bias,
):
    n_dev = lax.axis_size(DP)
    tokens, width = patches.shape
    cap = 2 * tokens
    half_rows = cap // n_dev // 2
    heads_width, hidden_width = query_weight.shape[1], expand_weight.shape[1]
    heads = heads_width // HD
    n_bits = n_dev.bit_length() - 1
    far_bits = (1, n_bits - 2)
    flips = [flip_of(k, far_bits) for k in range(4)]
    rest = [bit for bit in range(n_bits) if bit not in far_bits]
    mlp_orders = (rest, rest[::-1])
    others = list(range(2, n_bits - 2))
    attend_orders = (
        [0, 1] + others + [n_bits - 2, n_bits - 1],
        [1, 0] + others + [n_bits - 2, n_bits - 1],
    )
    attend_bounds = (0, 1152, 4 * heads_width)
    wq, wk, wv, wo, we, wr = (
        w.T for w in (query_weight, key_weight, value_weight, output_weight, expand_weight, reduce_weight)
    )
    vec = Vectors(
        gain1=width, shift1=width, bo=width, gain2=width, shift2=width, br=width, be=hidden_width,
        bq=heads_width, bv=heads_width,
    )
    vectors = [
        first_gain, first_shift, output_bias, second_gain, second_shift, reduce_bias, expand_bias,
        query_bias, value_bias,
    ]
    vectors = jnp.concatenate(
        [jnp.pad(v, (0, lane_pad(v.shape[0]) - v.shape[0])) for v in vectors]
    ).reshape(1, -1)
    sizes = dict(lengths=image_lengths.reshape(1, -1), owners=image_owner.reshape(1, -1))
    wide32, wide16 = ((cap, width), f32), ((cap, width), bf16)
    half16 = ((cap // 2, width), bf16)
    head16 = ((cap, heads_width), bf16)
    at_place = lambda body, *more: functools.partial(body, n_dev, half_rows, *more)
    scratch = pltpu.VMEM

    sent = call(
        at_place(pack, tokens), dict(**sizes, x=patches, g=cotangent), dict(send=wide16), far=True, vmem=62
    )
    got = spread(sent.send)
    arrived = dict(**sizes, mine=got, other=swap_cores(got))
    fwd = call(
        at_place(attend, vec),
        dict(**arrived, vec=vectors, wq=wq, wk=wk, wv=wv, wo=wo),
        dict(
            mask=((cap, cap), f32), x=wide16, h1=wide16, q=head16, k=head16, v=head16,
            log=((cap, heads), f32), att=head16, branch=wide16,
        ),
    )
    branch_other = swap_cores(fwd.branch)
    g = call(at_place(unpack), arrived, dict(g=wide16)).g
    mid = call(
        functools.partial(mlp, vec),
        dict(x=fwd.x, branch=fwd.branch, branch_other=branch_other, g=g, vec=vectors, we=we, wr=wr),
        dict(
            middle=wide32, h2=wide16, halves=wide16, sums=[wide16, wide16],
            be_grad=((1, lane_pad(hidden_width)), f32),
        ),
        scratch=[scratch((cap, width), f32)] * 2,
    )
    halves = [swap_dp(mid.halves, flip) for flip in flips[1:]]
    sums = dict(sums=mid.sums, sums_other=[swap_cores(rows) for rows in mid.sums])
    half_back = call(
        functools.partial(middle_back, vec),
        dict(g=g, middle=mid.middle, vec=vectors, wo=wo, **sums),
        dict(dmid=wide32, branch_grad=wide16, datt=head16, vec_grad=((1, 4 * width), f32)),
    )
    att_back = call(
        attend_back,
        dict(
            mask=fwd.mask, q=fwd.q, k=fwd.k, v=fwd.v, datt=half_back.datt, log=fwd.log,
            wq=wq, wk=wk, wv=wv,
        ),
        dict(
            dq=head16, dk=head16, dv=head16, dh1=[half16, half16],
            vec_grad=((1, 2 * lane_pad(heads_width)), f32),
        ),
    )
    first = call(
        functools.partial(first_back, vec),
        dict(
            x=fwd.x, dh1=att_back.dh1, dh1_other=[swap_cores(rows) for rows in att_back.dh1],
            vec=vectors, dmid=half_back.dmid,
        ),
        dict(dx=wide16, vec_grad=((1, 2 * width), f32)),
    )

    columns = attend_bounds[1]
    vec_rows = -(-vec.size // (16 * columns)) * 16
    keeps, gives = [], []
    for i in range(len(attend_orders)):
        span = attend_bounds[i + 1] - attend_bounds[i]
        keeps.append(((width // 2, span), bf16))
        gives.append(((width // 2 + (0 if i else 2 * vec_rows), span), bf16))
    products = call(
        functools.partial(attend_weights, n_dev, attend_orders, attend_bounds),
        dict(
            h1=fwd.h1, branch_grad=half_back.branch_grad,
            right=[att_back.dq, att_back.dk, att_back.dv, fwd.att],
            vec_grads=[first.vec_grad, half_back.vec_grad, mid.be_grad, att_back.vec_grad],
        ),
        dict(vec=((vec_rows, columns), f32), keep=keeps, give=gives),
        scratch=[scratch((width, cap), f32)] * 4,
    )
    a = Chains(products.keep, products.give, attend_orders, products.vec)
    dx = after(first.dx, products.keep[0])
    packed = call(
        at_place(back, vec), dict(**sizes, vec=vectors, middle=mid.middle, dx=dx, **sums), dict(back=wide16)
    ).back
    came = spread(packed)
    far = after(halves, packed)
    far_other = [swap_cores(rows) for rows in far[:2]]
    far[2] = after(far[2], far_other[0])
    far_other.append(swap_cores(far[2]))
    part = -(-hidden_width // 64) * 16
    mlp_bounds = (0, 768, lane_pad(2 * part))
    spans = [after_ - before for before, after_ in zip(mlp_bounds, mlp_bounds[1:])]
    mlp_half = [((width // 2, span), bf16) for span in spans]
    grads = call(
        functools.partial(
            mlp_weights, far_bits, [list(o) + list(far_bits) for o in mlp_orders], mlp_bounds, n_dev, vec
        ),
        dict(vec=vectors, we=we, wr=wr, h2=mid.h2, g=g, far=far, far_other=far_other),
        dict(give=mlp_half, keep=mlp_half),
        scratch=[scratch((4 * cap, width), bf16)] * 2 + [scratch((4 * cap, part), bf16)] * 2
        + [scratch((part, width), bf16)] * 2
        + [scratch((width, mlp_bounds[-1]), f32), scratch((width, max(spans)), f32)],
        vmem=36,
    )
    m = Chains(grads.keep, grads.give, mlp_orders)
    last = grads.keep[0]
    last = a.step(0, last)
    last = a.step(1, last)
    last = m.step(0, last)
    last = a.step(0, last)
    last = a.step(1, last)
    last = m.step(1, last)
    last = a.step(0, last)
    last = a.step(1, last)
    m.finish(last)
    a.finish(last)
    own_rows = width // n_dev
    cut = ((own_rows, mlp_bounds[-1]), bf16)
    cuts = call(
        functools.partial(mlp_cut, mlp_bounds), dict(keep=m.kept(), got=m.received()), dict(cuts=[cut] * 4)
    ).cuts
    cuts = [cuts[0]] + [swap_dp(rows, flip) for rows, flip in zip(cuts[1:], flips[1:])]
    final = call(
        at_place(home), dict(**sizes, mine=came, other=swap_cores(came)),
        dict(mixed=((tokens, width), bf16), grad=((tokens, width), bf16)),
    )
    mlp_own = call(
        functools.partial(mlp_last, far_bits, part), dict(cuts=cuts),
        dict(weights=[((own_rows, hidden_width), f32)] * 2),
    ).weights
    own = call(
        functools.partial(last_sums, attend_bounds, vec_rows),
        dict(vec=a.vec, keep=a.kept(), got=a.received()),
        dict(vec=((vec_rows, columns), f32), weights=[((own_rows, heads_width), f32)] * 4),
    )
    flat = own.vec.reshape(-1)
    total = types.SimpleNamespace(**{name: flat[getattr(vec, name)] for name in vec.names})
    wq_sum, wk_sum, wv_sum, wo_sum = own.weights
    wr_sum, we_sum = mlp_own
    return (
        final.mixed, final.grad, total.gain1, total.shift1, wq_sum, total.bq, wk_sum, wv_sum, total.bv,
        wo_sum, total.bo, total.gain2, total.shift2, we_sum, total.be, wr_sum, total.br,
    )


def solution(mesh):
    rows, all_same = P(DP, None), P()
    cols, vector = P(None, CORE), P(CORE)
    tiles = P(DP, CORE)
    in_specs = (
        rows, rows, all_same, all_same, all_same, all_same, cols, vector, cols, cols, vector, cols,
        all_same, all_same, all_same, cols, vector, cols, all_same,
    )
    out_specs = (
        rows, rows, all_same, all_same, tiles, vector, tiles, tiles, vector, tiles, all_same, all_same,
        all_same, tiles, vector, tiles, all_same,
    )
    return jax.shard_map(
        on_device, mesh=mesh, in_specs=in_specs, out_specs=out_specs, check_vma=False
    )
```

```python
import functools
import types

import jax
import jax.numpy as jnp
from jax import lax
from jax.experimental import pallas as pl
from jax.experimental.pallas import tpu as pltpu
from jax.sharding import PartitionSpec as P

HD = 72
DP, CORE = "dp", "tensor"
masked_score = -1000000000.0
norm_eps = 1e-06
gelu_scale = 0.7978845608028654
gelu_cubic = 0.044715
f32 = jnp.float32
bf16 = jnp.bfloat16
MIB = 1024 * 1024
NOWHERE = -1e6


def dot(left, right):
    return lax.dot_general(left, right, (((1,), (0,)), ((), ())), preferred_element_type=f32)


def dot_cols(left, right):
    return lax.dot_general(left, right, (((1,), (1,)), ((), ())), preferred_element_type=f32)


def dot_rows(left, right):
    return lax.dot_general(left, right, (((0,), (0,)), ((), ())), preferred_element_type=f32)


def iota(shape, dim):
    return lax.broadcasted_iota(jnp.int32, shape, dim).astype(f32)


def row_sum(values):
    return jnp.sum(values, axis=0, keepdims=True)


def lane_sum(values):
    return jnp.sum(values, axis=1, keepdims=True)


def lane_mean(values):
    return jnp.mean(values, axis=1, keepdims=True)


def lane_pad(size):
    return -(-size // 128) * 128


def put(ref, value):
    ref[...] = value.astype(ref.dtype)


def my_span(lengths, owners, me):
    base = lane_sum(jnp.where(owners < me, lengths, 0.0))
    used = lane_sum(jnp.where(owners == me, lengths, 0.0))
    return base, used


def token_slots(lengths, owners, me, n_dev, tokens, half_rows):
    device = iota((n_dev, lengths.shape[1]), 0)
    base = lane_sum(jnp.where(owners < device, lengths, 0.0))
    pos = iota((1, tokens), 1) * n_dev + me
    below = base <= pos
    target = row_sum(jnp.where(below, 1.0, 0.0)) - 1.0
    start = jnp.max(jnp.where(below, base, -1.0), axis=0, keepdims=True)
    slot = jnp.floor((pos - start) * (1.0 / n_dev))
    half = jnp.floor(slot * (1.0 / half_rows))
    return half, target * half_rows + slot - half * half_rows


def block_slots(base, n_dev, cap, half_rows):
    p = iota((cap, 1), 0)
    pos = base + p
    source = pos - n_dev * jnp.floor(pos * (1.0 / n_dev))
    slot = jnp.floor(p * (1.0 / n_dev))
    half = jnp.floor(slot * (1.0 / half_rows))
    return half, source * half_rows + slot - half * half_rows


def one_hot(index, shape, dim):
    return jnp.where(index == iota(shape, dim), 1.0, 0.0).astype(bf16)


def place():
    return lax.axis_index(DP).astype(f32), lax.axis_index(CORE).astype(f32)


def norm_parts(values):
    centered = values - lane_mean(values)
    scale = lax.rsqrt(lane_mean(centered * centered) + norm_eps)
    return centered * scale, scale


def norm_back(normed, scale, grad, gain):
    inner = grad * gain
    return scale * (inner - lane_mean(inner) - normed * lane_mean(inner * normed))


def gelu_both(values):
    square = values * values
    bent = jnp.tanh(gelu_scale * values * (1.0 + gelu_cubic * square))
    half = 0.5 * (1.0 + bent)
    slope = half + 0.5 * values * (1.0 - bent * bent) * (
        gelu_scale * (1.0 + 3.0 * gelu_cubic * square)
    )
    return values * half, slope


def flip_of(block, order):
    flip = 0 * block
    for step, bit in enumerate(order):
        flip = flip | (((block >> (len(order) - 1 - step)) & 1) << bit)
    return flip


def ordered_rows(out_ref, from_ref, n_dev, order):
    width = from_ref.shape[0]
    owner_rows = width // n_dev
    me = lax.axis_index(DP)
    if owner_rows % 8:
        i = iota((width, 1), 0)
        block = jnp.floor((i + 0.5) * (1.0 / owner_rows))
        owner = (flip_of(block.astype(jnp.int32), order) ^ me).astype(f32)
        pick = one_hot(owner * owner_rows + (i - block * owner_rows), (width, width), 1)
        out_ref[...] = dot(pick, from_ref[...].astype(bf16))
        return
    for block in range(n_dev):
        start = pl.multiple_of((me ^ flip_of(block, order)) * owner_rows, 8)
        rows = slice(block * owner_rows, (block + 1) * owner_rows)
        out_ref[rows, :] = from_ref[pl.ds(start, owner_rows), :]


def parts_between(bounds, group, size, count):
    for i in range(count):
        first, last = max(i * size, bounds[group]), min((i + 1) * size, bounds[group + 1])
        if first < last:
            yield (
                i,
                slice(first - i * size, last - i * size),
                slice(first - bounds[group], last - bounds[group]),
            )


def pieces_of(start, size, columns):
    done = 0
    while done < size:
        row, lane = (start + done) // columns, (start + done) % columns
        now = min(columns - lane, size - done)
        yield slice(done, done + now), slice(row, row + 1), slice(lane, lane + now)
        done += now


def call(body, ins, outs, scratch=(), vmem=16, far=False, us=0):
    ins_flat, ins_tree = jax.tree.flatten(ins)
    is_out = lambda x: isinstance(x, tuple)
    outs_flat, outs_tree = jax.tree.flatten(outs, is_leaf=is_out)
    n_in, n_out = len(ins_flat), len(outs_flat)

    def kernel(*refs):
        given, rest = refs[:n_in], refs[n_in + n_out :]
        if far:
            near, sems, rest = rest[:n_in], rest[n_in], rest[n_in + 1 :]
            copies = [
                pltpu.make_async_copy(ref, to, sems.at[i]) for i, (ref, to) in enumerate(zip(given, near))
            ]
            for copy in copies:
                copy.start()

            def arrival(copy, to):
                def wait():
                    copy.wait()
                    return to[...]

                return wait

            given = [arrival(copy, to) for copy, to in zip(copies, near)]
        given = types.SimpleNamespace(**jax.tree.unflatten(ins_tree, given))
        made = types.SimpleNamespace(**jax.tree.unflatten(outs_tree, refs[n_in : n_in + n_out]))
        body(given, made, *rest)

    copies = [pltpu.VMEM(x.shape, x.dtype) for x in ins_flat]
    copies += [pltpu.SemaphoreType.DMA((n_in,))]
    results = pl.pallas_call(
        kernel,
        name=getattr(body, "func", body).__name__,
        out_shape=[jax.ShapeDtypeStruct(shape, dtype) for shape, dtype in outs_flat],
        in_specs=[pl.BlockSpec(memory_space=pltpu.HBM if far else pltpu.VMEM)] * n_in,
        out_specs=[pl.BlockSpec(memory_space=pltpu.VMEM)] * n_out,
        scratch_shapes=(copies if far else []) + list(scratch),
        cost_estimate=pl.CostEstimate(flops=us * 10**9, bytes_accessed=us * 10**6, transcendentals=0),
        compiler_params=pltpu.CompilerParams(vmem_limit_bytes=vmem * MIB),
    )(*ins_flat)
    return types.SimpleNamespace(**jax.tree.unflatten(outs_tree, results))


def pack(n_dev, half_rows, tokens, given, made):
    me, core = place()
    lengths, owners = given.lengths().astype(f32), given.owners().astype(f32)
    half, index = token_slots(lengths, owners, me, n_dev, tokens, half_rows)
    target = jnp.floor(index * (1.0 / half_rows))
    index = jnp.where(half == core, index + target * half_rows, NOWHERE)
    shape = (2 * n_dev * half_rows, tokens)
    x_pick, g_pick = one_hot(index, shape, 0), one_hot(index + half_rows, shape, 0)
    rows = dot(x_pick, given.x())
    put(made.send, rows + dot(g_pick, given.g()))


def block_rows(given, n_dev, cap, half_rows, kind):
    me, core = place()
    base, _ = my_span(given.lengths[...].astype(f32), given.owners[...].astype(f32), me)
    half, index = block_slots(base, n_dev, cap, half_rows)
    source = jnp.floor(index * (1.0 / half_rows))
    index = index + (source + kind) * half_rows
    index = jnp.where(half == core, index, index + 2 * n_dev * half_rows)
    pick = one_hot(index, (cap, 2 * cap), 1)
    return dot(pick, jnp.concatenate([given.mine[...], given.other[...]], axis=0))


def image_mask(lengths, owners, cap):
    me, _ = place()
    base, used = my_span(lengths, owners, me)
    n_img = lengths.shape[1]
    starts = lane_sum(jnp.where(iota((n_img, n_img), 1) < iota((n_img, n_img), 0), lengths, 0.0))
    p = iota((1, cap), 1)
    count = row_sum(jnp.where(starts <= base + p, 1.0, 0.0))
    seg_row = jnp.where(p < used, count, 0.0)
    on_diagonal = iota((cap, cap), 0) == iota((cap, cap), 1)
    seg_col = lane_sum(jnp.where(on_diagonal, seg_row, 0.0))
    return jnp.where(seg_col == seg_row, 1.0, 0.0)


class Vectors:
    def __init__(self, **sizes):
        self.names, self.size = list(sizes), 0
        for name, size in sizes.items():
            setattr(self, name, slice(self.size, self.size + size))
            self.size += lane_pad(size)


def arrive(n_dev, half_rows, vec, given, made):
    cap = made.x.shape[0]
    x = block_rows(given, n_dev, cap, half_rows, 0)
    put(made.x, x)
    normed, _ = norm_parts(x)
    put(made.h1, normed * given.vec[:, vec.gain1] + given.vec[:, vec.shift1])
    put(made.g, block_rows(given, n_dev, cap, half_rows, 1))
    put(made.mask, image_mask(given.lengths[...].astype(f32), given.owners[...].astype(f32), cap))


def attend(vec, given, made):
    same = given.mask[...] > 0.5
    row, h1 = given.vec, given.h1[...]
    put(made.q, dot_cols(h1, given.wq[...]) + row[:, vec.bq])
    put(made.k, dot_cols(h1, given.wk[...]))
    put(made.v, dot_cols(h1, given.wv[...]) + row[:, vec.bv])
    for h in range(made.q.shape[1] // HD):
        cols = slice(h * HD, (h + 1) * HD)
        s = dot_cols(made.q[:, cols], made.k[:, cols]) * HD ** (-0.5)
        s = jnp.where(same, s, masked_score)
        top = jnp.max(s, axis=1, keepdims=True)
        e = jnp.exp(s - top)
        total = lane_sum(e)
        made.log[:, h : h + 1] = top + jnp.log(total)
        made.att[:, cols] = dot((e / total).astype(bf16), made.v[:, cols]).astype(bf16)
    put(made.branch, dot(made.att[...], given.wo[...]))


def both(mine, other, rows=slice(None)):
    return mine[rows, :].astype(f32) + other[rows, :].astype(f32)


def both_halves(mine, other, rows=slice(None)):
    return jnp.concatenate([both(a, b, rows) for a, b in zip(mine, other)], axis=0)


def chunks_of(width, step):
    full = width // step
    return full, full * step, width - full * step


def mlp(vec, given, made, out_total, dh2_total):
    cap = made.middle.shape[0]
    half = cap // 2
    row = given.vec
    branch = both(given.branch, given.branch_other) + row[:, vec.bo]
    middle = given.x[...].astype(f32) + branch
    put(made.middle, middle)
    normed, _ = norm_parts(middle)
    put(made.h2, normed * row[:, vec.gain2] + row[:, vec.shift2])
    start = pl.multiple_of(lax.axis_index(CORE) * half, half)
    made.halves[:half, :] = made.h2[pl.ds(start, half), :]
    made.halves[half:, :] = given.g[pl.ds(start, half), :]
    step = 512
    full, done, rest = chunks_of(given.we.shape[0], step)
    out_total[...] = jnp.zeros_like(out_total)
    dh2_total[...] = jnp.zeros_like(dh2_total)
    made.be_grad[...] = jnp.zeros_like(made.be_grad)
    first = vec.be.start

    def chunk(rows, bias):
        we, wr = given.we[rows, :], given.wr[rows, :]
        hidden, slope = gelu_both(dot_cols(made.h2[...], we) + row[:, bias])
        dexp = (dot_cols(given.g[...], wr) * slope).astype(bf16)
        made.be_grad[:, rows] = row_sum(dexp.astype(f32))
        out_total[...] += dot(hidden.astype(bf16), wr)
        dh2_total[...] += dot(dexp, we)

    @pl.loop(0, full, unroll=True)
    def _(i):
        at = pl.multiple_of(i * step, step)
        chunk(pl.ds(at, step), pl.ds(pl.multiple_of(first + at, 128), step))

    if rest:
        chunk(slice(done, done + rest), slice(first + done, first + done + rest))
    for i, ref in enumerate(made.sums):
        rows = slice(i * half, (i + 1) * half)
        ref[:half, :] = dh2_total[rows, :].astype(bf16)
        ref[half:, :] = out_total[rows, :].astype(bf16)


def middle_back(vec, given, made):
    width = given.middle.shape[1]
    half = given.sums[0].shape[0] // 2
    g = given.g[...].astype(f32)
    normed, scale = norm_parts(given.middle[...])
    dh2 = both_halves(given.sums, given.sums_other, slice(0, half))
    dmid = g + norm_back(normed, scale, dh2, given.vec[:, vec.gain2])
    put(made.dmid, dmid)
    branch = dmid.astype(bf16)
    put(made.branch_grad, branch)
    put(made.datt, dot_cols(branch, given.wo[...]))
    for i, values in enumerate([branch.astype(f32), dh2 * normed, dh2, g]):
        made.vec_grad[:, i * width : (i + 1) * width] = row_sum(values)


def attend_back(given, made):
    heads_width = made.dq.shape[1]
    same = given.mask[...] > 0.5
    for h in range(heads_width // HD):
        cols = slice(h * HD, (h + 1) * HD)
        q, k, v = given.q[:, cols], given.k[:, cols], given.v[:, cols]
        datt = given.datt[:, cols]
        s = jnp.where(same, dot_cols(q, k) * HD ** (-0.5), masked_score)
        prob = jnp.exp(s - given.log[:, h : h + 1])
        dprob = dot_cols(datt, v)
        ds = (prob * (dprob - lane_sum(prob * dprob))).astype(bf16)
        made.dq[:, cols] = (dot(ds, k) * HD ** (-0.5)).astype(bf16)
        made.dk[:, cols] = (dot_rows(ds, q) * HD ** (-0.5)).astype(bf16)
        made.dv[:, cols] = dot_rows(prob.astype(bf16), datt).astype(bf16)
    dh1 = dot(made.dq[...], given.wq[...])
    dh1 += dot(made.dk[...], given.wk[...])
    dh1 += dot(made.dv[...], given.wv[...])
    half = dh1.shape[0] // 2
    for i, ref in enumerate(made.dh1):
        put(ref, dh1[i * half : (i + 1) * half, :])
    row = made.vec_grad
    row[...] = jnp.zeros_like(row)
    row[:, :heads_width] = row_sum(made.dq[...].astype(f32))
    second = lane_pad(heads_width)
    row[:, second : second + heads_width] = row_sum(made.dv[...].astype(f32))


def put_vectors(give_ref, first, rows, values):
    high = values.astype(bf16)
    low = (values - high.astype(f32)).astype(bf16)
    give_ref[first : first + rows, :] = high
    give_ref[first + rows : first + 2 * rows, :] = low
    return high.astype(f32) + low.astype(f32)


def got_vectors(got_ref, rows):
    first = got_ref.shape[0] - 2 * rows
    high = got_ref[first : first + rows, :].astype(f32)
    return high + got_ref[first + rows :, :].astype(f32)


def attend_weights(n_dev, orders, bounds, given, made, h1_t, branch_t, left, branch_left):
    heads_width = given.right[0].shape[1]
    half = given.h1.shape[1] // 2
    h1_t[...] = jnp.transpose(given.h1[...].astype(f32))
    branch_t[...] = jnp.transpose(given.branch_grad[...].astype(f32))
    made.vec[...] = jnp.zeros_like(made.vec)
    at = 0
    for ref in given.vec_grads:
        for here, row, lanes in pieces_of(at, ref.shape[1], made.vec.shape[1]):
            made.vec[row, lanes] = ref[:, here]
        at += ref.shape[1]
    put(made.vec, put_vectors(made.give[0], half, made.vec.shape[0], made.vec[...]))
    for group, order in enumerate(orders):
        width = bounds[group + 1] - bounds[group]
        ordered_rows(left, h1_t, n_dev, order)
        for i, cols, lanes in parts_between(bounds, group, heads_width, 4):
            if i == 3:
                ordered_rows(branch_left, branch_t, n_dev, order)
            rows = (branch_left if i == 3 else left)[...].astype(bf16)
            product = dot(rows, given.right[i][:, cols]).astype(bf16)
            made.keep[group][:, lanes] = product[:half, :]
            made.give[group][:half, lanes] = product[half:, :]


def first_back(vec, given, made):
    width = given.x.shape[1]
    normed, scale = norm_parts(given.x[...].astype(f32))
    dh1 = both_halves(given.dh1, given.dh1_other)
    made.vec_grad[:, :width] = row_sum(dh1 * normed)
    made.vec_grad[:, width:] = row_sum(dh1)
    gain = given.vec[:, vec.gain1]
    put(made.dx, given.dmid[...] + norm_back(normed, scale, dh1, gain))


def back(n_dev, half_rows, vec, given, made):
    cap = given.dx.shape[0]
    half = given.sums[0].shape[0] // 2
    me, core = place()
    base, _ = my_span(given.lengths[...].astype(f32), given.owners[...].astype(f32), me)
    which, index = block_slots(base, n_dev, cap, half_rows)
    source = jnp.floor(index * (1.0 / half_rows))
    index = jnp.where(which == core, index + source * half_rows, NOWHERE)
    part = both_halves(given.sums, given.sums_other, slice(half, 2 * half))
    out = given.middle[...] + (part + given.vec[:, vec.br])
    rows = dot_rows(one_hot(index, (cap, cap), 1), out.astype(bf16))
    rows += dot_rows(one_hot(index + half_rows, (cap, cap), 1), given.dx[...])
    put(made.back, rows)


def home(n_dev, half_rows, given, made):
    me, core = place()
    tokens = made.mixed.shape[0]
    lengths, owners = given.lengths[...].astype(f32), given.owners[...].astype(f32)
    half, index = token_slots(lengths, owners, me, n_dev, tokens, half_rows)
    index = index + jnp.floor(index * (1.0 / half_rows)) * half_rows
    index = jnp.where(half == core, index, index + 2 * n_dev * half_rows)
    rows = jnp.concatenate([given.mine[...], given.other[...]], axis=0)
    shape = (rows.shape[0], tokens)
    put(made.mixed, dot_rows(one_hot(index, shape, 0), rows))
    put(made.grad, dot_rows(one_hot(index + half_rows, shape, 0), rows))


def share_of(far_bits):
    me = lax.axis_index(DP)
    return 2 * ((me >> far_bits[0]) & 1) + ((me >> far_bits[1]) & 1)


def mlp_weights(
    far_bits, orders, bounds, n_dev, vec, hidden_width, given, made, h2_all, g_all, hidden_all, dexp_all,
    natural, ordered,
):
    cap, width = given.h2.shape
    half_cap = cap // 2
    share = share_of(far_bits)
    part = given.we_part.shape[0]
    be = vec.be.start
    bias = jnp.zeros((1, part), f32)
    for i in range(4):
        end = min((i + 1) * part, hidden_width)
        piece = given.vec[:, be + i * part : be + end]
        if end < (i + 1) * part:
            piece = jnp.concatenate([piece, jnp.zeros((1, (i + 1) * part - end), f32)], axis=1)
        bias += jnp.where(share == i, piece, 0.0)
    for k in range(4):
        rows = slice(k * cap, (k + 1) * cap)
        if k == 0:
            h2_all[rows, :] = given.h2[...]
            g_all[rows, :] = given.g[...]
        else:
            for i, ref in enumerate((given.far[k - 1], given.far_other[k - 1])):
                at = slice(k * cap + i * half_cap, k * cap + (i + 1) * half_cap)
                h2_all[at, :] = ref[:half_cap, :]
                g_all[at, :] = ref[half_cap:, :]
        hidden, slope = gelu_both(dot_cols(h2_all[rows, :], given.we_part[...]) + bias)
        hidden_all[rows, :] = hidden.astype(bf16)
        dexp_all[rows, :] = (dot_cols(g_all[rows, :], given.wr_part[...]) * slope).astype(bf16)
    half = width // 2
    natural[:, :part] = dot_rows(g_all[...], hidden_all[...])
    natural[:, part : 2 * part] = dot_rows(h2_all[...], dexp_all[...])
    if 2 * part < bounds[-1]:
        natural[:, 2 * part :] = jnp.zeros((width, bounds[-1] - 2 * part), f32)
    for group, order in enumerate(orders):
        lanes = pl.ds(bounds[group], bounds[group + 1] - bounds[group])
        here = ordered.at[:, pl.ds(0, bounds[group + 1] - bounds[group])]
        ordered_rows(here, natural.at[:, lanes], n_dev, order)
        put(made.give[group], here[half:, :])
        put(made.keep[group], here[:half, :])


def turn(vec_rows, given, made):
    rows = given.keep.shape[0]
    total = given.keep[...].astype(f32) + given.got[:rows, :].astype(f32)
    put(made.keep, total[: rows // 2, :])
    made.give[: rows // 2, :] = total[rows // 2 :, :].astype(bf16)
    if vec_rows:
        vec = given.vec[...] + got_vectors(given.got, vec_rows)
        put(made.vec, put_vectors(made.give, rows // 2, vec_rows, vec))


def last_sums(bounds, vec_rows, vec, given, made):
    sums = given.vec[...] + got_vectors(given.got[0], vec_rows)
    for name, ref in zip(vec.names, made.vectors):
        at = getattr(vec, name)
        for here, row, lanes in pieces_of(at.start, at.stop - at.start, sums.shape[1]):
            ref[here] = sums[row, lanes].reshape(here.stop - here.start)
    for group, (keep, got) in enumerate(zip(given.keep, given.got)):
        value = keep[...].astype(f32) + got[: keep.shape[0], :].astype(f32)
        for i, cols, lanes in parts_between(bounds, group, made.weights[0].shape[1], 4):
            made.weights[i][:, cols] = value[:, lanes]


def mlp_cut(bounds, given, made):
    rows = given.keep[0].shape[0] // 4
    for group, (keep, got) in enumerate(zip(given.keep, given.got)):
        total = keep[...].astype(f32) + got[...].astype(f32)
        for k, ref in enumerate(made.cuts):
            ref[:, bounds[group] : bounds[group + 1]] = total[k * rows : (k + 1) * rows, :].astype(bf16)


def mlp_last(far_bits, part, given, made):
    share = share_of(far_bits)
    hidden_width = made.weights[0].shape[1]
    pieces = [ref[...].astype(f32) for ref in given.cuts]
    for i in range(4):
        own = jnp.zeros_like(pieces[0])
        for k, piece in enumerate(pieces):
            own += jnp.where((share ^ k) == i, piece, 0.0)
        end = min((i + 1) * part, hidden_width)
        for at, ref in enumerate(made.weights):
            ref[:, i * part : end] = own[:, at * part : at * part + end - i * part]


def swap_cores(values):
    return lax.ppermute(values, CORE, [(0, 1), (1, 0)])


def swap_dp(values, flip):
    return lax.ppermute(values, DP, [(i, i ^ flip) for i in range(lax.axis_size(DP))])


def spread(rows):
    return lax.all_to_all(rows, DP, split_axis=0, concat_axis=0, tiled=True)


def after(values, earlier):
    return lax.optimization_barrier((values, earlier))[0]


def next_step(pair, vec):
    keep, got = pair
    rows = keep.shape[0] // 2
    vec_rows = 0 if vec is None else vec.shape[0]
    if rows % 8:
        total = keep.astype(f32) + got[: 2 * rows].astype(f32)
        kept, give = total[:rows], total[rows:].astype(bf16)
        if vec is not None:
            got = got[2 * rows :].astype(f32)
            vec = vec + (got[:vec_rows] + got[vec_rows:])
            high = vec.astype(bf16)
            low = (vec - high.astype(f32)).astype(bf16)
            vec = high.astype(f32) + low.astype(f32)
            give = jnp.concatenate([give, high, low])
        return kept, give, vec
    columns = keep.shape[1]
    ins, outs = dict(keep=keep, got=got), dict(keep=((rows, columns), f32))
    outs.update(give=((rows + 2 * vec_rows, columns), bf16))
    if vec is not None:
        ins.update(vec=vec)
        outs.update(vec=(vec.shape, f32))
    made = call(functools.partial(turn, vec_rows), ins, outs)
    return made.keep, made.give, None if vec is None else made.vec


class Chains:
    def __init__(self, keep, give, orders, vec=None):
        self.orders, self.vec = orders, vec
        self.done = [1] * len(orders)
        self.pairs = [(k, swap_dp(g, 1 << order[0])) for k, g, order in zip(keep, give, orders)]

    def step(self, group, earlier):
        step = self.done[group]
        self.done[group] += 1
        pair = after(self.pairs[group], earlier)
        keep, give, vec = next_step(pair, None if group else self.vec)
        if not group:
            self.vec = vec
        self.pairs[group] = (keep, swap_dp(give, 1 << self.orders[group][step]))
        return keep

    def finish(self, earlier):
        for group, order in enumerate(self.orders):
            while self.done[group] < len(order):
                earlier = self.step(group, earlier)

    def kept(self):
        return [pair[0] for pair in self.pairs]

    def received(self):
        return [pair[1] for pair in self.pairs]


def on_device(
    patches, cotangent, image_lengths, image_owner, first_gain, first_shift, query_weight,
    query_bias, key_weight, value_weight, value_bias, output_weight, output_bias, second_gain,
    second_shift, expand_weight, expand_bias, reduce_weight, reduce_bias,
):
    n_dev = lax.axis_size(DP)
    tokens, width = patches.shape
    cap = 2 * tokens
    half_rows = cap // n_dev // 2
    heads_width, hidden_width = query_weight.shape[1], expand_weight.shape[1]
    heads = heads_width // HD
    n_bits = n_dev.bit_length() - 1
    far_bits = (1, n_bits - 2)
    flips = [flip_of(k, far_bits) for k in range(4)]
    rest = [bit for bit in range(n_bits) if bit not in far_bits]
    mlp_orders = (rest, rest[::-1])
    others = list(range(2, n_bits - 2))
    attend_orders = (
        [0, 1] + others + [n_bits - 2, n_bits - 1],
        [1, 0] + others + [n_bits - 2, n_bits - 1],
    )
    attend_bounds = (0, 1152, 4 * heads_width)
    wq, wk, wv, wo, we, wr = (
        w.T for w in (query_weight, key_weight, value_weight, output_weight, expand_weight, reduce_weight)
    )
    vec = Vectors(
        gain1=width, shift1=width, bo=width, gain2=width, shift2=width, br=width, be=hidden_width,
        bq=heads_width, bv=heads_width,
    )
    vector_args = [
        first_gain, first_shift, output_bias, second_gain, second_shift, reduce_bias, expand_bias,
        query_bias, value_bias,
    ]
    vectors = jnp.concatenate(
        [jnp.pad(v, (0, lane_pad(v.shape[0]) - v.shape[0])) for v in vector_args]
    ).reshape(1, -1)
    sizes = dict(lengths=image_lengths.reshape(1, -1), owners=image_owner.reshape(1, -1))
    wide32, wide16 = ((cap, width), f32), ((cap, width), bf16)
    half16 = ((cap // 2, width), bf16)
    head16 = ((cap, heads_width), bf16)
    at_place = lambda body, *more: functools.partial(body, n_dev, half_rows, *more)
    scratch = pltpu.VMEM

    sent = call(
        at_place(pack, tokens), dict(**sizes, x=patches, g=cotangent), dict(send=wide16), far=True, vmem=62
    )
    part = -(-hidden_width // 64) * 16
    at_share = share_of(far_bits) * part
    padding = ((0, 4 * part - hidden_width), (0, 0))
    we_part, wr_part = (
        lax.dynamic_slice_in_dim(jnp.pad(w, padding), at_share, part, 0) for w in (we, wr)
    )
    got, we_part, wr_part = lax.optimization_barrier((spread(sent.send), we_part, wr_part))
    arrived = dict(**sizes, mine=got, other=swap_cores(got))
    came_in = call(
        at_place(arrive, vec), dict(**arrived, vec=vectors),
        dict(mask=((cap, cap), f32), x=wide16, h1=wide16, g=wide16), us=6,
    )
    mask, x, h1, g = came_in.mask, came_in.x, came_in.h1, came_in.g
    fwd = call(
        functools.partial(attend, vec),
        dict(h1=h1, mask=mask, vec=vectors, wq=wq, wk=wk, wv=wv, wo=wo),
        dict(q=head16, k=head16, v=head16, log=((cap, heads), f32), att=head16, branch=wide16),
        us=5,
    )
    branch_other = swap_cores(fwd.branch)
    mid = call(
        functools.partial(mlp, vec),
        dict(x=x, branch=fwd.branch, branch_other=branch_other, g=g, vec=vectors, we=we, wr=wr),
        dict(
            middle=wide32, h2=wide16, halves=wide16, sums=[wide16, wide16],
            be_grad=((1, lane_pad(hidden_width)), f32),
        ),
        scratch=[scratch((cap, width), f32)] * 2,
    )
    halves = [swap_dp(mid.halves, flip) for flip in flips[1:]]
    sums = dict(sums=mid.sums, sums_other=[swap_cores(rows) for rows in mid.sums])
    half_back = call(
        functools.partial(middle_back, vec),
        dict(g=g, middle=mid.middle, vec=vectors, wo=wo, **sums),
        dict(dmid=wide32, branch_grad=wide16, datt=head16, vec_grad=((1, 4 * width), f32)),
    )
    att_back = call(
        attend_back,
        dict(
            mask=mask, q=fwd.q, k=fwd.k, v=fwd.v, datt=half_back.datt, log=fwd.log,
            wq=wq, wk=wk, wv=wv,
        ),
        dict(
            dq=head16, dk=head16, dv=head16, dh1=[half16, half16],
            vec_grad=((1, 2 * lane_pad(heads_width)), f32),
        ),
    )
    first = call(
        functools.partial(first_back, vec),
        dict(
            x=x, dh1=att_back.dh1, dh1_other=[swap_cores(rows) for rows in att_back.dh1],
            vec=vectors, dmid=half_back.dmid,
        ),
        dict(dx=wide16, vec_grad=((1, 2 * width), f32)),
    )

    columns = attend_bounds[1]
    vec_rows = -(-vec.size // (16 * columns)) * 16
    keeps, gives = [], []
    for i in range(len(attend_orders)):
        span = attend_bounds[i + 1] - attend_bounds[i]
        keeps.append(((width // 2, span), bf16))
        gives.append(((width // 2 + (0 if i else 2 * vec_rows), span), bf16))
    products = call(
        functools.partial(attend_weights, n_dev, attend_orders, attend_bounds),
        dict(
            h1=h1, branch_grad=half_back.branch_grad,
            right=[att_back.dq, att_back.dk, att_back.dv, fwd.att],
            vec_grads=[first.vec_grad, half_back.vec_grad, mid.be_grad, att_back.vec_grad],
        ),
        dict(vec=((vec_rows, columns), f32), keep=keeps, give=gives),
        scratch=[scratch((width, cap), f32)] * 4,
    )
    a = Chains(products.keep, products.give, attend_orders, products.vec)
    dx = after(first.dx, products.keep[0])
    packed = call(
        at_place(back, vec), dict(**sizes, vec=vectors, middle=mid.middle, dx=dx, **sums), dict(back=wide16)
    ).back
    came = spread(packed)
    far = after(halves, packed)
    far_other = [swap_cores(rows) for rows in far[:2]]
    far[2] = after(far[2], far_other[0])
    far_other.append(swap_cores(far[2]))
    mlp_bounds = (0, 768, lane_pad(2 * part))
    spans = [after_ - before for before, after_ in zip(mlp_bounds, mlp_bounds[1:])]
    mlp_half = [((width // 2, span), bf16) for span in spans]
    grads = call(
        functools.partial(
            mlp_weights, far_bits, [list(o) + list(far_bits) for o in mlp_orders], mlp_bounds, n_dev, vec,
            hidden_width,
        ),
        dict(vec=vectors, we_part=we_part, wr_part=wr_part, h2=mid.h2, g=g, far=far, far_other=far_other),
        dict(give=mlp_half, keep=mlp_half),
        scratch=[scratch((4 * cap, width), bf16)] * 2 + [scratch((4 * cap, part), bf16)] * 2
        + [scratch((width, mlp_bounds[-1]), f32), scratch((width, max(spans)), f32)],
        vmem=36,
    )
    m = Chains(grads.keep, grads.give, mlp_orders)
    last = grads.keep[0]
    last = a.step(0, last)
    last = a.step(1, last)
    last = m.step(0, last)
    last = a.step(0, last)
    last = a.step(1, last)
    last = m.step(1, last)
    last = a.step(0, last)
    last = a.step(1, last)
    m.finish(last)
    a.finish(last)
    own_rows = width // n_dev
    cut = ((own_rows, mlp_bounds[-1]), bf16)
    cuts = call(
        functools.partial(mlp_cut, mlp_bounds), dict(keep=m.kept(), got=m.received()), dict(cuts=[cut] * 4)
    ).cuts
    cuts = [cuts[0]] + [swap_dp(rows, flip) for rows, flip in zip(cuts[1:], flips[1:])]
    final = call(
        at_place(home), dict(**sizes, mine=came, other=swap_cores(came)),
        dict(mixed=((tokens, width), bf16), grad=((tokens, width), bf16)),
    )
    mlp_own = call(
        functools.partial(mlp_last, far_bits, part), dict(cuts=cuts),
        dict(weights=[((own_rows, hidden_width), f32)] * 2),
    ).weights
    own = call(
        functools.partial(last_sums, attend_bounds, vec_rows, vec),
        dict(vec=a.vec, keep=a.kept(), got=a.received()),
        dict(
            vectors=[((v.shape[0],), f32) for v in vector_args],
            weights=[((own_rows, heads_width), f32)] * 4,
        ),
    )
    total = types.SimpleNamespace(**dict(zip(vec.names, own.vectors)))
    wq_sum, wk_sum, wv_sum, wo_sum = own.weights
    wr_sum, we_sum = mlp_own
    return (
        final.mixed, final.grad, total.gain1, total.shift1, wq_sum, total.bq, wk_sum, wv_sum, total.bv,
        wo_sum, total.bo, total.gain2, total.shift2, we_sum, total.be, wr_sum, total.br,
    )


def solution(mesh):
    rows, all_same = P(DP, None), P()
    cols, vector = P(None, CORE), P(CORE)
    tiles = P(DP, CORE)
    in_specs = (
        rows, rows, all_same, all_same, all_same, all_same, cols, vector, cols, cols, vector, cols,
        all_same, all_same, all_same, cols, vector, cols, all_same,
    )
    out_specs = (
        rows, rows, all_same, all_same, tiles, vector, tiles, tiles, vector, tiles, all_same, all_same,
        all_same, tiles, vector, tiles, all_same,
    )
    return jax.shard_map(
        on_device, mesh=mesh, in_specs=in_specs, out_specs=out_specs, check_vma=False
    )
```

```python
import functools
import types

import jax
import jax.numpy as jnp
from jax import lax
from jax.experimental import pallas as pl
from jax.experimental.pallas import tpu as pltpu
from jax.sharding import PartitionSpec as P

HD = 72
DP, CORE = "dp", "tensor"
masked_score = -1000000000.0
norm_eps = 1e-06
gelu_scale = 0.7978845608028654
gelu_cubic = 0.044715
f32 = jnp.float32
bf16 = jnp.bfloat16
MIB = 1024 * 1024
NOWHERE = -1e6


def dot(left, right):
    return lax.dot_general(left, right, (((1,), (0,)), ((), ())), preferred_element_type=f32)


def dot_cols(left, right):
    return lax.dot_general(left, right, (((1,), (1,)), ((), ())), preferred_element_type=f32)


def dot_rows(left, right):
    return lax.dot_general(left, right, (((0,), (0,)), ((), ())), preferred_element_type=f32)


def iota(shape, dim):
    return lax.broadcasted_iota(jnp.int32, shape, dim).astype(f32)


def row_sum(values):
    return jnp.sum(values, axis=0, keepdims=True)


def lane_sum(values):
    return jnp.sum(values, axis=1, keepdims=True)


def lane_mean(values):
    return jnp.mean(values, axis=1, keepdims=True)


def lane_pad(size):
    return -(-size // 128) * 128


def put(ref, value):
    ref[...] = value.astype(ref.dtype)


def my_span(lengths, owners, me):
    base = lane_sum(jnp.where(owners < me, lengths, 0.0))
    used = lane_sum(jnp.where(owners == me, lengths, 0.0))
    return base, used


def token_slots(lengths, owners, me, n_dev, tokens, half_rows):
    device = iota((n_dev, lengths.shape[1]), 0)
    base = lane_sum(jnp.where(owners < device, lengths, 0.0))
    pos = iota((1, tokens), 1) * n_dev + me
    below = base <= pos
    target = row_sum(jnp.where(below, 1.0, 0.0)) - 1.0
    start = jnp.max(jnp.where(below, base, -1.0), axis=0, keepdims=True)
    slot = jnp.floor((pos - start) * (1.0 / n_dev))
    half = jnp.floor(slot * (1.0 / half_rows))
    return half, target * half_rows + slot - half * half_rows


def block_slots(base, n_dev, cap, half_rows):
    p = iota((cap, 1), 0)
    pos = base + p
    source = pos - n_dev * jnp.floor(pos * (1.0 / n_dev))
    slot = jnp.floor(p * (1.0 / n_dev))
    half = jnp.floor(slot * (1.0 / half_rows))
    return half, source * half_rows + slot - half * half_rows


def one_hot(index, shape, dim):
    return jnp.where(index == iota(shape, dim), 1.0, 0.0).astype(bf16)


def place():
    return lax.axis_index(DP).astype(f32), lax.axis_index(CORE).astype(f32)


def norm_parts(values):
    centered = values - lane_mean(values)
    scale = lax.rsqrt(lane_mean(centered * centered) + norm_eps)
    return centered * scale, scale


def norm_back(normed, scale, grad, gain):
    inner = grad * gain
    return scale * (inner - lane_mean(inner) - normed * lane_mean(inner * normed))


def gelu_both(values):
    square = values * values
    bent = jnp.tanh(gelu_scale * values * (1.0 + gelu_cubic * square))
    half = 0.5 * (1.0 + bent)
    slope = half + 0.5 * values * (1.0 - bent * bent) * (
        gelu_scale * (1.0 + 3.0 * gelu_cubic * square)
    )
    return values * half, slope


def flip_of(block, order):
    flip = 0 * block
    for step, bit in enumerate(order):
        flip = flip | (((block >> (len(order) - 1 - step)) & 1) << bit)
    return flip


def ordered_rows(out_ref, from_ref, n_dev, order):
    width = from_ref.shape[0]
    owner_rows = width // n_dev
    me = lax.axis_index(DP)
    if owner_rows % 8:
        i = iota((width, 1), 0)
        block = jnp.floor((i + 0.5) * (1.0 / owner_rows))
        owner = (flip_of(block.astype(jnp.int32), order) ^ me).astype(f32)
        pick = one_hot(owner * owner_rows + (i - block * owner_rows), (width, width), 1)
        out_ref[...] = dot(pick, from_ref[...].astype(bf16))
        return
    for block in range(n_dev):
        start = pl.multiple_of((me ^ flip_of(block, order)) * owner_rows, 8)
        rows = slice(block * owner_rows, (block + 1) * owner_rows)
        out_ref[rows, :] = from_ref[pl.ds(start, owner_rows), :]


def parts_between(bounds, group, size, count):
    for i in range(count):
        first, last = max(i * size, bounds[group]), min((i + 1) * size, bounds[group + 1])
        if first < last:
            yield (
                i,
                slice(first - i * size, last - i * size),
                slice(first - bounds[group], last - bounds[group]),
            )


def pieces_of(start, size, columns):
    done = 0
    while done < size:
        row, lane = (start + done) // columns, (start + done) % columns
        now = min(columns - lane, size - done)
        yield slice(done, done + now), slice(row, row + 1), slice(lane, lane + now)
        done += now


def call(body, ins, outs, scratch=(), vmem=16, far=False, us=0):
    ins_flat, ins_tree = jax.tree.flatten(ins)
    is_out = lambda x: isinstance(x, tuple)
    outs_flat, outs_tree = jax.tree.flatten(outs, is_leaf=is_out)
    n_in, n_out = len(ins_flat), len(outs_flat)

    def kernel(*refs):
        given, rest = refs[:n_in], refs[n_in + n_out :]
        if far:
            near, sems, rest = rest[:n_in], rest[n_in], rest[n_in + 1 :]
            copies = [
                pltpu.make_async_copy(ref, to, sems.at[i]) for i, (ref, to) in enumerate(zip(given, near))
            ]
            for copy in copies:
                copy.start()

            def arrival(copy, to):
                def wait():
                    copy.wait()
                    return to[...]

                return wait

            given = [arrival(copy, to) for copy, to in zip(copies, near)]
        given = types.SimpleNamespace(**jax.tree.unflatten(ins_tree, given))
        made = types.SimpleNamespace(**jax.tree.unflatten(outs_tree, refs[n_in : n_in + n_out]))
        body(given, made, *rest)

    copies = [pltpu.VMEM(x.shape, x.dtype) for x in ins_flat]
    copies += [pltpu.SemaphoreType.DMA((n_in,))]
    results = pl.pallas_call(
        kernel,
        name=getattr(body, "func", body).__name__,
        out_shape=[jax.ShapeDtypeStruct(shape, dtype) for shape, dtype in outs_flat],
        in_specs=[pl.BlockSpec(memory_space=pltpu.HBM if far else pltpu.VMEM)] * n_in,
        out_specs=[pl.BlockSpec(memory_space=pltpu.VMEM)] * n_out,
        scratch_shapes=(copies if far else []) + list(scratch),
        cost_estimate=pl.CostEstimate(flops=us * 10**9, bytes_accessed=us * 10**6, transcendentals=0),
        compiler_params=pltpu.CompilerParams(vmem_limit_bytes=vmem * MIB),
    )(*ins_flat)
    return types.SimpleNamespace(**jax.tree.unflatten(outs_tree, results))


def pack(n_dev, half_rows, tokens, given, made):
    me, core = place()
    lengths, owners = given.lengths().astype(f32), given.owners().astype(f32)
    half, index = token_slots(lengths, owners, me, n_dev, tokens, half_rows)
    target = jnp.floor(index * (1.0 / half_rows))
    index = jnp.where(half == core, index + target * half_rows, NOWHERE)
    shape = (2 * n_dev * half_rows, tokens)
    x_pick, g_pick = one_hot(index, shape, 0), one_hot(index + half_rows, shape, 0)
    rows = dot(x_pick, given.x())
    put(made.send, rows + dot(g_pick, given.g()))


def block_rows(given, n_dev, cap, half_rows, kind):
    me, core = place()
    base, _ = my_span(given.lengths[...].astype(f32), given.owners[...].astype(f32), me)
    half, index = block_slots(base, n_dev, cap, half_rows)
    source = jnp.floor(index * (1.0 / half_rows))
    index = index + (source + kind) * half_rows
    index = jnp.where(half == core, index, index + 2 * n_dev * half_rows)
    pick = one_hot(index, (cap, 2 * cap), 1)
    return dot(pick, jnp.concatenate([given.mine[...], given.other[...]], axis=0))


def image_mask(lengths, owners, cap):
    me, _ = place()
    base, used = my_span(lengths, owners, me)
    n_img = lengths.shape[1]
    starts = lane_sum(jnp.where(iota((n_img, n_img), 1) < iota((n_img, n_img), 0), lengths, 0.0))
    p = iota((1, cap), 1)
    count = row_sum(jnp.where(starts <= base + p, 1.0, 0.0))
    seg_row = jnp.where(p < used, count, 0.0)
    on_diagonal = iota((cap, cap), 0) == iota((cap, cap), 1)
    seg_col = lane_sum(jnp.where(on_diagonal, seg_row, 0.0))
    return jnp.where(seg_col == seg_row, 1.0, 0.0)


class Vectors:
    def __init__(self, **sizes):
        self.names, self.size = list(sizes), 0
        for name, size in sizes.items():
            setattr(self, name, slice(self.size, self.size + size))
            self.size += lane_pad(size)


def arrive(n_dev, half_rows, vec, given, made):
    cap = made.x.shape[0]
    x = block_rows(given, n_dev, cap, half_rows, 0)
    put(made.x, x)
    normed, _ = norm_parts(x)
    put(made.h1, normed * given.vec[:, vec.gain1] + given.vec[:, vec.shift1])
    put(made.g, block_rows(given, n_dev, cap, half_rows, 1))
    put(made.mask, image_mask(given.lengths[...].astype(f32), given.owners[...].astype(f32), cap))


def attend(vec, given, made):
    same = given.mask[...] > 0.5
    row, h1 = given.vec, given.h1[...]
    put(made.q, dot_cols(h1, given.wq[...]) + row[:, vec.bq])
    put(made.k, dot_cols(h1, given.wk[...]))
    put(made.v, dot_cols(h1, given.wv[...]) + row[:, vec.bv])
    for h in range(made.q.shape[1] // HD):
        cols = slice(h * HD, (h + 1) * HD)
        s = dot_cols(made.q[:, cols], made.k[:, cols]) * HD ** (-0.5)
        s = jnp.where(same, s, masked_score)
        top = jnp.max(s, axis=1, keepdims=True)
        e = jnp.exp(s - top)
        total = lane_sum(e)
        made.log[:, h : h + 1] = top + jnp.log(total)
        made.att[:, cols] = dot((e / total).astype(bf16), made.v[:, cols]).astype(bf16)
    put(made.branch, dot(made.att[...], given.wo[...]))


def both(mine, other, rows=slice(None)):
    return mine[rows, :].astype(f32) + other[rows, :].astype(f32)


def both_halves(mine, other, rows=slice(None)):
    return jnp.concatenate([both(a, b, rows) for a, b in zip(mine, other)], axis=0)


def chunks_of(width, step):
    full = width // step
    return full, full * step, width - full * step


def mlp(vec, given, made, out_total, dh2_total):
    cap = made.middle.shape[0]
    half = cap // 2
    row = given.vec
    branch = both(given.branch, given.branch_other) + row[:, vec.bo]
    middle = given.x[...].astype(f32) + branch
    put(made.middle, middle)
    normed, _ = norm_parts(middle)
    put(made.h2, normed * row[:, vec.gain2] + row[:, vec.shift2])
    start = pl.multiple_of(lax.axis_index(CORE) * half, half)
    made.halves[:half, :] = made.h2[pl.ds(start, half), :]
    made.halves[half:, :] = given.g[pl.ds(start, half), :]
    step = 1024
    full, done, rest = chunks_of(given.we.shape[0], step)
    out_total[...] = jnp.zeros_like(out_total)
    dh2_total[...] = jnp.zeros_like(dh2_total)
    made.be_grad[...] = jnp.zeros_like(made.be_grad)
    first = vec.be.start

    def chunk(rows, bias):
        we, wr = given.we[rows, :], given.wr[rows, :]
        hidden, slope = gelu_both(dot_cols(made.h2[...], we) + row[:, bias])
        dexp = (dot_cols(given.g[...], wr) * slope).astype(bf16)
        made.be_grad[:, rows] = row_sum(dexp.astype(f32))
        out_total[...] += dot(hidden.astype(bf16), wr)
        dh2_total[...] += dot(dexp, we)

    @pl.loop(0, full, unroll=True)
    def _(i):
        at = pl.multiple_of(i * step, step)
        chunk(pl.ds(at, step), pl.ds(pl.multiple_of(first + at, 128), step))

    if rest:
        chunk(slice(done, done + rest), slice(first + done, first + done + rest))
    for i, ref in enumerate(made.sums):
        rows = slice(i * half, (i + 1) * half)
        ref[:half, :] = dh2_total[rows, :].astype(bf16)
        ref[half:, :] = out_total[rows, :].astype(bf16)


def middle_back(vec, given, made):
    width = given.middle.shape[1]
    half = given.sums[0].shape[0] // 2
    g = given.g[...].astype(f32)
    normed, scale = norm_parts(given.middle[...])
    dh2 = both_halves(given.sums, given.sums_other, slice(0, half))
    dmid = g + norm_back(normed, scale, dh2, given.vec[:, vec.gain2])
    put(made.dmid, dmid)
    branch = dmid.astype(bf16)
    put(made.branch_grad, branch)
    put(made.datt, dot_cols(branch, given.wo[...]))
    for i, values in enumerate([branch.astype(f32), dh2 * normed, dh2, g]):
        made.vec_grad[:, i * width : (i + 1) * width] = row_sum(values)


def attend_back(given, made):
    heads_width = made.dq.shape[1]
    same = given.mask[...] > 0.5
    for h in range(heads_width // HD):
        cols = slice(h * HD, (h + 1) * HD)
        q, k, v = given.q[:, cols], given.k[:, cols], given.v[:, cols]
        datt = given.datt[:, cols]
        s = jnp.where(same, dot_cols(q, k) * HD ** (-0.5), masked_score)
        prob = jnp.exp(s - given.log[:, h : h + 1])
        dprob = dot_cols(datt, v)
        ds = (prob * (dprob - lane_sum(prob * dprob))).astype(bf16)
        made.dq[:, cols] = (dot(ds, k) * HD ** (-0.5)).astype(bf16)
        made.dk[:, cols] = (dot_rows(ds, q) * HD ** (-0.5)).astype(bf16)
        made.dv[:, cols] = dot_rows(prob.astype(bf16), datt).astype(bf16)
    dh1 = dot(made.dq[...], given.wq[...])
    dh1 += dot(made.dk[...], given.wk[...])
    dh1 += dot(made.dv[...], given.wv[...])
    half = dh1.shape[0] // 2
    for i, ref in enumerate(made.dh1):
        put(ref, dh1[i * half : (i + 1) * half, :])
    row = made.vec_grad
    row[...] = jnp.zeros_like(row)
    row[:, :heads_width] = row_sum(made.dq[...].astype(f32))
    second = lane_pad(heads_width)
    row[:, second : second + heads_width] = row_sum(made.dv[...].astype(f32))


def put_vectors(give_ref, first, rows, values):
    high = values.astype(bf16)
    low = (values - high.astype(f32)).astype(bf16)
    give_ref[first : first + rows, :] = high
    give_ref[first + rows : first + 2 * rows, :] = low
    return high.astype(f32) + low.astype(f32)


def got_vectors(got_ref, rows):
    first = got_ref.shape[0] - 2 * rows
    high = got_ref[first : first + rows, :].astype(f32)
    return high + got_ref[first + rows :, :].astype(f32)


def attend_weights(n_dev, orders, bounds, given, made, h1_t, branch_t, left, branch_left):
    heads_width = given.right[0].shape[1]
    half = given.h1.shape[1] // 2
    h1_t[...] = jnp.transpose(given.h1[...].astype(f32))
    branch_t[...] = jnp.transpose(given.branch_grad[...].astype(f32))
    made.vec[...] = jnp.zeros_like(made.vec)
    at = 0
    for ref in given.vec_grads:
        for here, row, lanes in pieces_of(at, ref.shape[1], made.vec.shape[1]):
            made.vec[row, lanes] = ref[:, here]
        at += ref.shape[1]
    put(made.vec, put_vectors(made.give[0], half, made.vec.shape[0], made.vec[...]))
    for group, order in enumerate(orders):
        width = bounds[group + 1] - bounds[group]
        ordered_rows(left, h1_t, n_dev, order)
        parts = list(parts_between(bounds, group, heads_width, 4))
        for shift in (False, True):
            chosen = [part for part in parts if (part[0] == 3) == shift]
            if not chosen:
                continue
            if shift:
                ordered_rows(branch_left, branch_t, n_dev, order)
            rows = (branch_left if shift else left)[...].astype(bf16)
            right = [given.right[i][:, cols] for i, cols, _ in chosen]
            right = jnp.concatenate(right, axis=1) if len(right) > 1 else right[0]
            product = dot(rows, right).astype(bf16)
            lanes = slice(chosen[0][2].start, chosen[-1][2].stop)
            made.keep[group][:, lanes] = product[:half, :]
            made.give[group][:half, lanes] = product[half:, :]


def first_back(vec, given, made):
    width = given.x.shape[1]
    normed, scale = norm_parts(given.x[...].astype(f32))
    dh1 = both_halves(given.dh1, given.dh1_other)
    made.vec_grad[:, :width] = row_sum(dh1 * normed)
    made.vec_grad[:, width:] = row_sum(dh1)
    gain = given.vec[:, vec.gain1]
    put(made.dx, given.dmid[...] + norm_back(normed, scale, dh1, gain))


def back(n_dev, half_rows, vec, given, made):
    cap = given.dx.shape[0]
    half = given.sums[0].shape[0] // 2
    me, core = place()
    base, _ = my_span(given.lengths[...].astype(f32), given.owners[...].astype(f32), me)
    which, index = block_slots(base, n_dev, cap, half_rows)
    source = jnp.floor(index * (1.0 / half_rows))
    index = jnp.where(which == core, index + source * half_rows, NOWHERE)
    part = both_halves(given.sums, given.sums_other, slice(half, 2 * half))
    out = given.middle[...] + (part + given.vec[:, vec.br])
    rows = dot_rows(one_hot(index, (cap, cap), 1), out.astype(bf16))
    rows += dot_rows(one_hot(index + half_rows, (cap, cap), 1), given.dx[...])
    put(made.back, rows)


def home(n_dev, half_rows, given, made):
    me, core = place()
    tokens = made.mixed.shape[0]
    lengths, owners = given.lengths[...].astype(f32), given.owners[...].astype(f32)
    half, index = token_slots(lengths, owners, me, n_dev, tokens, half_rows)
    index = index + jnp.floor(index * (1.0 / half_rows)) * half_rows
    index = jnp.where(half == core, index, index + 2 * n_dev * half_rows)
    rows = jnp.concatenate([given.mine[...], given.other[...]], axis=0)
    shape = (rows.shape[0], tokens)
    put(made.mixed, dot_rows(one_hot(index, shape, 0), rows))
    put(made.grad, dot_rows(one_hot(index + half_rows, shape, 0), rows))


def share_of(far_bits):
    me = lax.axis_index(DP)
    return 2 * ((me >> far_bits[0]) & 1) + ((me >> far_bits[1]) & 1)


def mlp_weights(
    far_bits, orders, bounds, n_dev, vec, hidden_width, given, made, h2_all, g_all, hidden_all, dexp_all,
    natural, ordered,
):
    cap, width = given.h2.shape
    half_cap = cap // 2
    share = share_of(far_bits)
    part = given.we_part.shape[0]
    be = vec.be.start
    bias = jnp.zeros((1, part), f32)
    for i in range(4):
        end = min((i + 1) * part, hidden_width)
        piece = given.vec[:, be + i * part : be + end]
        if end < (i + 1) * part:
            piece = jnp.concatenate([piece, jnp.zeros((1, (i + 1) * part - end), f32)], axis=1)
        bias += jnp.where(share == i, piece, 0.0)
    for k in range(4):
        rows = slice(k * cap, (k + 1) * cap)
        if k == 0:
            h2_all[rows, :] = given.h2[...]
            g_all[rows, :] = given.g[...]
        else:
            for i, ref in enumerate((given.far[k - 1], given.far_other[k - 1])):
                at = slice(k * cap + i * half_cap, k * cap + (i + 1) * half_cap)
                h2_all[at, :] = ref[:half_cap, :]
                g_all[at, :] = ref[half_cap:, :]
        hidden, slope = gelu_both(dot_cols(h2_all[rows, :], given.we_part[...]) + bias)
        hidden_all[rows, :] = hidden.astype(bf16)
        dexp_all[rows, :] = (dot_cols(g_all[rows, :], given.wr_part[...]) * slope).astype(bf16)
    half = width // 2
    natural[:, :part] = dot_rows(g_all[...], hidden_all[...])
    natural[:, part : 2 * part] = dot_rows(h2_all[...], dexp_all[...])
    if 2 * part < bounds[-1]:
        natural[:, 2 * part :] = jnp.zeros((width, bounds[-1] - 2 * part), f32)
    for group, order in enumerate(orders):
        lanes = pl.ds(bounds[group], bounds[group + 1] - bounds[group])
        here = ordered.at[:, pl.ds(0, bounds[group + 1] - bounds[group])]
        ordered_rows(here, natural.at[:, lanes], n_dev, order)
        put(made.give[group], here[half:, :])
        put(made.keep[group], here[:half, :])


def turn(vec_rows, given, made):
    rows = given.keep.shape[0]
    total = given.keep[...].astype(f32) + given.got[:rows, :].astype(f32)
    put(made.keep, total[: rows // 2, :])
    made.give[: rows // 2, :] = total[rows // 2 :, :].astype(bf16)
    if vec_rows:
        vec = given.vec[...] + got_vectors(given.got, vec_rows)
        put(made.vec, put_vectors(made.give, rows // 2, vec_rows, vec))


def last_sums(bounds, vec_rows, vec, given, made):
    sums = given.vec[...] + got_vectors(given.got[0], vec_rows)
    for name, ref in zip(vec.names, made.vectors):
        at = getattr(vec, name)
        for here, row, lanes in pieces_of(at.start, at.stop - at.start, sums.shape[1]):
            ref[here] = sums[row, lanes].reshape(here.stop - here.start)
    for group, (keep, got) in enumerate(zip(given.keep, given.got)):
        value = keep[...].astype(f32) + got[: keep.shape[0], :].astype(f32)
        for i, cols, lanes in parts_between(bounds, group, made.weights[0].shape[1], 4):
            made.weights[i][:, cols] = value[:, lanes]


def mlp_cut(bounds, given, made):
    rows = given.keep[0].shape[0] // 4
    for group, (keep, got) in enumerate(zip(given.keep, given.got)):
        total = keep[...].astype(f32) + got[...].astype(f32)
        for k, ref in enumerate(made.cuts):
            ref[:, bounds[group] : bounds[group + 1]] = total[k * rows : (k + 1) * rows, :].astype(bf16)


def mlp_last(far_bits, part, given, made):
    share = share_of(far_bits)
    hidden_width = made.weights[0].shape[1]
    pieces = [ref[...].astype(f32) for ref in given.cuts]
    for i in range(4):
        own = jnp.zeros_like(pieces[0])
        for k, piece in enumerate(pieces):
            own += jnp.where((share ^ k) == i, piece, 0.0)
        end = min((i + 1) * part, hidden_width)
        for at, ref in enumerate(made.weights):
            ref[:, i * part : end] = own[:, at * part : at * part + end - i * part]


def swap_cores(values):
    return lax.ppermute(values, CORE, [(0, 1), (1, 0)])


def swap_dp(values, flip):
    return lax.ppermute(values, DP, [(i, i ^ flip) for i in range(lax.axis_size(DP))])


def spread(rows):
    return lax.all_to_all(rows, DP, split_axis=0, concat_axis=0, tiled=True)


def after(values, earlier):
    return lax.optimization_barrier((values, earlier))[0]


def next_step(pair, vec):
    keep, got = pair
    rows = keep.shape[0] // 2
    vec_rows = 0 if vec is None else vec.shape[0]
    if rows % 8:
        total = keep.astype(f32) + got[: 2 * rows].astype(f32)
        kept, give = total[:rows], total[rows:].astype(bf16)
        if vec is not None:
            got = got[2 * rows :].astype(f32)
            vec = vec + (got[:vec_rows] + got[vec_rows:])
            high = vec.astype(bf16)
            low = (vec - high.astype(f32)).astype(bf16)
            vec = high.astype(f32) + low.astype(f32)
            give = jnp.concatenate([give, high, low])
        return kept, give, vec
    columns = keep.shape[1]
    ins, outs = dict(keep=keep, got=got), dict(keep=((rows, columns), f32))
    outs.update(give=((rows + 2 * vec_rows, columns), bf16))
    if vec is not None:
        ins.update(vec=vec)
        outs.update(vec=(vec.shape, f32))
    made = call(functools.partial(turn, vec_rows), ins, outs)
    return made.keep, made.give, None if vec is None else made.vec


class Chains:
    def __init__(self, keep, give, orders, vec=None):
        self.orders, self.vec = orders, vec
        self.done = [1] * len(orders)
        self.pairs = [(k, swap_dp(g, 1 << order[0])) for k, g, order in zip(keep, give, orders)]

    def step(self, group, earlier):
        step = self.done[group]
        self.done[group] += 1
        pair = after(self.pairs[group], earlier)
        keep, give, vec = next_step(pair, None if group else self.vec)
        if not group:
            self.vec = vec
        self.pairs[group] = (keep, swap_dp(give, 1 << self.orders[group][step]))
        return keep

    def finish(self, earlier):
        for group, order in enumerate(self.orders):
            while self.done[group] < len(order):
                earlier = self.step(group, earlier)

    def kept(self):
        return [pair[0] for pair in self.pairs]

    def received(self):
        return [pair[1] for pair in self.pairs]


def on_device(
    patches, cotangent, image_lengths, image_owner, first_gain, first_shift, query_weight,
    query_bias, key_weight, value_weight, value_bias, output_weight, output_bias, second_gain,
    second_shift, expand_weight, expand_bias, reduce_weight, reduce_bias,
):
    n_dev = lax.axis_size(DP)
    tokens, width = patches.shape
    cap = 2 * tokens
    half_rows = cap // n_dev // 2
    heads_width, hidden_width = query_weight.shape[1], expand_weight.shape[1]
    heads = heads_width // HD
    n_bits = n_dev.bit_length() - 1
    far_bits = (1, n_bits - 2)
    flips = [flip_of(k, far_bits) for k in range(4)]
    rest = [bit for bit in range(n_bits) if bit not in far_bits]
    mlp_orders = (rest, rest[::-1])
    others = list(range(2, n_bits - 2))
    attend_orders = (
        [0, 1] + others + [n_bits - 2, n_bits - 1],
        [n_bits - 2, 1, 0] + others + [n_bits - 1],
    )
    attend_bounds = (0, 1152, 4 * heads_width)
    wq, wk, wv, wo, we, wr = (
        w.T for w in (query_weight, key_weight, value_weight, output_weight, expand_weight, reduce_weight)
    )
    vec = Vectors(
        gain1=width, shift1=width, bo=width, gain2=width, shift2=width, br=width, be=hidden_width,
        bq=heads_width, bv=heads_width,
    )
    vector_args = [
        first_gain, first_shift, output_bias, second_gain, second_shift, reduce_bias, expand_bias,
        query_bias, value_bias,
    ]
    vectors = jnp.concatenate(
        [jnp.pad(v, (0, lane_pad(v.shape[0]) - v.shape[0])) for v in vector_args]
    ).reshape(1, -1)
    sizes = dict(lengths=image_lengths.reshape(1, -1), owners=image_owner.reshape(1, -1))
    wide32, wide16 = ((cap, width), f32), ((cap, width), bf16)
    half16 = ((cap // 2, width), bf16)
    head16 = ((cap, heads_width), bf16)
    at_place = lambda body, *more: functools.partial(body, n_dev, half_rows, *more)
    scratch = pltpu.VMEM

    sent = call(
        at_place(pack, tokens), dict(**sizes, x=patches, g=cotangent), dict(send=wide16), far=True, vmem=62
    )
    part = -(-hidden_width // 64) * 16
    at_share = share_of(far_bits) * part
    padding = ((0, 4 * part - hidden_width), (0, 0))
    we_part, wr_part = (
        lax.dynamic_slice_in_dim(jnp.pad(w, padding), at_share, part, 0) for w in (we, wr)
    )
    got = spread(sent.send)
    got_late, we_part, wr_part = lax.optimization_barrier((got, we_part, wr_part))
    arrived = dict(**sizes, mine=got, other=swap_cores(got_late))
    came_in = call(
        at_place(arrive, vec), dict(**arrived, vec=vectors),
        dict(mask=((cap, cap), f32), x=wide16, h1=wide16, g=wide16), us=6,
    )
    mask, x, h1, g = came_in.mask, came_in.x, came_in.h1, came_in.g
    fwd = call(
        functools.partial(attend, vec),
        dict(h1=h1, mask=mask, vec=vectors, wq=wq, wk=wk, wv=wv, wo=wo),
        dict(q=head16, k=head16, v=head16, log=((cap, heads), f32), att=head16, branch=wide16),
        us=5,
    )
    branch_other = swap_cores(fwd.branch)
    mid = call(
        functools.partial(mlp, vec),
        dict(x=x, branch=fwd.branch, branch_other=branch_other, g=g, vec=vectors, we=we, wr=wr),
        dict(
            middle=wide32, h2=wide16, halves=wide16, sums=[wide16, wide16],
            be_grad=((1, lane_pad(hidden_width)), f32),
        ),
        scratch=[scratch((cap, width), f32)] * 2,
    )
    halves = [swap_dp(mid.halves, flip) for flip in flips[1:]]
    sums = dict(sums=mid.sums, sums_other=[swap_cores(rows) for rows in mid.sums])
    half_back = call(
        functools.partial(middle_back, vec),
        dict(g=g, middle=mid.middle, vec=vectors, wo=wo, **sums),
        dict(dmid=wide32, branch_grad=wide16, datt=head16, vec_grad=((1, 4 * width), f32)),
    )
    att_back = call(
        attend_back,
        dict(
            mask=mask, q=fwd.q, k=fwd.k, v=fwd.v, datt=half_back.datt, log=fwd.log,
            wq=wq, wk=wk, wv=wv,
        ),
        dict(
            dq=head16, dk=head16, dv=head16, dh1=[half16, half16],
            vec_grad=((1, 2 * lane_pad(heads_width)), f32),
        ),
    )
    first = call(
        functools.partial(first_back, vec),
        dict(
            x=x, dh1=att_back.dh1, dh1_other=[swap_cores(rows) for rows in att_back.dh1],
            vec=vectors, dmid=half_back.dmid,
        ),
        dict(dx=wide16, vec_grad=((1, 2 * width), f32)),
    )

    columns = attend_bounds[1]
    vec_rows = -(-vec.size // (16 * columns)) * 16
    keeps, gives = [], []
    for i in range(len(attend_orders)):
        span = attend_bounds[i + 1] - attend_bounds[i]
        keeps.append(((width // 2, span), bf16))
        gives.append(((width // 2 + (0 if i else 2 * vec_rows), span), bf16))
    products = call(
        functools.partial(attend_weights, n_dev, attend_orders, attend_bounds),
        dict(
            h1=h1, branch_grad=half_back.branch_grad,
            right=[att_back.dq, att_back.dk, att_back.dv, fwd.att],
            vec_grads=[first.vec_grad, half_back.vec_grad, mid.be_grad, att_back.vec_grad],
        ),
        dict(vec=((vec_rows, columns), f32), keep=keeps, give=gives),
        scratch=[scratch((width, cap), f32)] * 4,
    )
    a = Chains(products.keep, products.give, attend_orders, products.vec)
    dx = after(first.dx, products.keep[0])
    packed = call(
        at_place(back, vec), dict(**sizes, vec=vectors, middle=mid.middle, dx=dx, **sums), dict(back=wide16)
    ).back
    came = spread(packed)
    far = after(halves, packed)
    far_other = [swap_cores(rows) for rows in far[:2]]
    far[2] = after(far[2], far_other[0])
    far_other.append(swap_cores(far[2]))
    mlp_bounds = (0, 768, lane_pad(2 * part))
    spans = [after_ - before for before, after_ in zip(mlp_bounds, mlp_bounds[1:])]
    mlp_half = [((width // 2, span), bf16) for span in spans]
    grads = call(
        functools.partial(
            mlp_weights, far_bits, [list(o) + list(far_bits) for o in mlp_orders], mlp_bounds, n_dev, vec,
            hidden_width,
        ),
        dict(vec=vectors, we_part=we_part, wr_part=wr_part, h2=mid.h2, g=g, far=far, far_other=far_other),
        dict(give=mlp_half, keep=mlp_half),
        scratch=[scratch((4 * cap, width), bf16)] * 2 + [scratch((4 * cap, part), bf16)] * 2
        + [scratch((width, mlp_bounds[-1]), f32), scratch((width, max(spans)), f32)],
        vmem=36,
    )
    m = Chains(grads.keep, grads.give, mlp_orders)
    last = grads.keep[0]
    last = a.step(0, last)
    last = a.step(1, last)
    last = m.step(0, last)
    last = a.step(0, last)
    last = a.step(1, last)
    last = m.step(1, last)
    last = a.step(0, last)
    last = a.step(1, last)
    m.finish(last)
    a.finish(last)
    own_rows = width // n_dev
    cut = ((own_rows, mlp_bounds[-1]), bf16)
    cuts = call(
        functools.partial(mlp_cut, mlp_bounds), dict(keep=m.kept(), got=m.received()), dict(cuts=[cut] * 4)
    ).cuts
    cuts = [cuts[0]] + [swap_dp(rows, flip) for rows, flip in zip(cuts[1:], flips[1:])]
    final = call(
        at_place(home), dict(**sizes, mine=came, other=swap_cores(came)),
        dict(mixed=((tokens, width), bf16), grad=((tokens, width), bf16)),
    )
    mlp_own = call(
        functools.partial(mlp_last, far_bits, part), dict(cuts=cuts),
        dict(weights=[((own_rows, hidden_width), f32)] * 2),
    ).weights
    own = call(
        functools.partial(last_sums, attend_bounds, vec_rows, vec),
        dict(vec=a.vec, keep=a.kept(), got=a.received()),
        dict(
            vectors=[((v.shape[0],), f32) for v in vector_args],
            weights=[((own_rows, heads_width), f32)] * 4,
        ),
    )
    total = types.SimpleNamespace(**dict(zip(vec.names, own.vectors)))
    wq_sum, wk_sum, wv_sum, wo_sum = own.weights
    wr_sum, we_sum = mlp_own
    return (
        final.mixed, final.grad, total.gain1, total.shift1, wq_sum, total.bq, wk_sum, wv_sum, total.bv,
        wo_sum, total.bo, total.gain2, total.shift2, we_sum, total.be, wr_sum, total.br,
    )


def solution(mesh):
    rows, all_same = P(DP, None), P()
    cols, vector = P(None, CORE), P(CORE)
    tiles = P(DP, CORE)
    in_specs = (
        rows, rows, all_same, all_same, all_same, all_same, cols, vector, cols, cols, vector, cols,
        all_same, all_same, all_same, cols, vector, cols, all_same,
    )
    out_specs = (
        rows, rows, all_same, all_same, tiles, vector, tiles, tiles, vector, tiles, all_same, all_same,
        all_same, tiles, vector, tiles, all_same,
    )
    return jax.shard_map(
        on_device, mesh=mesh, in_specs=in_specs, out_specs=out_specs, check_vma=False
    )
```

```python
import functools
import types

import jax
import jax.numpy as jnp
from jax import lax
from jax.experimental import pallas as pl
from jax.experimental.pallas import tpu as pltpu
from jax.sharding import PartitionSpec as P

HD = 72
DP, CORE = "dp", "tensor"
masked_score = -1000000000.0
norm_eps = 1e-06
gelu_scale = 0.7978845608028654
gelu_cubic = 0.044715
f32 = jnp.float32
bf16 = jnp.bfloat16
MIB = 1024 * 1024
NOWHERE = -1e6


def dot(left, right):
    return lax.dot_general(left, right, (((1,), (0,)), ((), ())), preferred_element_type=f32)


def dot_cols(left, right):
    return lax.dot_general(left, right, (((1,), (1,)), ((), ())), preferred_element_type=f32)


def dot_rows(left, right):
    return lax.dot_general(left, right, (((0,), (0,)), ((), ())), preferred_element_type=f32)


def iota(shape, dim):
    return lax.broadcasted_iota(jnp.int32, shape, dim).astype(f32)


def row_sum(values):
    return jnp.sum(values, axis=0, keepdims=True)


def lane_sum(values):
    return jnp.sum(values, axis=1, keepdims=True)


def lane_mean(values):
    return jnp.mean(values, axis=1, keepdims=True)


def lane_pad(size):
    return -(-size // 128) * 128


def put(ref, value):
    ref[...] = value.astype(ref.dtype)


def my_span(lengths, owners, me):
    base = lane_sum(jnp.where(owners < me, lengths, 0.0))
    used = lane_sum(jnp.where(owners == me, lengths, 0.0))
    return base, used


def token_slots(lengths, owners, me, n_dev, tokens, half_rows):
    device = iota((n_dev, lengths.shape[1]), 0)
    base = lane_sum(jnp.where(owners < device, lengths, 0.0))
    pos = iota((1, tokens), 1) * n_dev + me
    below = base <= pos
    target = row_sum(jnp.where(below, 1.0, 0.0)) - 1.0
    start = jnp.max(jnp.where(below, base, -1.0), axis=0, keepdims=True)
    slot = jnp.floor((pos - start) * (1.0 / n_dev))
    half = jnp.floor(slot * (1.0 / half_rows))
    return half, target * half_rows + slot - half * half_rows


def block_slots(base, n_dev, cap, half_rows):
    p = iota((cap, 1), 0)
    pos = base + p
    source = pos - n_dev * jnp.floor(pos * (1.0 / n_dev))
    slot = jnp.floor(p * (1.0 / n_dev))
    half = jnp.floor(slot * (1.0 / half_rows))
    return half, source * half_rows + slot - half * half_rows


def one_hot(index, shape, dim):
    return jnp.where(index == iota(shape, dim), 1.0, 0.0).astype(bf16)


def place():
    return lax.axis_index(DP).astype(f32), lax.axis_index(CORE).astype(f32)


def norm_parts(values):
    centered = values - lane_mean(values)
    scale = lax.rsqrt(lane_mean(centered * centered) + norm_eps)
    return centered * scale, scale


def norm_back(normed, scale, grad, gain):
    inner = grad * gain
    return scale * (inner - lane_mean(inner) - normed * lane_mean(inner * normed))


def gelu_both(values):
    square = values * values
    bent = jnp.tanh(gelu_scale * values * (1.0 + gelu_cubic * square))
    half = 0.5 * (1.0 + bent)
    slope = half + 0.5 * values * (1.0 - bent * bent) * (
        gelu_scale * (1.0 + 3.0 * gelu_cubic * square)
    )
    return values * half, slope


def flip_of(block, order):
    flip = 0 * block
    for step, bit in enumerate(order):
        flip = flip | (((block >> (len(order) - 1 - step)) & 1) << bit)
    return flip


def ordered_rows(out_ref, from_ref, n_dev, order):
    width = from_ref.shape[0]
    owner_rows = width // n_dev
    me = lax.axis_index(DP)
    if owner_rows % 8:
        i = iota((width, 1), 0)
        block = jnp.floor((i + 0.5) * (1.0 / owner_rows))
        owner = (flip_of(block.astype(jnp.int32), order) ^ me).astype(f32)
        pick = one_hot(owner * owner_rows + (i - block * owner_rows), (width, width), 1)
        out_ref[...] = dot(pick, from_ref[...].astype(bf16))
        return
    for block in range(n_dev):
        start = pl.multiple_of((me ^ flip_of(block, order)) * owner_rows, 8)
        rows = slice(block * owner_rows, (block + 1) * owner_rows)
        out_ref[rows, :] = from_ref[pl.ds(start, owner_rows), :]


def parts_between(bounds, group, size, count):
    for i in range(count):
        first, last = max(i * size, bounds[group]), min((i + 1) * size, bounds[group + 1])
        if first < last:
            yield (
                i,
                slice(first - i * size, last - i * size),
                slice(first - bounds[group], last - bounds[group]),
            )


def pieces_of(start, size, columns):
    done = 0
    while done < size:
        row, lane = (start + done) // columns, (start + done) % columns
        now = min(columns - lane, size - done)
        yield slice(done, done + now), slice(row, row + 1), slice(lane, lane + now)
        done += now


def call(body, ins, outs, scratch=(), vmem=16, far=False, us=0):
    ins_flat, ins_tree = jax.tree.flatten(ins)
    is_out = lambda x: isinstance(x, tuple)
    outs_flat, outs_tree = jax.tree.flatten(outs, is_leaf=is_out)
    n_in, n_out = len(ins_flat), len(outs_flat)

    def kernel(*refs):
        given, rest = refs[:n_in], refs[n_in + n_out :]
        if far:
            near, sems, rest = rest[:n_in], rest[n_in], rest[n_in + 1 :]
            copies = [
                pltpu.make_async_copy(ref, to, sems.at[i]) for i, (ref, to) in enumerate(zip(given, near))
            ]
            for copy in copies:
                copy.start()

            def arrival(copy, to):
                def wait():
                    copy.wait()
                    return to[...]

                return wait

            given = [arrival(copy, to) for copy, to in zip(copies, near)]
        given = types.SimpleNamespace(**jax.tree.unflatten(ins_tree, given))
        made = types.SimpleNamespace(**jax.tree.unflatten(outs_tree, refs[n_in : n_in + n_out]))
        body(given, made, *rest)

    copies = [pltpu.VMEM(x.shape, x.dtype) for x in ins_flat]
    copies += [pltpu.SemaphoreType.DMA((n_in,))]
    results = pl.pallas_call(
        kernel,
        name=getattr(body, "func", body).__name__,
        out_shape=[jax.ShapeDtypeStruct(shape, dtype) for shape, dtype in outs_flat],
        in_specs=[pl.BlockSpec(memory_space=pltpu.HBM if far else pltpu.VMEM)] * n_in,
        out_specs=[pl.BlockSpec(memory_space=pltpu.VMEM)] * n_out,
        scratch_shapes=(copies if far else []) + list(scratch),
        cost_estimate=pl.CostEstimate(flops=us * 10**9, bytes_accessed=us * 10**6, transcendentals=0),
        compiler_params=pltpu.CompilerParams(vmem_limit_bytes=vmem * MIB),
    )(*ins_flat)
    return types.SimpleNamespace(**jax.tree.unflatten(outs_tree, results))


def pack(n_dev, half_rows, tokens, given, made):
    me, core = place()
    lengths, owners = given.lengths().astype(f32), given.owners().astype(f32)
    half, index = token_slots(lengths, owners, me, n_dev, tokens, half_rows)
    target = jnp.floor(index * (1.0 / half_rows))
    index = jnp.where(half == core, index + target * half_rows, NOWHERE)
    shape = (2 * n_dev * half_rows, tokens)
    x_pick, g_pick = one_hot(index, shape, 0), one_hot(index + half_rows, shape, 0)
    rows = dot(x_pick, given.x())
    put(made.send, rows + dot(g_pick, given.g()))


def block_rows(given, n_dev, cap, half_rows, kind):
    me, core = place()
    base, _ = my_span(given.lengths[...].astype(f32), given.owners[...].astype(f32), me)
    half, index = block_slots(base, n_dev, cap, half_rows)
    source = jnp.floor(index * (1.0 / half_rows))
    index = index + (source + kind) * half_rows
    index = jnp.where(half == core, index, index + 2 * n_dev * half_rows)
    pick = one_hot(index, (cap, 2 * cap), 1)
    return dot(pick, jnp.concatenate([given.mine[...], given.other[...]], axis=0))


def image_mask(lengths, owners, cap):
    me, _ = place()
    base, used = my_span(lengths, owners, me)
    n_img = lengths.shape[1]
    starts = lane_sum(jnp.where(iota((n_img, n_img), 1) < iota((n_img, n_img), 0), lengths, 0.0))
    p = iota((1, cap), 1)
    count = row_sum(jnp.where(starts <= base + p, 1.0, 0.0))
    seg_row = jnp.where(p < used, count, 0.0)
    on_diagonal = iota((cap, cap), 0) == iota((cap, cap), 1)
    seg_col = lane_sum(jnp.where(on_diagonal, seg_row, 0.0))
    return jnp.where(seg_col == seg_row, 1.0, 0.0)


class Vectors:
    def __init__(self, **sizes):
        self.names, self.size = list(sizes), 0
        for name, size in sizes.items():
            setattr(self, name, slice(self.size, self.size + size))
            self.size += lane_pad(size)


def arrive(n_dev, half_rows, vec, given, made):
    cap = made.x.shape[0]
    x = block_rows(given, n_dev, cap, half_rows, 0)
    put(made.x, x)
    normed, _ = norm_parts(x)
    put(made.h1, normed * given.vec[:, vec.gain1] + given.vec[:, vec.shift1])
    put(made.g, block_rows(given, n_dev, cap, half_rows, 1))
    put(made.mask, image_mask(given.lengths[...].astype(f32), given.owners[...].astype(f32), cap))


def attend(vec, given, made):
    same = given.mask[...] > 0.5
    row, h1 = given.vec, given.h1[...]
    put(made.q, dot_cols(h1, given.wq[...]) + row[:, vec.bq])
    put(made.k, dot_cols(h1, given.wk[...]))
    put(made.v, dot_cols(h1, given.wv[...]) + row[:, vec.bv])
    for h in range(made.q.shape[1] // HD):
        cols = slice(h * HD, (h + 1) * HD)
        s = dot_cols(made.q[:, cols], made.k[:, cols]) * HD ** (-0.5)
        s = jnp.where(same, s, masked_score)
        top = jnp.max(s, axis=1, keepdims=True)
        e = jnp.exp(s - top)
        total = lane_sum(e)
        made.log[:, h : h + 1] = top + jnp.log(total)
        made.att[:, cols] = dot((e * (1.0 / total)).astype(bf16), made.v[:, cols]).astype(bf16)
    put(made.branch, dot(made.att[...], given.wo[...]))


def both(mine, other, rows=slice(None)):
    return mine[rows, :].astype(f32) + other[rows, :].astype(f32)


def both_halves(mine, other, rows=slice(None)):
    return jnp.concatenate([both(a, b, rows) for a, b in zip(mine, other)], axis=0)


def chunks_of(width, step):
    full = width // step
    return full, full * step, width - full * step


def mlp(vec, given, made, out_total, dh2_total):
    cap = made.middle.shape[0]
    half = cap // 2
    row = given.vec
    branch = both(given.branch, given.branch_other) + row[:, vec.bo]
    middle = given.x[...].astype(f32) + branch
    put(made.middle, middle)
    normed, _ = norm_parts(middle)
    put(made.h2, normed * row[:, vec.gain2] + row[:, vec.shift2])
    start = pl.multiple_of(lax.axis_index(CORE) * half, half)
    made.halves[:half, :] = made.h2[pl.ds(start, half), :]
    made.halves[half:, :] = given.g[pl.ds(start, half), :]
    step = 1024
    full, done, rest = chunks_of(given.we.shape[0], step)
    out_total[...] = jnp.zeros_like(out_total)
    dh2_total[...] = jnp.zeros_like(dh2_total)
    made.be_grad[...] = jnp.zeros_like(made.be_grad)
    first = vec.be.start

    def chunk(rows, bias):
        we, wr = given.we[rows, :], given.wr[rows, :]
        hidden, slope = gelu_both(dot_cols(made.h2[...], we) + row[:, bias])
        dexp = (dot_cols(given.g[...], wr) * slope).astype(bf16)
        made.be_grad[:, rows] = row_sum(dexp.astype(f32))
        out_total[...] += dot(hidden.astype(bf16), wr)
        dh2_total[...] += dot(dexp, we)

    @pl.loop(0, full, unroll=True)
    def _(i):
        at = pl.multiple_of(i * step, step)
        chunk(pl.ds(at, step), pl.ds(pl.multiple_of(first + at, 128), step))

    if rest:
        chunk(slice(done, done + rest), slice(first + done, first + done + rest))
    for i, ref in enumerate(made.sums):
        rows = slice(i * half, (i + 1) * half)
        ref[:half, :] = dh2_total[rows, :].astype(bf16)
        ref[half:, :] = out_total[rows, :].astype(bf16)


def middle_back(vec, given, made):
    width = given.middle.shape[1]
    half = given.sums[0].shape[0] // 2
    g = given.g[...].astype(f32)
    normed, scale = norm_parts(given.middle[...])
    dh2 = both_halves(given.sums, given.sums_other, slice(0, half))
    dmid = g + norm_back(normed, scale, dh2, given.vec[:, vec.gain2])
    put(made.dmid, dmid)
    branch = dmid.astype(bf16)
    put(made.branch_grad, branch)
    put(made.datt, dot_cols(branch, given.wo[...]))
    for i, values in enumerate([branch.astype(f32), dh2 * normed, dh2, g]):
        made.vec_grad[:, i * width : (i + 1) * width] = row_sum(values)


def attend_back(given, made):
    heads_width = made.dq.shape[1]
    same = given.mask[...] > 0.5
    for h in range(heads_width // HD):
        cols = slice(h * HD, (h + 1) * HD)
        q, k, v = given.q[:, cols], given.k[:, cols], given.v[:, cols]
        datt = given.datt[:, cols]
        s = jnp.where(same, dot_cols(q, k) * HD ** (-0.5), masked_score)
        prob = jnp.exp(s - given.log[:, h : h + 1])
        dprob = dot_cols(datt, v)
        ds = (prob * (dprob - lane_sum(prob * dprob))).astype(bf16)
        made.dq[:, cols] = (dot(ds, k) * HD ** (-0.5)).astype(bf16)
        made.dk[:, cols] = (dot_rows(ds, q) * HD ** (-0.5)).astype(bf16)
        made.dv[:, cols] = dot_rows(prob.astype(bf16), datt).astype(bf16)
    dh1 = dot(made.dq[...], given.wq[...])
    dh1 += dot(made.dk[...], given.wk[...])
    dh1 += dot(made.dv[...], given.wv[...])
    half = dh1.shape[0] // 2
    for i, ref in enumerate(made.dh1):
        put(ref, dh1[i * half : (i + 1) * half, :])
    row = made.vec_grad
    row[...] = jnp.zeros_like(row)
    row[:, :heads_width] = row_sum(made.dq[...].astype(f32))
    second = lane_pad(heads_width)
    row[:, second : second + heads_width] = row_sum(made.dv[...].astype(f32))


def put_vectors(give_ref, first, rows, values):
    rounded = values.astype(bf16)
    give_ref[first : first + rows, :] = rounded
    return rounded.astype(f32)


def got_vectors(got_ref, rows):
    return got_ref[got_ref.shape[0] - rows :, :].astype(f32)


def attend_weights(n_dev, orders, bounds, given, made, h1_t, branch_t, left, branch_left):
    heads_width = given.right[0].shape[1]
    half = given.h1.shape[1] // 2
    h1_t[...] = jnp.transpose(given.h1[...].astype(f32))
    branch_t[...] = jnp.transpose(given.branch_grad[...].astype(f32))
    made.vec[...] = jnp.zeros_like(made.vec)
    at = 0
    for ref in given.vec_grads:
        for here, row, lanes in pieces_of(at, ref.shape[1], made.vec.shape[1]):
            made.vec[row, lanes] = ref[:, here]
        at += ref.shape[1]
    put(made.vec, put_vectors(made.give[0], half, made.vec.shape[0], made.vec[...]))
    for group, order in enumerate(orders):
        width = bounds[group + 1] - bounds[group]
        ordered_rows(left, h1_t, n_dev, order)
        parts = list(parts_between(bounds, group, heads_width, 4))
        for shift in (False, True):
            chosen = [part for part in parts if (part[0] == 3) == shift]
            if not chosen:
                continue
            if shift:
                ordered_rows(branch_left, branch_t, n_dev, order)
            rows = (branch_left if shift else left)[...].astype(bf16)
            right = [given.right[i][:, cols] for i, cols, _ in chosen]
            right = jnp.concatenate(right, axis=1) if len(right) > 1 else right[0]
            product = dot(rows, right).astype(bf16)
            lanes = slice(chosen[0][2].start, chosen[-1][2].stop)
            made.keep[group][:, lanes] = product[:half, :]
            made.give[group][:half, lanes] = product[half:, :]


def first_back(vec, given, made):
    width = given.x.shape[1]
    normed, scale = norm_parts(given.x[...].astype(f32))
    dh1 = both_halves(given.dh1, given.dh1_other)
    made.vec_grad[:, :width] = row_sum(dh1 * normed)
    made.vec_grad[:, width:] = row_sum(dh1)
    gain = given.vec[:, vec.gain1]
    put(made.dx, given.dmid[...] + norm_back(normed, scale, dh1, gain))


def back(n_dev, half_rows, vec, given, made):
    cap = given.dx.shape[0]
    half = given.sums[0].shape[0] // 2
    me, core = place()
    base, _ = my_span(given.lengths[...].astype(f32), given.owners[...].astype(f32), me)
    which, index = block_slots(base, n_dev, cap, half_rows)
    source = jnp.floor(index * (1.0 / half_rows))
    index = jnp.where(which == core, index + source * half_rows, NOWHERE)
    part = both_halves(given.sums, given.sums_other, slice(half, 2 * half))
    out = given.middle[...] + (part + given.vec[:, vec.br])
    rows = dot_rows(one_hot(index, (cap, cap), 1), out.astype(bf16))
    rows += dot_rows(one_hot(index + half_rows, (cap, cap), 1), given.dx[...])
    put(made.back, rows)


def home(n_dev, half_rows, given, made):
    me, core = place()
    tokens = made.mixed.shape[0]
    lengths, owners = given.lengths[...].astype(f32), given.owners[...].astype(f32)
    half, index = token_slots(lengths, owners, me, n_dev, tokens, half_rows)
    index = index + jnp.floor(index * (1.0 / half_rows)) * half_rows
    index = jnp.where(half == core, index, index + 2 * n_dev * half_rows)
    rows = jnp.concatenate([given.mine[...], given.other[...]], axis=0)
    shape = (rows.shape[0], tokens)
    put(made.mixed, dot_rows(one_hot(index, shape, 0), rows))
    put(made.grad, dot_rows(one_hot(index + half_rows, shape, 0), rows))


def share_of(far_bits):
    me = lax.axis_index(DP)
    return 2 * ((me >> far_bits[0]) & 1) + ((me >> far_bits[1]) & 1)


def mlp_weights(
    far_bits, orders, bounds, n_dev, vec, hidden_width, given, made, h2_all, g_all, hidden_all, dexp_all,
    natural, ordered,
):
    cap, width = given.h2.shape
    half_cap = cap // 2
    share = share_of(far_bits)
    part = given.we_part.shape[0]
    be = vec.be.start
    bias = jnp.zeros((1, part), f32)
    for i in range(4):
        end = min((i + 1) * part, hidden_width)
        piece = given.vec[:, be + i * part : be + end]
        if end < (i + 1) * part:
            piece = jnp.concatenate([piece, jnp.zeros((1, (i + 1) * part - end), f32)], axis=1)
        bias += jnp.where(share == i, piece, 0.0)
    for k in range(4):
        rows = slice(k * cap, (k + 1) * cap)
        if k == 0:
            h2_all[rows, :] = given.h2[...]
            g_all[rows, :] = given.g[...]
        else:
            for i, ref in enumerate((given.far[k - 1], given.far_other[k - 1])):
                at = slice(k * cap + i * half_cap, k * cap + (i + 1) * half_cap)
                h2_all[at, :] = ref[:half_cap, :]
                g_all[at, :] = ref[half_cap:, :]
        hidden, slope = gelu_both(dot_cols(h2_all[rows, :], given.we_part[...]) + bias)
        hidden_all[rows, :] = hidden.astype(bf16)
        dexp_all[rows, :] = (dot_cols(g_all[rows, :], given.wr_part[...]) * slope).astype(bf16)
    half = width // 2
    natural[:, :part] = dot_rows(g_all[...], hidden_all[...])
    natural[:, part : 2 * part] = dot_rows(h2_all[...], dexp_all[...])
    if 2 * part < bounds[-1]:
        natural[:, 2 * part :] = jnp.zeros((width, bounds[-1] - 2 * part), f32)
    for group, order in enumerate(orders):
        lanes = pl.ds(bounds[group], bounds[group + 1] - bounds[group])
        here = ordered.at[:, pl.ds(0, bounds[group + 1] - bounds[group])]
        ordered_rows(here, natural.at[:, lanes], n_dev, order)
        put(made.give[group], here[half:, :])
        put(made.keep[group], here[:half, :])


def turn(vec_rows, given, made):
    rows = given.keep.shape[0]
    total = given.keep[...].astype(f32) + given.got[:rows, :].astype(f32)
    put(made.keep, total[: rows // 2, :])
    made.give[: rows // 2, :] = total[rows // 2 :, :].astype(bf16)
    if vec_rows:
        vec = given.vec[...] + got_vectors(given.got, vec_rows)
        put(made.vec, put_vectors(made.give, rows // 2, vec_rows, vec))


def last_sums(bounds, vec_rows, vec, given, made):
    sums = given.vec[...] + got_vectors(given.got[0], vec_rows)
    for name, ref in zip(vec.names, made.vectors):
        at = getattr(vec, name)
        for here, row, lanes in pieces_of(at.start, at.stop - at.start, sums.shape[1]):
            ref[here] = sums[row, lanes].reshape(here.stop - here.start)
    for group, (keep, got) in enumerate(zip(given.keep, given.got)):
        value = keep[...].astype(f32) + got[: keep.shape[0], :].astype(f32)
        for i, cols, lanes in parts_between(bounds, group, made.weights[0].shape[1], 4):
            made.weights[i][:, cols] = value[:, lanes]


def mlp_cut(bounds, given, made):
    rows = given.keep[0].shape[0] // 4
    for group, (keep, got) in enumerate(zip(given.keep, given.got)):
        total = keep[...].astype(f32) + got[...].astype(f32)
        for k, ref in enumerate(made.cuts):
            ref[:, bounds[group] : bounds[group + 1]] = total[k * rows : (k + 1) * rows, :].astype(bf16)


def mlp_last(far_bits, part, given, made):
    share = share_of(far_bits)
    hidden_width = made.weights[0].shape[1]
    pieces = [ref[...].astype(f32) for ref in given.cuts]
    for i in range(4):
        own = jnp.zeros_like(pieces[0])
        for k, piece in enumerate(pieces):
            own += jnp.where((share ^ k) == i, piece, 0.0)
        end = min((i + 1) * part, hidden_width)
        for at, ref in enumerate(made.weights):
            ref[:, i * part : end] = own[:, at * part : at * part + end - i * part]


def swap_cores(values):
    return lax.ppermute(values, CORE, [(0, 1), (1, 0)])


def swap_dp(values, flip):
    return lax.ppermute(values, DP, [(i, i ^ flip) for i in range(lax.axis_size(DP))])


def spread(rows):
    return lax.all_to_all(rows, DP, split_axis=0, concat_axis=0, tiled=True)


def after(values, earlier):
    return lax.optimization_barrier((values, earlier))[0]


def next_step(pair, vec):
    keep, got = pair
    rows = keep.shape[0] // 2
    vec_rows = 0 if vec is None else vec.shape[0]
    if rows % 8:
        total = keep.astype(f32) + got[: 2 * rows].astype(f32)
        kept, give = total[:rows], total[rows:].astype(bf16)
        if vec is not None:
            rounded = (vec + got[2 * rows :].astype(f32)).astype(bf16)
            vec = rounded.astype(f32)
            give = jnp.concatenate([give, rounded])
        return kept, give, vec
    columns = keep.shape[1]
    ins, outs = dict(keep=keep, got=got), dict(keep=((rows, columns), f32))
    outs.update(give=((rows + vec_rows, columns), bf16))
    if vec is not None:
        ins.update(vec=vec)
        outs.update(vec=(vec.shape, f32))
    made = call(functools.partial(turn, vec_rows), ins, outs)
    return made.keep, made.give, None if vec is None else made.vec


class Chains:
    def __init__(self, keep, give, orders, vec=None):
        self.orders, self.vec = orders, vec
        self.done = [1] * len(orders)
        self.pairs = [(k, swap_dp(g, 1 << order[0])) for k, g, order in zip(keep, give, orders)]

    def step(self, group, earlier):
        step = self.done[group]
        self.done[group] += 1
        pair = after(self.pairs[group], earlier)
        keep, give, vec = next_step(pair, None if group else self.vec)
        if not group:
            self.vec = vec
        self.pairs[group] = (keep, swap_dp(give, 1 << self.orders[group][step]))
        return keep

    def finish(self, earlier):
        for group, order in enumerate(self.orders):
            while self.done[group] < len(order):
                earlier = self.step(group, earlier)

    def kept(self):
        return [pair[0] for pair in self.pairs]

    def received(self):
        return [pair[1] for pair in self.pairs]


def on_device(
    patches, cotangent, image_lengths, image_owner, first_gain, first_shift, query_weight,
    query_bias, key_weight, value_weight, value_bias, output_weight, output_bias, second_gain,
    second_shift, expand_weight, expand_bias, reduce_weight, reduce_bias,
):
    n_dev = lax.axis_size(DP)
    tokens, width = patches.shape
    cap = 2 * tokens
    half_rows = cap // n_dev // 2
    heads_width, hidden_width = query_weight.shape[1], expand_weight.shape[1]
    heads = heads_width // HD
    n_bits = n_dev.bit_length() - 1
    far_bits = (1, n_bits - 2)
    flips = [flip_of(k, far_bits) for k in range(4)]
    rest = [bit for bit in range(n_bits) if bit not in far_bits]
    mlp_orders = (rest, rest[::-1])
    others = list(range(2, n_bits - 2))
    attend_orders = (
        [0, 1] + others + [n_bits - 2, n_bits - 1],
        [n_bits - 2, 1, 0] + others + [n_bits - 1],
    )
    attend_bounds = (0, 1152, 4 * heads_width)
    wq, wk, wv, wo, we, wr = (
        w.T for w in (query_weight, key_weight, value_weight, output_weight, expand_weight, reduce_weight)
    )
    vec = Vectors(
        gain1=width, shift1=width, bo=width, gain2=width, shift2=width, br=width, be=hidden_width,
        bq=heads_width, bv=heads_width,
    )
    vector_args = [
        first_gain, first_shift, output_bias, second_gain, second_shift, reduce_bias, expand_bias,
        query_bias, value_bias,
    ]
    vectors = jnp.concatenate(
        [jnp.pad(v, (0, lane_pad(v.shape[0]) - v.shape[0])) for v in vector_args]
    ).reshape(1, -1)
    sizes = dict(lengths=image_lengths.reshape(1, -1), owners=image_owner.reshape(1, -1))
    wide32, wide16 = ((cap, width), f32), ((cap, width), bf16)
    half16 = ((cap // 2, width), bf16)
    head16 = ((cap, heads_width), bf16)
    at_place = lambda body, *more: functools.partial(body, n_dev, half_rows, *more)
    scratch = pltpu.VMEM

    sent = call(
        at_place(pack, tokens), dict(**sizes, x=patches, g=cotangent), dict(send=wide16), far=True, vmem=62
    )
    part = -(-hidden_width // 64) * 16
    at_share = share_of(far_bits) * part
    padding = ((0, 4 * part - hidden_width), (0, 0))
    we_part, wr_part = (
        lax.dynamic_slice_in_dim(jnp.pad(w, padding), at_share, part, 0) for w in (we, wr)
    )
    got = spread(sent.send)
    got_late, we_part, wr_part = lax.optimization_barrier((got, we_part, wr_part))
    arrived = dict(**sizes, mine=got, other=swap_cores(got_late))
    came_in = call(
        at_place(arrive, vec), dict(**arrived, vec=vectors),
        dict(mask=((cap, cap), f32), x=wide16, h1=wide16, g=wide16), us=6,
    )
    mask, x, h1, g = came_in.mask, came_in.x, came_in.h1, came_in.g
    fwd = call(
        functools.partial(attend, vec),
        dict(h1=h1, mask=mask, vec=vectors, wq=wq, wk=wk, wv=wv, wo=wo),
        dict(q=head16, k=head16, v=head16, log=((cap, heads), f32), att=head16, branch=wide16),
        us=5,
    )
    branch_other = swap_cores(fwd.branch)
    mid = call(
        functools.partial(mlp, vec),
        dict(x=x, branch=fwd.branch, branch_other=branch_other, g=g, vec=vectors, we=we, wr=wr),
        dict(
            middle=wide32, h2=wide16, halves=wide16, sums=[wide16, wide16],
            be_grad=((1, lane_pad(hidden_width)), f32),
        ),
        scratch=[scratch((cap, width), f32)] * 2,
    )
    halves = [swap_dp(mid.halves, flip) for flip in flips[1:]]
    sums = dict(sums=mid.sums, sums_other=[swap_cores(rows) for rows in mid.sums])
    half_back = call(
        functools.partial(middle_back, vec),
        dict(g=g, middle=mid.middle, vec=vectors, wo=wo, **sums),
        dict(dmid=wide32, branch_grad=wide16, datt=head16, vec_grad=((1, 4 * width), f32)),
    )
    att_back = call(
        attend_back,
        dict(
            mask=mask, q=fwd.q, k=fwd.k, v=fwd.v, datt=half_back.datt, log=fwd.log,
            wq=wq, wk=wk, wv=wv,
        ),
        dict(
            dq=head16, dk=head16, dv=head16, dh1=[half16, half16],
            vec_grad=((1, 2 * lane_pad(heads_width)), f32),
        ),
    )
    first = call(
        functools.partial(first_back, vec),
        dict(
            x=x, dh1=att_back.dh1, dh1_other=[swap_cores(rows) for rows in att_back.dh1],
            vec=vectors, dmid=half_back.dmid,
        ),
        dict(dx=wide16, vec_grad=((1, 2 * width), f32)),
    )

    columns = attend_bounds[1]
    vec_rows = -(-vec.size // (16 * columns)) * 16
    keeps, gives = [], []
    for i in range(len(attend_orders)):
        span = attend_bounds[i + 1] - attend_bounds[i]
        keeps.append(((width // 2, span), bf16))
        gives.append(((width // 2 + (0 if i else vec_rows), span), bf16))
    products = call(
        functools.partial(attend_weights, n_dev, attend_orders, attend_bounds),
        dict(
            h1=h1, branch_grad=half_back.branch_grad,
            right=[att_back.dq, att_back.dk, att_back.dv, fwd.att],
            vec_grads=[first.vec_grad, half_back.vec_grad, mid.be_grad, att_back.vec_grad],
        ),
        dict(vec=((vec_rows, columns), f32), keep=keeps, give=gives),
        scratch=[scratch((width, cap), f32)] * 4,
    )
    a = Chains(products.keep, products.give, attend_orders, products.vec)
    dx = after(first.dx, products.keep[0])
    packed = call(
        at_place(back, vec), dict(**sizes, vec=vectors, middle=mid.middle, dx=dx, **sums), dict(back=wide16)
    ).back
    came = spread(packed)
    far = after(halves, packed)
    far_other = [swap_cores(rows) for rows in far[:2]]
    far[2] = after(far[2], far_other[0])
    cut_at = 4 * cap // 8
    far_other.append(jnp.concatenate([swap_cores(far[2][:cut_at]), swap_cores(far[2][cut_at:])]))
    mlp_bounds = (0, 768, lane_pad(2 * part))
    spans = [after_ - before for before, after_ in zip(mlp_bounds, mlp_bounds[1:])]
    mlp_half = [((width // 2, span), bf16) for span in spans]
    grads = call(
        functools.partial(
            mlp_weights, far_bits, [list(o) + list(far_bits) for o in mlp_orders], mlp_bounds, n_dev, vec,
            hidden_width,
        ),
        dict(vec=vectors, we_part=we_part, wr_part=wr_part, h2=mid.h2, g=g, far=far, far_other=far_other),
        dict(give=mlp_half, keep=mlp_half),
        scratch=[scratch((4 * cap, width), bf16)] * 2 + [scratch((4 * cap, part), bf16)] * 2
        + [scratch((width, mlp_bounds[-1]), f32), scratch((width, max(spans)), f32)],
        vmem=36,
    )
    m = Chains(grads.keep, grads.give, mlp_orders)
    last = grads.keep[0]
    last = a.step(0, last)
    last = m.step(1, last)
    last = a.step(1, last)
    last = m.step(0, last)
    last = a.step(0, last)
    last = a.step(1, last)
    last = a.step(0, last)
    last = a.step(1, last)
    m.finish(last)
    a.finish(last)
    own_rows = width // n_dev
    cut = ((own_rows, mlp_bounds[-1]), bf16)
    cuts = call(
        functools.partial(mlp_cut, mlp_bounds), dict(keep=m.kept(), got=m.received()), dict(cuts=[cut] * 4)
    ).cuts
    cuts = [cuts[0]] + [swap_dp(rows, flip) for rows, flip in zip(cuts[1:], flips[1:])]
    final = call(
        at_place(home), dict(**sizes, mine=came, other=swap_cores(came)),
        dict(mixed=((tokens, width), bf16), grad=((tokens, width), bf16)),
    )
    mlp_own = call(
        functools.partial(mlp_last, far_bits, part), dict(cuts=cuts),
        dict(weights=[((own_rows, hidden_width), f32)] * 2),
    ).weights
    own = call(
        functools.partial(last_sums, attend_bounds, vec_rows, vec),
        dict(vec=a.vec, keep=a.kept(), got=a.received()),
        dict(
            vectors=[((v.shape[0],), f32) for v in vector_args],
            weights=[((own_rows, heads_width), f32)] * 4,
        ),
    )
    total = types.SimpleNamespace(**dict(zip(vec.names, own.vectors)))
    wq_sum, wk_sum, wv_sum, wo_sum = own.weights
    wr_sum, we_sum = mlp_own
    return (
        final.mixed, final.grad, total.gain1, total.shift1, wq_sum, total.bq, wk_sum, wv_sum, total.bv,
        wo_sum, total.bo, total.gain2, total.shift2, we_sum, total.be, wr_sum, total.br,
    )


def solution(mesh):
    rows, all_same = P(DP, None), P()
    cols, vector = P(None, CORE), P(CORE)
    tiles = P(DP, CORE)
    in_specs = (
        rows, rows, all_same, all_same, all_same, all_same, cols, vector, cols, cols, vector, cols,
        all_same, all_same, all_same, cols, vector, cols, all_same,
    )
    out_specs = (
        rows, rows, all_same, all_same, tiles, vector, tiles, tiles, vector, tiles, all_same, all_same,
        all_same, tiles, vector, tiles, all_same,
    )
    return jax.shard_map(
        on_device, mesh=mesh, in_specs=in_specs, out_specs=out_specs, check_vma=False
    )
```
